32 devices in a mesh: dp: 4 (over z), tensor: 8 (over y, x, core).
Axes of the slice: x: 2, y: 2, z: 4, core: 2. Of those that a mesh axis runs over, the one named last changes fastest.
Arguments:
- tokens: bfloat16 [64, 128, 1536], P(('dp', 'tensor')), may hold values from -60 to 60
- cached: bfloat16 [64, 512, 1536], P(('dp', 'tensor')), may hold values from -60 to 60
- norm_gains: float32 [2, 1536], replicated, may hold values from 0.5 to 1.5
- w_qkv: bfloat16 [1536, 3072], replicated, may hold values from -0.15625 to 0.15625
- w_out: bfloat16 [1536, 1536], replicated, may hold values from -0.15625 to 0.15625
- mlp_weights: bfloat16 [3, 1536, 4096], P(None, None, 'tensor'), may hold values from -0.15625 to 0.15625
- request_order: int32 [64], replicated, may hold values from 0 to 63, as said below
- new_lengths: int32 [64], replicated, may hold values from 1 to 128, 5120 in all
- cached_lengths: int32 [64], replicated, may hold values from 0 to 384
- decode_slots: int32 [64], replicated, may hold values from 0 to 63, as said below
Outputs:
- layer_out: bfloat16 [64, 128, 1536], P(('dp', 'tensor'))
- kv_decode: bfloat16 [64, 512, 1536], P('dp', 'tensor')
The draws below stay inside these ranges and needn't reach their ends.
Inputs may be any that keep to these rules, and one draw needn't show every extreme that they name: `request_order`: each value once; the device at index k of dp+tensor holds prefill slots k * 2 to (k + 1) * 2 - 1. `decode_slots`: each value once; the 16 requests held by the prefill slots of one index of dp take exactly 4 slots of every aligned block of 16 decode slots.
All inputs are finite; a program needn't handle non-finite values.
Results may differ from the reference program's by a relative error of at most 0.015.
Values may be sent and summed in bfloat16 or wider, within the bound.
No kernel may reach another device: no remote copies, remote signals or barrier semaphores. Data moves between devices by JAX's collectives and lax.ppermute only.
A program may use at most 192 MiB of HBM per device.

```python
import math
import jax
import jax.numpy as jnp
import numpy as np
from jax import lax

D = 1536
HEADS = 16
KV_HEADS = 8
HEAD_DIM = 96
FF = 4096
NEW = 128
CTX = 512
KVW = 1536
REQS = 64
GROUP_REQS = 16
SHARE = 4
N_TENSOR = 8


def dealing(key):
    groups = REQS // GROUP_REQS
    ordering = jax.random.permutation(jax.random.fold_in(key, 11), REQS)
    mixing = jax.vmap(lambda subkey: jax.random.permutation(subkey, GROUP_REQS))(jax.random.split(jax.random.fold_in(key, 12), groups))
    within = jax.vmap(lambda subkey: jax.random.permutation(subkey, GROUP_REQS))(jax.random.split(jax.random.fold_in(key, 13), groups))
    target = mixing // SHARE
    placed = jnp.arange(groups)[:, None] * SHARE + mixing % SHARE
    slot_rows = target * GROUP_REQS + within[target, placed]
    slot_table = jnp.zeros((REQS,), jnp.int32).at[ordering].set(slot_rows.reshape(REQS).astype(jnp.int32))
    return (ordering.astype(jnp.int32), slot_table)


def draw_request_order(key, part):
    return dealing(key)[0]


def draw_decode_slots(key, part):
    return dealing(key)[1]


def draw_cached_lengths(key, part):
    drawn = jax.random.randint(jax.random.fold_in(key, 21), (REQS,), 0, CTX - NEW + 1)
    longest = jax.random.randint(jax.random.fold_in(key, 22), (), 0, REQS)
    shortest = (longest + 1 + jax.random.randint(jax.random.fold_in(key, 23), (), 0, REQS - 1)) % REQS
    return drawn.at[longest].set(CTX - NEW).at[shortest].set(0).astype(jnp.int32)


def draw_cached(key, part):
    normal_part = jax.random.normal(jax.random.fold_in(key, 31), (REQS, CTX, KVW), jnp.float32)
    return jnp.clip(normal_part, -6.0, 6.0).astype(jnp.bfloat16)


def draw_tokens(key, part):
    normal_part = jax.random.normal(jax.random.fold_in(key, 41), (REQS, NEW, D), jnp.float32)
    return jnp.clip(normal_part, -6.0, 6.0).astype(jnp.bfloat16)


def block_levels(own_key, dims, cuts, smallest, largest):
    def one(axis_at, parts):
        draws = jax.random.uniform(jax.random.fold_in(jax.random.fold_in(own_key, 6), axis_at), (parts,), jnp.float32, smallest / len(cuts), largest / len(cuts))
        return jnp.repeat(jnp.exp(draws), dims[axis_at] // parts).reshape((-1,) + (1,) * (len(dims) - axis_at - 1))

    factor_of = one(*cuts[0])
    for cut in cuts[1:]:
        factor_of = factor_of * one(*cut)
    return factor_of


def length_profile(number_of, total, reach, lean):
    loads = [(1 << 20) // math.isqrt(standing ** lean) + 1 for standing in range(2, number_of + 1)]
    surplus, holding = total - reach - (number_of - 1), [1] * (number_of - 1)
    while surplus > 0:
        candidates = [i for i in range(number_of - 1) if holding[i] < reach]
        mass, left = sum([loads[i] for i in candidates]), surplus
        for i in candidates:
            extra = min(reach - holding[i], max(1, left * loads[i] // mass), surplus)
            holding[i] = holding[i] + extra
            surplus = surplus - extra
    return np.array([reach] + holding)


def uneven(stream_key, amount, total, limit, skew):
    if amount == 2:
        one = jax.random.randint(stream_key, (), max(1, total - limit), min(limit, total - 1) + 1)
        return jnp.stack([one, total - one])
    lengths = jnp.asarray(length_profile(amount, total, limit, skew), jnp.int32)
    twos = (amount - 1) // 2
    source_of, receiver = lengths[1:1 + 2 * twos:2], lengths[2:2 + 2 * twos:2]
    room = jnp.minimum(source_of - 1, limit - receiver)
    moved = jax.random.randint(jax.random.fold_in(stream_key, 1), (twos,), 0, 1 << 20) % (room + 1)
    lengths = lengths.at[1:1 + 2 * twos:2].set(source_of - moved).at[2:2 + 2 * twos:2].set(receiver + moved)
    return lengths[jax.random.permutation(jax.random.fold_in(stream_key, 2), amount)]


def bell_draw(stream_key, extent, scale, bound, pieces=(), kind=jnp.bfloat16):
    loudness = block_levels(stream_key, extent, pieces, -0.22, 0.18) if pieces else 1.0
    array = jax.random.normal(stream_key, extent, jnp.float32) * scale * loudness
    return jnp.minimum(jnp.maximum(array, -bound), bound).astype(kind)


def setup_inputs(seed: int = 0) -> dict:
    key_list = jax.random.split(jax.random.key(seed), 11)
    return {
        "tokens": draw_tokens(jax.random.fold_in(key_list[10], 71), 0),
        "cached": draw_cached(jax.random.fold_in(key_list[10], 71), 0),
        "norm_gains": jnp.clip(1.0 + 0.1 * jax.random.normal(key_list[2], (2, D), jnp.float32), 0.5, 1.5),
        "w_qkv": bell_draw(key_list[3], (D, D + KVW), D ** -0.5, 0.15625),
        "w_out": bell_draw(key_list[4], (D, D), D ** -0.5, 0.15625),
        "mlp_weights": bell_draw(key_list[5], (3, D, FF), D ** -0.5, 0.15625, ((2, 8),)),
        "request_order": draw_request_order(jax.random.fold_in(key_list[10], 71), 0),
        "new_lengths": uneven(key_list[7], REQS, REQS * NEW * 5 // 8, NEW, 2).astype(jnp.int32),
        "cached_lengths": draw_cached_lengths(jax.random.fold_in(key_list[10], 71), 0),
        "decode_slots": draw_decode_slots(jax.random.fold_in(key_list[10], 71), 0),
    }


epsilon = 1e-05
rope_base = 100000.0

def norm_rows(values, gain):
    widened = values.astype(jnp.float32)
    factor = lax.rsqrt(lax.optimization_barrier(jnp.mean(widened * widened, axis=-1, keepdims=True)) + epsilon)
    return (widened * factor * gain).astype(jnp.bfloat16)

def rotate(values, positions):
    half_dim = values.shape[-1] // 2
    frequency = rope_base ** (-2.0 * jnp.arange(half_dim, dtype=jnp.float32) / values.shape[-1])
    angles = positions[:, None, None] * frequency
    cosine = jnp.cos(angles)
    sine_part = jnp.sin(angles)
    leading = values[..., :half_dim]
    trailing = values[..., half_dim:]
    return jnp.concatenate([leading * cosine - trailing * sine_part, trailing * cosine + leading * sine_part], axis=-1)

def place_context(fresh_rows, cached_rows, new_count, cached_count):
    offsets = jnp.arange(NEW, dtype=jnp.int32)
    kept = jnp.where((offsets < new_count)[:, None], fresh_rows, jnp.zeros_like(fresh_rows))
    canvas = jnp.zeros((CTX, fresh_rows.shape[1]), fresh_rows.dtype)
    placed = lax.dynamic_update_slice_in_dim(canvas, kept, cached_count.astype(jnp.int32), 0)
    spots = jnp.arange(CTX, dtype=jnp.int32)
    return jnp.where((spots < cached_count)[:, None], cached_rows, placed)

def attend(queries, context, cached_count):
    group_size = HEADS // KV_HEADS
    key_width = KV_HEADS * HEAD_DIM
    key_heads = context[:, :key_width].reshape(CTX, KV_HEADS, HEAD_DIM).astype(jnp.float32)
    value_heads = context[:, key_width:].reshape(CTX, KV_HEADS, HEAD_DIM).astype(jnp.float32)
    grouped = queries.reshape(NEW, KV_HEADS, group_size, HEAD_DIM).astype(jnp.float32)
    scores = jnp.einsum('qkgd,pkd->kgqp', grouped, key_heads) * HEAD_DIM ** (-0.5)
    last_key = cached_count + jnp.arange(NEW, dtype=jnp.int32)
    allowed = jnp.arange(CTX, dtype=jnp.int32)[None, :] <= last_key[:, None]
    scores = jnp.where(allowed, scores, -jnp.inf)
    highest = lax.optimization_barrier(jnp.max(scores, axis=-1, keepdims=True))
    exponent = jnp.exp(scores - highest)
    weights = (exponent / lax.optimization_barrier(jnp.sum(exponent, axis=-1, keepdims=True))).astype(jnp.bfloat16)
    attended = jnp.einsum('kgqp,pkd->qkgd', weights.astype(jnp.float32), value_heads)
    return attended.reshape(NEW, HEADS * HEAD_DIM).astype(jnp.bfloat16)

def reference(tokens, cached, norm_gains, w_qkv, w_out, mlp_weights, request_order, new_lengths, cached_lengths, decode_slots):
    new_counts = new_lengths[request_order]
    cached_counts = cached_lengths[request_order]
    key_width = KV_HEADS * HEAD_DIM
    down_wide = mlp_weights[2].reshape(D, N_TENSOR, FF // N_TENSOR).astype(jnp.float32)

    def one_request(inputs):
        request_tokens, request_cache, new_count, cached_count = inputs
        normed = norm_rows(request_tokens, norm_gains[0])
        projected = jnp.dot(normed, w_qkv, preferred_element_type=jnp.float32)
        positions = (cached_count + jnp.arange(NEW, dtype=jnp.int32)).astype(jnp.float32)
        queries = rotate(projected[:, :D].reshape(NEW, HEADS, HEAD_DIM), positions).astype(jnp.bfloat16)
        key_rows = rotate(projected[:, D:D + key_width].reshape(NEW, KV_HEADS, HEAD_DIM), positions).reshape(NEW, key_width)
        fresh_rows = jnp.concatenate([key_rows, projected[:, D + key_width:]], axis=1).astype(jnp.bfloat16)
        context = place_context(fresh_rows, request_cache, new_count, cached_count)
        attended = attend(queries, context, cached_count)
        residual = (request_tokens.astype(jnp.float32) + jnp.dot(attended, w_out, preferred_element_type=jnp.float32)).astype(jnp.bfloat16)
        post_norm = norm_rows(residual, norm_gains[1])
        gate_out = jnp.dot(post_norm, mlp_weights[0], preferred_element_type=jnp.float32)
        up_out = jnp.dot(post_norm, mlp_weights[1], preferred_element_type=jnp.float32)
        activated = (jax.nn.silu(gate_out) * up_out).astype(jnp.bfloat16)
        spread = activated.reshape(NEW, N_TENSOR, FF // N_TENSOR).astype(jnp.float32)
        partial_sums = jnp.einsum('rmw,dmw->mrd', spread, down_wide).astype(jnp.bfloat16)
        mlp_sum = lax.optimization_barrier(jnp.sum(partial_sums.astype(jnp.float32), axis=0))
        live = (jnp.arange(NEW, dtype=jnp.int32) < new_count)[:, None]
        layer_rows = jnp.where(live, residual.astype(jnp.float32) + mlp_sum, 0.0).astype(jnp.bfloat16)
        return (layer_rows, context)
    outputs, contexts = lax.map(one_request, (tokens, cached, new_counts, cached_counts))
    request_at_slot = jnp.argsort(decode_slots)
    prefill_of_request = jnp.argsort(request_order)
    kv_decode = contexts[prefill_of_request[request_at_slot]]
    return (outputs, kv_decode)
```

```python
import functools

import jax
import jax.numpy as jnp
import numpy as np
from jax import lax
from jax.experimental import pallas as pl
from jax.experimental.pallas import tpu as pltpu
from jax.sharding import PartitionSpec as P

HEADS = 16
KV_HEADS = 8
HEAD_DIM = 96
GROUP = 384
VMEM = 48 * 1024 * 1024

epsilon = 1e-05
rope_base = 100000.0
bf16 = jnp.bfloat16
f32 = jnp.float32


def frequencies():
    half = HEAD_DIM // 2
    steps = np.arange(half, dtype=np.float32)
    frequency = np.float32(rope_base) ** (np.float32(-2.0) * steps / np.float32(HEAD_DIM))
    row = np.zeros((1, 128), np.float32)
    row[0, :half] = frequency
    row[0, half:HEAD_DIM] = frequency
    return row


def norm_value(values, gain):
    factor = lax.rsqrt(jnp.mean(values * values, axis=-1, keepdims=True) + epsilon)
    return (values * factor * gain).astype(bf16)


def rotate(values, cosine, sine):
    width = values.shape[-1]
    half = HEAD_DIM // 2
    lane = lax.broadcasted_iota(jnp.int32, values.shape, 1)
    first = lax.rem(lane, HEAD_DIM) < half
    swapped = jnp.where(
        first, pltpu.roll(values, width - half, 1), pltpu.roll(values, half, 1)
    )
    return values * cosine + swapped * sine


def place(fresh, cached, new_count, cached_count):
    rows, new = cached.shape[0], fresh.shape[0]
    spot = lax.broadcasted_iota(jnp.int32, (rows, new), 0)
    token = lax.broadcasted_iota(jnp.int32, (rows, new), 1)
    chosen = (spot - cached_count == token) & (token < new_count)
    placed = jnp.dot(jnp.where(chosen, 1.0, 0.0).astype(bf16), fresh, preferred_element_type=f32)
    keep = lax.broadcasted_iota(jnp.int32, cached.shape, 0) < cached_count
    return jnp.where(keep, cached.astype(f32), placed).astype(bf16)


def key_kernel(
    order, news, olds, dev, tokens, gain, freq, weight, cached, context, normed, cosine, sine
):
    reqs, new, width = tokens.shape

    @pl.when(pl.program_id(0) == 0)
    def _():
        lane = lax.broadcasted_iota(jnp.int32, (new, 128), 1)
        row = lax.broadcasted_iota(jnp.int32, (new, 128), 0)
        sign = jnp.where(lane < HEAD_DIM // 2, -1.0, 1.0)
        for r in range(reqs):
            normed[r] = norm_value(tokens[r].astype(f32), gain[0:1, :])
            old = olds[order[dev[0] * reqs + r]]
            angles = (row + old).astype(f32) * freq[...]
            cos_part = jnp.cos(angles)[:, :HEAD_DIM]
            sin_part = (jnp.sin(angles) * sign)[:, :HEAD_DIM]
            cosine[r] = jnp.concatenate([cos_part] * 4, axis=1)
            sine[r] = jnp.concatenate([sin_part] * 4, axis=1)

    rows = normed[...].reshape(reqs * new, width)
    projected = jnp.dot(rows, weight[...], preferred_element_type=f32)
    turned = rotate(
        projected,
        cosine[...].reshape(reqs * new, GROUP),
        sine[...].reshape(reqs * new, GROUP),
    ).astype(bf16)
    parts, _, depth, _ = context.shape
    for r in range(reqs):
        request = order[dev[0] * reqs + r]
        merged = place(turned[r * new : (r + 1) * new], cached[r], news[request], olds[request])
        context[:, r] = merged.reshape(parts, depth, GROUP)


def value_kernel(order, news, olds, dev, normed, weight, cached, context):
    reqs, new, width = normed.shape
    rows = normed[...].reshape(reqs * new, width)
    projected = jnp.dot(rows, weight[...], preferred_element_type=f32).astype(bf16)
    parts, _, depth, _ = context.shape
    for r in range(reqs):
        request = order[dev[0] * reqs + r]
        merged = place(projected[r * new : (r + 1) * new], cached[r], news[request], olds[request])
        context[:, r] = merged.reshape(parts, depth, GROUP)


def attention_kernel(
    order, olds, dev, normed, cosine, sine, weight, keys, values, w_out, tokens, gain,
    residual, post, total, attended,
):
    step = pl.program_id(0)
    reqs, new, width = normed.shape
    parts, _, depth, _ = keys.shape
    ctx = parts * depth
    flat = reqs * new
    rows = normed[...].reshape(flat, width)
    projected = jnp.dot(rows, weight[...], preferred_element_type=f32)
    cos_part = cosine[...].reshape(flat, GROUP)
    sin_part = sine[...].reshape(flat, GROUP)
    queries = [
        rotate(projected[:, GROUP * i : GROUP * (i + 1)], cos_part, sin_part).astype(bf16)
        for i in range(2)
    ]
    spot = lax.broadcasted_iota(jnp.int32, (new, ctx), 1)
    token = lax.broadcasted_iota(jnp.int32, (new, ctx), 0)
    for r in range(reqs):
        old = olds[order[dev[0] * reqs + r]]
        key_rows = keys[:, r].reshape(ctx, GROUP)
        value_rows = values[:, r].reshape(ctx, GROUP)
        allowed = spot <= old + token
        pieces = []
        for k in range(4):
            key = key_rows[:, HEAD_DIM * k : HEAD_DIM * (k + 1)]
            value = value_rows[:, HEAD_DIM * k : HEAD_DIM * (k + 1)]
            for h in (2 * k, 2 * k + 1):
                place_at = HEAD_DIM * (h % 4)
                query = queries[h // 4][r * new : (r + 1) * new, place_at : place_at + HEAD_DIM]
                scores = lax.dot_general(
                    query, key, (((1,), (1,)), ((), ())), preferred_element_type=f32
                )
                scores = jnp.where(allowed, scores * HEAD_DIM ** (-0.5), -jnp.inf)
                highest = jnp.max(scores, axis=-1, keepdims=True)
                exponent = jnp.exp(scores - highest)
                weights = (exponent / jnp.sum(exponent, axis=-1, keepdims=True)).astype(bf16)
                pieces.append(jnp.dot(weights, value, preferred_element_type=f32))
        attended[r * new : (r + 1) * new, :] = jnp.concatenate(pieces, axis=1).astype(bf16)
    term = jnp.dot(attended[...], w_out[...], preferred_element_type=f32)

    @pl.when(step == 0)
    def _():
        total[...] = tokens[...].astype(f32).reshape(flat, width) + term

    @pl.when(step > 0)
    def _():
        total[...] += term

    @pl.when(step == pl.num_programs(0) - 1)
    def _():
        rounded = total[...].astype(bf16)
        residual[...] = rounded
        post[...] = norm_value(rounded.astype(f32), gain[1:2, :])


def mlp_kernel(rows, own, other, out, total):
    step = pl.program_id(0)
    values = rows[...]
    term = None
    for weights in (own, other):
        gate = jnp.dot(values, weights[0], preferred_element_type=f32)
        up = jnp.dot(values, weights[1], preferred_element_type=f32)
        hidden = (gate / (1.0 + jnp.exp(-gate)) * up).astype(bf16)
        product = lax.dot_general(
            hidden, weights[2], (((1,), (1,)), ((), ())), preferred_element_type=f32
        )
        term = product if term is None else term + product

    @pl.when(step == 0)
    def _():
        total[...] = term

    @pl.when(step > 0)
    def _():
        total[...] += term

    @pl.when(step == pl.num_programs(0) - 1)
    def _():
        out[...] = total[...].astype(bf16)


def pack_kernel(rank, source, target, sems):
    copies = [
        pltpu.make_async_copy(source.at[i], target.at[rank[i]], sems.at[i])
        for i in range(source.shape[0])
    ]
    for copy in copies:
        copy.start()
    for copy in copies:
        copy.wait()


def unpack_kernel(columns, rows, source, *rest):
    target, sems = rest[-2], rest[-1]
    width = source.shape[-1]
    copies = [
        pltpu.make_async_copy(
            source.at[rows[i]], target.at[i, :, pl.ds(columns, width)], sems.at[i]
        )
        for i in range(source.shape[0])
    ]
    for copy in copies:
        copy.start()
    for copy in copies:
        copy.wait()


def call(kernel, prefetched, grid, in_specs, out_specs, out_shape, scratch, operands, cost=None, aliases={}):
    return pl.pallas_call(
        kernel,
        out_shape=out_shape,
        grid_spec=pltpu.PrefetchScalarGridSpec(
            num_scalar_prefetch=len(prefetched),
            grid=grid,
            in_specs=in_specs,
            out_specs=out_specs,
            scratch_shapes=scratch,
        ),
        compiler_params=pltpu.CompilerParams(vmem_limit_bytes=VMEM),
        cost_estimate=cost,
        input_output_aliases=aliases,
    )(*prefetched, *operands)


def shape(dims, dtype=bf16):
    return jax.ShapeDtypeStruct(dims, dtype)


def whole(dims):
    return pl.BlockSpec(dims, lambda *_: (0,) * len(dims))


def local(
    tokens,
    cached,
    norm_gains,
    w_qkv,
    w_out,
    mlp_weights,
    request_order,
    new_lengths,
    cached_lengths,
    decode_slots,
):
    tensor_size = lax.axis_size("tensor")
    group_total = lax.axis_size("dp")
    reqs, new, width = tokens.shape
    ctx = cached.shape[1]
    depth = ctx // tensor_size
    flat = reqs * new
    group_reqs = reqs * tensor_size
    group_index = lax.axis_index("dp")
    device = group_index * tensor_size + lax.axis_index("tensor")
    dev = device.astype(jnp.int32).reshape(1)
    key_width = KV_HEADS * HEAD_DIM
    groups = key_width // GROUP
    scalars = (request_order, new_lengths, cached_lengths, dev)
    freq = jnp.asarray(frequencies())

    other_weights = lax.ppermute(
        mlp_weights, "tensor", [(t, t ^ 1) for t in range(tensor_size)]
    )

    context_shape = (tensor_size, reqs, depth, key_width)
    context_spec = pl.BlockSpec((tensor_size, reqs, depth, GROUP), lambda g, *_: (0, 0, 0, g))
    table = (reqs, new, GROUP)
    keys, normed, cosine, sine = call(
        key_kernel,
        scalars,
        (groups,),
        [
            whole(tokens.shape),
            whole(norm_gains.shape),
            whole((1, 128)),
            pl.BlockSpec((width, GROUP), lambda g, *_: (0, width // GROUP + g)),
            pl.BlockSpec((reqs, ctx, GROUP), lambda g, *_: (0, 0, g)),
        ],
        [context_spec, whole(tokens.shape), whole(table), whole(table)],
        [shape(context_shape), shape(tokens.shape), shape(table, f32), shape(table, f32)],
        [],
        (tokens, norm_gains, freq, w_qkv, cached),
        pl.CostEstimate(flops=2 * flat * width * key_width, bytes_accessed=8 << 20, transcendentals=0),
    )
    keys_moved = lax.all_to_all(keys, "tensor", split_axis=0, concat_axis=0, tiled=True)
    values = call(
        value_kernel,
        scalars,
        (groups,),
        [
            whole(tokens.shape),
            pl.BlockSpec((width, GROUP), lambda g, *_: (0, (width + key_width) // GROUP + g)),
            pl.BlockSpec((reqs, ctx, GROUP), lambda g, *_: (0, 0, groups + g)),
        ],
        context_spec,
        shape(context_shape),
        [],
        (normed, w_qkv, cached),
        pl.CostEstimate(flops=2 * flat * width * key_width, bytes_accessed=8 << 20, transcendentals=0),
    )
    values_moved = lax.all_to_all(values, "tensor", split_axis=0, concat_axis=0, tiled=True)

    residual, post = call(
        attention_kernel,
        (request_order, cached_lengths, dev),
        (groups,),
        [
            whole(tokens.shape),
            whole(table),
            whole(table),
            pl.BlockSpec((width, 2 * GROUP), lambda g, *_: (0, g)),
            context_spec,
            context_spec,
            pl.BlockSpec((2 * GROUP, width), lambda g, *_: (g, 0)),
            whole(tokens.shape),
            whole(norm_gains.shape),
        ],
        [whole((flat, width))] * 2,
        [shape((flat, width))] * 2,
        [pltpu.VMEM((flat, width), f32), pltpu.VMEM((flat, 2 * GROUP), bf16)],
        (normed, cosine, sine, w_qkv, keys, values, w_out, tokens, norm_gains),
        pl.CostEstimate(flops=12 * flat * width * width, bytes_accessed=16 << 20, transcendentals=0),
    )

    units = mlp_weights.shape[2]
    chunk = 256 if units % 256 == 0 else units

    def mlp(rows):
        return call(
            mlp_kernel,
            (),
            (units // chunk,),
            [
                whole((flat, width)),
                pl.BlockSpec((3, width, chunk), lambda c: (0, 0, c)),
                pl.BlockSpec((3, width, chunk), lambda c: (0, 0, c)),
            ],
            whole((flat, width)),
            shape((flat, width)),
            [pltpu.VMEM((flat, width), f32)],
            (rows, mlp_weights, other_weights),
            pl.CostEstimate(flops=12 * flat * width * units, bytes_accessed=12 * width * units, transcendentals=0),
        )

    partners = [
        [(t, t ^ (2 * s)) for t in range(tensor_size)] for s in range(1, tensor_size // 2)
    ]
    arrivals = [lax.ppermute(post, "tensor", pairs) for pairs in partners]
    partials = [mlp(post)]
    for pairs, rows in zip(partners, arrivals):
        partials.append(lax.ppermute(mlp(rows), "tensor", pairs))

    every = request_order.shape[0]
    indices = jnp.arange(every, dtype=jnp.int32)
    slot_of = jnp.sum(
        jnp.where(request_order[:, None] == indices[None, :], decode_slots[None, :], 0), axis=1
    )
    count_of = jnp.sum(
        jnp.where(request_order[:, None] == indices[None, :], new_lengths[None, :], 0), axis=1
    )
    own_slots = lax.dynamic_slice_in_dim(slot_of, group_index * group_reqs, group_reqs)
    rank = jnp.sum((own_slots[None, :] < own_slots[:, None]).astype(jnp.int32), axis=1)
    slot_ids = group_index * group_reqs + jnp.arange(group_reqs, dtype=jnp.int32)
    owners = jnp.sum(
        jnp.where(slot_of[None, :] == slot_ids[:, None], indices[None, :] // group_reqs, 0), axis=1
    )
    per_group = group_reqs // group_total
    ordinal = jnp.arange(group_reqs, dtype=jnp.int32)
    same_owner = (owners[:, None] == owners[None, :]) & (ordinal[None, :] < ordinal[:, None])
    source_rows = owners * per_group + jnp.sum(same_owner.astype(jnp.int32), axis=1)

    half_shape = (group_reqs, depth, key_width)
    anywhere = pl.BlockSpec(memory_space=pl.ANY)
    sems = [pltpu.SemaphoreType.DMA((group_reqs,))]

    def across(moved):
        packed = call(
            pack_kernel, (rank,), (1,), [anywhere], anywhere, shape(half_shape), sems,
            (moved.reshape(half_shape),),
            pl.CostEstimate(flops=0, bytes_accessed=6 << 20, transcendentals=0),
        )
        return lax.all_to_all(packed, "dp", split_axis=0, concat_axis=0, tiled=True)

    keys_arrived = across(keys_moved)
    values_arrived = across(values_moved)
    full_shape = shape((group_reqs, depth, 2 * key_width))
    kv_half = call(
        functools.partial(unpack_kernel, 0), (source_rows,), (1,), [anywhere], anywhere,
        full_shape, sems, (keys_arrived,),
        pl.CostEstimate(flops=0, bytes_accessed=6 << 20, transcendentals=0),
    )
    kv_decode = call(
        functools.partial(unpack_kernel, key_width), (source_rows,), (1,), [anywhere, anywhere],
        anywhere, full_shape, sems, (values_arrived, kv_half),
        pl.CostEstimate(flops=0, bytes_accessed=6 << 20, transcendentals=0), {2: 0},
    )

    own_counts = lax.dynamic_slice_in_dim(count_of, device * reqs, reqs)
    live = (jnp.arange(new, dtype=jnp.int32)[None, :] < own_counts[:, None]).reshape(flat, 1)
    total = residual.astype(f32)
    for partial in partials:
        total = total + partial.astype(f32)
    layer_out = jnp.where(live, total, 0.0).astype(bf16).reshape(reqs, new, width)
    return (layer_out, kv_decode)


def solution(mesh):
    in_specs = (
        P(("dp", "tensor"), None, None),
        P(("dp", "tensor"), None, None),
        P(),
        P(),
        P(),
        P(None, None, "tensor"),
        P(),
        P(),
        P(),
        P(),
    )
    out_specs = (P(("dp", "tensor"), None, None), P("dp", "tensor", None))
    return jax.shard_map(local, mesh=mesh, in_specs=in_specs, out_specs=out_specs, check_vma=False)
```

```python
import functools
import math

import jax
import jax.numpy as jnp
import numpy as np
from jax import lax
from jax.experimental import pallas as pl
from jax.experimental.pallas import tpu as pltpu
from jax.sharding import PartitionSpec as P

HEADS = 16
KV_HEADS = 8
HEAD_DIM = 96
GROUP = 384
VMEM = 60 * 1024 * 1024

epsilon = 1e-05
rope_base = 100000.0
bf16 = jnp.bfloat16
f32 = jnp.float32


def frequencies():
    half = HEAD_DIM // 2
    steps = np.arange(half, dtype=np.float32)
    frequency = np.float32(rope_base) ** (np.float32(-2.0) * steps / np.float32(HEAD_DIM))
    row = np.zeros((1, 128), np.float32)
    row[0, :half] = frequency
    row[0, half:HEAD_DIM] = frequency
    return row


def norm_value(values, gain):
    factor = lax.rsqrt(jnp.mean(values * values, axis=-1, keepdims=True) + epsilon)
    return (values * factor * gain).astype(bf16)


def rotate(values, cosine, sine):
    width = values.shape[-1]
    half = HEAD_DIM // 2
    lane = lax.broadcasted_iota(jnp.int32, values.shape, 1)
    first = lax.rem(lane, HEAD_DIM) < half
    swapped = jnp.where(
        first, pltpu.roll(values, width - half, 1), pltpu.roll(values, half, 1)
    )
    return values * cosine + swapped * sine


def place(fresh, cached, new_count, cached_count):
    rows, new = cached.shape[0], fresh.shape[0]
    spot = lax.broadcasted_iota(jnp.int32, (rows, new), 0)
    token = lax.broadcasted_iota(jnp.int32, (rows, new), 1)
    chosen = (spot - cached_count == token) & (token < new_count)
    placed = jnp.dot(jnp.where(chosen, 1.0, 0.0).astype(bf16), fresh, preferred_element_type=f32)
    keep = lax.broadcasted_iota(jnp.int32, cached.shape, 0) < cached_count
    return jnp.where(keep, cached.astype(f32), placed).astype(bf16)


def key_kernel(
    order, news, olds, dev, tokens, gain, freq, weight, cached, context, normed, cosine, sine
):
    reqs, new, width = tokens.shape

    @pl.when(pl.program_id(0) == 0)
    def _():
        lane = lax.broadcasted_iota(jnp.int32, (new, 128), 1)
        row = lax.broadcasted_iota(jnp.int32, (new, 128), 0)
        sign = jnp.where(lane < HEAD_DIM // 2, -1.0, 1.0)
        for r in range(reqs):
            normed[r] = norm_value(tokens[r].astype(f32), gain[0:1, :])
            old = olds[order[dev[0] * reqs + r]]
            angles = (row + old).astype(f32) * freq[...]
            cos_part = jnp.cos(angles)[:, :HEAD_DIM]
            sin_part = (jnp.sin(angles) * sign)[:, :HEAD_DIM]
            cosine[r] = jnp.concatenate([cos_part] * 4, axis=1)
            sine[r] = jnp.concatenate([sin_part] * 4, axis=1)

    rows = normed[...].reshape(reqs * new, width)
    projected = jnp.dot(rows, weight[...], preferred_element_type=f32)
    turned = rotate(
        projected,
        cosine[...].reshape(reqs * new, GROUP),
        sine[...].reshape(reqs * new, GROUP),
    ).astype(bf16)
    parts, _, depth, _ = context.shape
    for r in range(reqs):
        request = order[dev[0] * reqs + r]
        merged = place(turned[r * new : (r + 1) * new], cached[r], news[request], olds[request])
        context[:, r] = merged.reshape(parts, depth, GROUP)


def value_kernel(order, news, olds, dev, normed, weight, cached, context):
    reqs, new, width = normed.shape
    rows = normed[...].reshape(reqs * new, width)
    projected = jnp.dot(rows, weight[...], preferred_element_type=f32).astype(bf16)
    parts, _, depth, _ = context.shape
    for r in range(reqs):
        request = order[dev[0] * reqs + r]
        merged = place(projected[r * new : (r + 1) * new], cached[r], news[request], olds[request])
        context[:, r] = merged.reshape(parts, depth, GROUP)


def attention_kernel(
    order, olds, dev, normed, cosine, sine, weight, keys, values, w_out, tokens, gain,
    residual, post, total, attended,
):
    step = pl.program_id(0)
    reqs, new, width = normed.shape
    parts, _, depth, _ = keys.shape
    ctx = parts * depth
    flat = reqs * new
    rows = normed[...].reshape(flat, width)
    projected = jnp.dot(rows, weight[...], preferred_element_type=f32)
    cos_part = cosine[...].reshape(flat, GROUP)
    sin_part = sine[...].reshape(flat, GROUP)
    queries = [
        rotate(projected[:, GROUP * i : GROUP * (i + 1)], cos_part, sin_part).astype(bf16)
        for i in range(2)
    ]
    spot = lax.broadcasted_iota(jnp.int32, (new, ctx), 1)
    token = lax.broadcasted_iota(jnp.int32, (new, ctx), 0)
    scale = HEAD_DIM ** (-0.5) * math.log2(math.e)
    for r in range(reqs):
        old = olds[order[dev[0] * reqs + r]]
        key_rows = keys[:, r].reshape(ctx, GROUP)
        value_rows = values[:, r].reshape(ctx, GROUP)
        mask = jnp.where(spot <= old + token, 0.0, -jnp.inf)
        bias = jnp.concatenate([mask, mask], axis=0)
        pieces = []
        for k in range(4):
            key = key_rows[:, HEAD_DIM * k : HEAD_DIM * (k + 1)]
            value = value_rows[:, HEAD_DIM * k : HEAD_DIM * (k + 1)]
            pair = []
            for h in (2 * k, 2 * k + 1):
                at = HEAD_DIM * (h % 4)
                pair.append(queries[h // 4][r * new : (r + 1) * new, at : at + HEAD_DIM])
            scores = lax.dot_general(
                jnp.concatenate(pair, axis=0), key, (((1,), (1,)), ((), ())),
                preferred_element_type=f32,
            )
            scores = scores * scale + bias
            exponent = jnp.exp2(scores - jnp.max(scores, axis=-1, keepdims=True))
            bottom = jnp.sum(exponent, axis=-1, keepdims=True)
            mixed = jnp.dot(exponent.astype(bf16), value, preferred_element_type=f32) / bottom
            pieces += [mixed[:new], mixed[new:]]
        attended[r * new : (r + 1) * new, :] = jnp.concatenate(pieces, axis=1).astype(bf16)
    term = jnp.dot(attended[...], w_out[...], preferred_element_type=f32)

    @pl.when(step == 0)
    def _():
        total[...] = tokens[...].astype(f32).reshape(flat, width) + term

    @pl.when(step > 0)
    def _():
        total[...] += term

    @pl.when(step == pl.num_programs(0) - 1)
    def _():
        rounded = total[...].astype(bf16)
        residual[...] = rounded
        post[...] = norm_value(rounded.astype(f32), gain[1:2, :])


def mlp_kernel(own, other, *refs):
    total = refs[-1]
    inputs = refs[: (len(refs) - 1) // 2]
    outputs = refs[(len(refs) - 1) // 2 : -1]
    step = pl.program_id(0)
    flat = inputs[0].shape[0]
    values = jnp.concatenate([rows[...] for rows in inputs], axis=0)
    term = None
    for weights in (own, other):
        gate = jnp.dot(values, weights[0], preferred_element_type=f32)
        up = jnp.dot(values, weights[1], preferred_element_type=f32)
        hidden = (gate / (1.0 + jnp.exp(-gate)) * up).astype(bf16)
        product = lax.dot_general(
            hidden, weights[2], (((1,), (1,)), ((), ())), preferred_element_type=f32
        )
        term = product if term is None else term + product

    @pl.when(step == 0)
    def _():
        total[...] = term

    @pl.when(step > 0)
    def _():
        total[...] += term

    @pl.when(step == pl.num_programs(0) - 1)
    def _():
        for i, out in enumerate(outputs):
            out[...] = total[i * flat : (i + 1) * flat].astype(bf16)


def run_copies(copies):
    for copy in copies:
        copy.start()
    for copy in copies:
        copy.wait()


def pack_kernel(picked, source, *rest):
    targets, sems = rest[:-1], rest[-1]
    share = targets[0].shape[0]
    run_copies(
        [
            pltpu.make_async_copy(
                source.at[picked[s * share + k]], target.at[k], sems.at[s * share + k]
            )
            for s, target in enumerate(targets)
            for k in range(share)
        ]
    )


def unpack_kernel(columns, count, spots, *refs):
    sources, target, sems = refs[:count], refs[-2], refs[-1]
    share, _, width = sources[0].shape
    run_copies(
        [
            pltpu.make_async_copy(
                source.at[k],
                target.at[spots[s * share + k], :, pl.ds(columns, width)],
                sems.at[s * share + k],
            )
            for s, source in enumerate(sources)
            for k in range(share)
        ]
    )


def call(
    kernel, prefetched, grid, in_specs, out_specs, out_shape, scratch, operands,
    flops=0, moved=6 << 20, aliases={}, after=(),
):
    begin = len(prefetched) + len(operands)

    def ordered(*refs):
        kernel(*refs[:begin], *refs[begin + len(after) :])

    return pl.pallas_call(
        ordered,
        out_shape=out_shape,
        grid_spec=pltpu.PrefetchScalarGridSpec(
            num_scalar_prefetch=len(prefetched),
            grid=grid,
            in_specs=list(in_specs) + [pl.BlockSpec(memory_space=pl.ANY)] * len(after),
            out_specs=out_specs,
            scratch_shapes=scratch,
        ),
        compiler_params=pltpu.CompilerParams(vmem_limit_bytes=VMEM),
        cost_estimate=pl.CostEstimate(flops=flops, bytes_accessed=moved, transcendentals=0),
        input_output_aliases=aliases,
    )(*prefetched, *operands, *after)


def shape(dims, dtype=bf16):
    return jax.ShapeDtypeStruct(dims, dtype)


def whole(dims):
    return pl.BlockSpec(dims, lambda *_: (0,) * len(dims))


def local(
    tokens,
    cached,
    norm_gains,
    w_qkv,
    w_out,
    mlp_weights,
    request_order,
    new_lengths,
    cached_lengths,
    decode_slots,
):
    tensor_size = lax.axis_size("tensor")
    group_total = lax.axis_size("dp")
    reqs, new, width = tokens.shape
    ctx = cached.shape[1]
    depth = ctx // tensor_size
    flat = reqs * new
    group_reqs = reqs * tensor_size
    group_index = lax.axis_index("dp")
    device = group_index * tensor_size + lax.axis_index("tensor")
    dev = device.astype(jnp.int32).reshape(1)
    key_width = KV_HEADS * HEAD_DIM
    groups = key_width // GROUP
    scalars = (request_order, new_lengths, cached_lengths, dev)
    freq = jnp.asarray(frequencies())

    other_weights = lax.ppermute(
        mlp_weights, "tensor", [(t, t ^ 1) for t in range(tensor_size)]
    )

    context_shape = (tensor_size, reqs, depth, key_width)
    context_spec = pl.BlockSpec((tensor_size, reqs, depth, GROUP), lambda g, *_: (0, 0, 0, g))
    table = (reqs, new, GROUP)
    keys, normed, cosine, sine = call(
        key_kernel,
        scalars,
        (groups,),
        [
            whole(tokens.shape),
            whole(norm_gains.shape),
            whole((1, 128)),
            pl.BlockSpec((width, GROUP), lambda g, *_: (0, width // GROUP + g)),
            pl.BlockSpec((reqs, ctx, GROUP), lambda g, *_: (0, 0, g)),
        ],
        [context_spec, whole(tokens.shape), whole(table), whole(table)],
        [shape(context_shape), shape(tokens.shape), shape(table, f32), shape(table, f32)],
        [],
        (tokens, norm_gains, freq, w_qkv, cached),
        2 * flat * width * key_width,
        8 << 20,
    )
    keys_moved = lax.all_to_all(keys, "tensor", split_axis=0, concat_axis=0, tiled=True)
    values = call(
        value_kernel,
        scalars,
        (groups,),
        [
            whole(tokens.shape),
            pl.BlockSpec((width, GROUP), lambda g, *_: (0, (width + key_width) // GROUP + g)),
            pl.BlockSpec((reqs, ctx, GROUP), lambda g, *_: (0, 0, groups + g)),
        ],
        context_spec,
        shape(context_shape),
        [],
        (normed, w_qkv, cached),
        2 * flat * width * key_width,
        8 << 20,
    )
    values_moved = lax.all_to_all(values, "tensor", split_axis=0, concat_axis=0, tiled=True)

    residual, post = call(
        attention_kernel,
        (request_order, cached_lengths, dev),
        (groups,),
        [
            whole(tokens.shape),
            whole(table),
            whole(table),
            pl.BlockSpec((width, 2 * GROUP), lambda g, *_: (0, g)),
            context_spec,
            context_spec,
            pl.BlockSpec((2 * GROUP, width), lambda g, *_: (g, 0)),
            whole(tokens.shape),
            whole(norm_gains.shape),
        ],
        [whole((flat, width))] * 2,
        [shape((flat, width))] * 2,
        [pltpu.VMEM((flat, width), f32), pltpu.VMEM((flat, 2 * GROUP), bf16)],
        (normed, cosine, sine, w_qkv, keys, values, w_out, tokens, norm_gains),
        12 * flat * width * width,
        16 << 20,
    )

    units = mlp_weights.shape[2]
    chunk = 256 if units % 256 == 0 else units

    def mlp(pieces, after):
        count = len(pieces)
        weight_spec = pl.BlockSpec((3, width, chunk), lambda c: (0, 0, c))
        return call(
            mlp_kernel,
            (),
            (units // chunk,),
            [weight_spec] * 2 + [whole((flat, width))] * count,
            [whole((flat, width))] * count,
            [shape((flat, width))] * count,
            [pltpu.VMEM((count * flat, width), f32)],
            (mlp_weights, other_weights, *pieces),
            12 * count * flat * width * units,
            12 * width * units,
            after=after,
        )

    every = request_order.shape[0]
    indices = jnp.arange(every, dtype=jnp.int32)
    slot_of = jnp.sum(
        jnp.where(request_order[:, None] == indices[None, :], decode_slots[None, :], 0), axis=1
    )
    count_of = jnp.sum(
        jnp.where(request_order[:, None] == indices[None, :], new_lengths[None, :], 0), axis=1
    )
    ordinal = jnp.arange(group_reqs, dtype=jnp.int32)

    def inverse(keys_of):
        position = jnp.sum((keys_of[None, :] < keys_of[:, None]).astype(jnp.int32), axis=1)
        return jnp.sum(
            jnp.where(position[None, :] == ordinal[:, None], ordinal[None, :], 0), axis=1
        )

    own_slots = lax.dynamic_slice_in_dim(slot_of, group_index * group_reqs, group_reqs)
    goal = lax.rem(own_slots // group_reqs - group_index + group_total, group_total)
    picked = inverse(goal * group_reqs + lax.rem(own_slots, group_reqs))
    slot_ids = group_index * group_reqs + ordinal
    owners = jnp.sum(
        jnp.where(slot_of[None, :] == slot_ids[:, None], indices[None, :] // group_reqs, 0), axis=1
    )
    origin = lax.rem(group_index - owners + group_total, group_total)
    spots = inverse(origin * group_reqs + ordinal)

    share = group_reqs // group_total
    piece = (share, depth, key_width)
    anywhere = pl.BlockSpec(memory_space=pl.ANY)
    sems = [pltpu.SemaphoreType.DMA((group_reqs,))]
    shifts = [
        [(g, (g + s) % group_total) for g in range(group_total)] for s in range(1, group_total)
    ]

    def pack(moved, after):
        return call(
            pack_kernel, (picked,), (1,), [anywhere], [anywhere] * group_total,
            [shape(piece)] * group_total, sems, (moved.reshape(group_reqs, depth, key_width),),
            after=after,
        )

    def across(packed):
        return [packed[0]] + [
            lax.ppermute(rows, "dp", pairs) for rows, pairs in zip(packed[1:], shifts)
        ]

    def unpack(columns, arrived, target, after):
        return call(
            functools.partial(unpack_kernel, columns, group_total), (spots,), (1,),
            [anywhere] * (group_total + len(target)), anywhere,
            shape((group_reqs, depth, 2 * key_width)), sems, (*arrived, *target),
            aliases={1 + group_total: 0} if target else {}, after=after,
        )

    partners = [
        [(t, t ^ (2 * s)) for t in range(tensor_size)] for s in range(1, tensor_size // 2)
    ]
    gathered = [lax.ppermute(post, "tensor", pairs) for pairs in partners]
    keys_packed = pack(keys_moved, (post,))
    keys_arrived = across(keys_packed)
    partials = list(mlp([post], (keys_packed[0],)))
    values_packed = pack(values_moved, (partials[0],))
    values_arrived = across(values_packed)
    latest = values_packed[0]
    batches = [range(0, 2)] + [range(s, min(s + 2, len(partners))) for s in range(2, len(partners), 2)]
    for batch in batches:
        results = mlp([gathered[s] for s in batch], (latest,))
        latest = results[0]
        partials += [lax.ppermute(rows, "tensor", partners[s]) for s, rows in zip(batch, results)]
    kv_half = unpack(0, keys_arrived, (), (latest,))
    kv_decode = unpack(key_width, values_arrived, (kv_half,), ())

    own_counts = lax.dynamic_slice_in_dim(count_of, device * reqs, reqs)
    live = (jnp.arange(new, dtype=jnp.int32)[None, :] < own_counts[:, None]).reshape(flat, 1)
    total = residual.astype(f32)
    for partial in partials:
        total = total + partial.astype(f32)
    layer_out = jnp.where(live, total, 0.0).astype(bf16).reshape(reqs, new, width)
    return (layer_out, kv_decode)


def solution(mesh):
    in_specs = (
        P(("dp", "tensor"), None, None),
        P(("dp", "tensor"), None, None),
        P(),
        P(),
        P(),
        P(None, None, "tensor"),
        P(),
        P(),
        P(),
        P(),
    )
    out_specs = (P(("dp", "tensor"), None, None), P("dp", "tensor", None))
    return jax.shard_map(local, mesh=mesh, in_specs=in_specs, out_specs=out_specs, check_vma=False)
```

```python
import functools
import math

import jax
import jax.numpy as jnp
import numpy as np
from jax import lax
from jax.experimental import pallas as pl
from jax.experimental.pallas import tpu as pltpu
from jax.sharding import PartitionSpec as P

HEADS = 16
KV_HEADS = 8
HEAD_DIM = 96
GROUP = 384
VMEM = 60 * 1024 * 1024

epsilon = 1e-05
rope_base = 100000.0
bf16 = jnp.bfloat16
f32 = jnp.float32


def frequencies():
    half = HEAD_DIM // 2
    steps = np.arange(half, dtype=np.float32)
    frequency = np.float32(rope_base) ** (np.float32(-2.0) * steps / np.float32(HEAD_DIM))
    row = np.zeros((1, 128), np.float32)
    row[0, :half] = frequency
    row[0, half:HEAD_DIM] = frequency
    return row


def norm_value(values, gain):
    factor = lax.rsqrt(jnp.mean(values * values, axis=-1, keepdims=True) + epsilon)
    return (values * factor * gain).astype(bf16)


def rotate(values, cosine, sine):
    width = values.shape[-1]
    half = HEAD_DIM // 2
    lane = lax.broadcasted_iota(jnp.int32, values.shape, 1)
    first = lax.rem(lane, HEAD_DIM) < half
    swapped = jnp.where(
        first, pltpu.roll(values, width - half, 1), pltpu.roll(values, half, 1)
    )
    return values * cosine + swapped * sine


def place(fresh, cached, new_count, cached_count):
    rows, new = cached.shape[0], fresh.shape[0]
    spot = lax.broadcasted_iota(jnp.int32, (rows, new), 0)
    token = lax.broadcasted_iota(jnp.int32, (rows, new), 1)
    chosen = (spot - cached_count == token) & (token < new_count)
    placed = jnp.dot(jnp.where(chosen, 1.0, 0.0).astype(bf16), fresh, preferred_element_type=f32)
    keep = lax.broadcasted_iota(jnp.int32, cached.shape, 0) < cached_count
    return jnp.where(keep, cached.astype(f32), placed).astype(bf16)


def key_kernel(
    order, news, olds, dev, tokens, gain, freq, weight, cached, context, normed, cosine, sine
):
    reqs, new, width = tokens.shape

    @pl.when(pl.program_id(0) == 0)
    def _():
        lane = lax.broadcasted_iota(jnp.int32, (new, 128), 1)
        row = lax.broadcasted_iota(jnp.int32, (new, 128), 0)
        sign = jnp.where(lane < HEAD_DIM // 2, -1.0, 1.0)
        for r in range(reqs):
            normed[r] = norm_value(tokens[r].astype(f32), gain[0:1, :])
            old = olds[order[dev[0] * reqs + r]]
            angles = (row + old).astype(f32) * freq[...]
            cos_part = jnp.cos(angles)[:, :HEAD_DIM]
            sin_part = (jnp.sin(angles) * sign)[:, :HEAD_DIM]
            cosine[r] = jnp.concatenate([cos_part] * 4, axis=1)
            sine[r] = jnp.concatenate([sin_part] * 4, axis=1)

    rows = normed[...].reshape(reqs * new, width)
    projected = jnp.dot(rows, weight[...], preferred_element_type=f32)
    turned = rotate(
        projected,
        cosine[...].reshape(reqs * new, GROUP),
        sine[...].reshape(reqs * new, GROUP),
    ).astype(bf16)
    parts, _, depth, _ = context.shape
    for r in range(reqs):
        request = order[dev[0] * reqs + r]
        merged = place(turned[r * new : (r + 1) * new], cached[r], news[request], olds[request])
        context[:, r] = merged.reshape(parts, depth, GROUP)


def attention_kernel(
    order, news, olds, dev, normed, cosine, sine, weight, w_value, keys, cached, tokens, gain, w_out,
    values, residual, post, total, attended, out_weight, sems,
):
    step = pl.program_id(0)
    reqs, new, width = normed.shape
    parts, _, depth, _ = keys.shape
    ctx = parts * depth
    flat = reqs * new

    def stream(g):
        source = w_out.at[pl.ds(g * 2 * GROUP, 2 * GROUP)]
        return pltpu.make_async_copy(source, out_weight.at[g], sems.at[g])

    @pl.when(step == 0)
    def _():
        for g in range(out_weight.shape[0]):
            stream(g).start()

    rows = normed[...].reshape(flat, width)
    fresh = jnp.dot(rows, w_value[...], preferred_element_type=f32).astype(bf16)
    projected = jnp.dot(rows, weight[...], preferred_element_type=f32)
    cos_part = cosine[...].reshape(flat, GROUP)
    sin_part = sine[...].reshape(flat, GROUP)
    queries = [
        rotate(projected[:, GROUP * i : GROUP * (i + 1)], cos_part, sin_part).astype(bf16)
        for i in range(2)
    ]
    spot = lax.broadcasted_iota(jnp.int32, (new, ctx), 1)
    token = lax.broadcasted_iota(jnp.int32, (new, ctx), 0)
    scale = HEAD_DIM ** (-0.5) * math.log2(math.e)
    for r in range(reqs):
        request = order[dev[0] * reqs + r]
        old = olds[request]
        key_rows = keys[:, r].reshape(ctx, GROUP)
        value_rows = place(fresh[r * new : (r + 1) * new], cached[r], news[request], old)
        values[:, r] = value_rows.reshape(parts, depth, GROUP)
        mask = jnp.where(spot <= old + token, 0.0, -jnp.inf)
        bias = jnp.concatenate([mask, mask], axis=0)
        pieces = []
        for k in range(4):
            key = key_rows[:, HEAD_DIM * k : HEAD_DIM * (k + 1)]
            value = value_rows[:, HEAD_DIM * k : HEAD_DIM * (k + 1)]
            pair = []
            for h in (2 * k, 2 * k + 1):
                at = HEAD_DIM * (h % 4)
                pair.append(queries[h // 4][r * new : (r + 1) * new, at : at + HEAD_DIM])
            scores = lax.dot_general(
                jnp.concatenate(pair, axis=0), key, (((1,), (1,)), ((), ())),
                preferred_element_type=f32,
            )
            scores = scores * scale + bias
            exponent = jnp.exp2(scores - jnp.max(scores, axis=-1, keepdims=True))
            bottom = jnp.sum(exponent, axis=-1, keepdims=True)
            mixed = jnp.dot(exponent.astype(bf16), value, preferred_element_type=f32) / bottom
            pieces += [mixed[:new], mixed[new:]]
        attended[r * new : (r + 1) * new, :] = jnp.concatenate(pieces, axis=1).astype(bf16)
    stream(step).wait()
    term = jnp.dot(attended[...], out_weight[step], preferred_element_type=f32)

    @pl.when(step == 0)
    def _():
        total[...] = tokens[...].astype(f32).reshape(flat, width) + term

    @pl.when(step > 0)
    def _():
        total[...] += term

    @pl.when(step == pl.num_programs(0) - 1)
    def _():
        rounded = total[...].astype(bf16)
        residual[...] = rounded
        post[...] = norm_value(rounded.astype(f32), gain[1:2, :])


def mlp_kernel(own, other, *refs):
    total = refs[-1]
    inputs = refs[: (len(refs) - 1) // 2]
    outputs = refs[(len(refs) - 1) // 2 : -1]
    step = pl.program_id(0)
    flat = inputs[0].shape[0]
    values = jnp.concatenate([rows[...] for rows in inputs], axis=0)
    term = None
    for weights in (own, other):
        gate = jnp.dot(values, weights[0], preferred_element_type=f32)
        up = jnp.dot(values, weights[1], preferred_element_type=f32)
        hidden = (gate / (1.0 + jnp.exp(-gate)) * up).astype(bf16)
        product = lax.dot_general(
            hidden, weights[2], (((1,), (1,)), ((), ())), preferred_element_type=f32
        )
        term = product if term is None else term + product

    @pl.when(step == 0)
    def _():
        total[...] = term

    @pl.when(step > 0)
    def _():
        total[...] += term

    @pl.when(step == pl.num_programs(0) - 1)
    def _():
        for i, out in enumerate(outputs):
            out[...] = total[i * flat : (i + 1) * flat].astype(bf16)


def run_copies(copies):
    for copy in copies:
        copy.start()
    for copy in copies:
        copy.wait()


def pack_kernel(picked, source, *rest):
    targets, sems = rest[:-1], rest[-1]
    share = targets[0].shape[0]
    run_copies(
        [
            pltpu.make_async_copy(
                source.at[picked[s * share + k]], target.at[k], sems.at[s * share + k]
            )
            for s, target in enumerate(targets)
            for k in range(share)
        ]
    )


def unpack_kernel(columns, count, spots, *refs):
    sources, target, sems = refs[:count], refs[-2], refs[-1]
    share, _, width = sources[0].shape
    run_copies(
        [
            pltpu.make_async_copy(
                source.at[k],
                target.at[spots[s * share + k], :, pl.ds(columns, width)],
                sems.at[s * share + k],
            )
            for s, source in enumerate(sources)
            for k in range(share)
        ]
    )


def call(
    kernel, prefetched, grid, in_specs, out_specs, out_shape, scratch, operands,
    flops=0, moved=6 << 20, aliases={}, after=(),
):
    begin = len(prefetched) + len(operands)

    def ordered(*refs):
        kernel(*refs[:begin], *refs[begin + len(after) :])

    return pl.pallas_call(
        ordered,
        out_shape=out_shape,
        grid_spec=pltpu.PrefetchScalarGridSpec(
            num_scalar_prefetch=len(prefetched),
            grid=grid,
            in_specs=list(in_specs) + [pl.BlockSpec(memory_space=pl.ANY)] * len(after),
            out_specs=out_specs,
            scratch_shapes=scratch,
        ),
        compiler_params=pltpu.CompilerParams(vmem_limit_bytes=VMEM),
        cost_estimate=pl.CostEstimate(flops=flops, bytes_accessed=moved, transcendentals=0),
        input_output_aliases=aliases,
    )(*prefetched, *operands, *after)


def shape(dims, dtype=bf16):
    return jax.ShapeDtypeStruct(dims, dtype)


def whole(dims):
    return pl.BlockSpec(dims, lambda *_: (0,) * len(dims))


def local(
    tokens,
    cached,
    norm_gains,
    w_qkv,
    w_out,
    mlp_weights,
    request_order,
    new_lengths,
    cached_lengths,
    decode_slots,
):
    tensor_size = lax.axis_size("tensor")
    group_total = lax.axis_size("dp")
    reqs, new, width = tokens.shape
    ctx = cached.shape[1]
    depth = ctx // tensor_size
    flat = reqs * new
    group_reqs = reqs * tensor_size
    group_index = lax.axis_index("dp")
    device = group_index * tensor_size + lax.axis_index("tensor")
    dev = device.astype(jnp.int32).reshape(1)
    key_width = KV_HEADS * HEAD_DIM
    groups = key_width // GROUP
    scalars = (request_order, new_lengths, cached_lengths, dev)
    freq = jnp.asarray(frequencies())

    other_weights = lax.ppermute(
        mlp_weights, "tensor", [(t, t ^ 1) for t in range(tensor_size)]
    )

    context_shape = (tensor_size, reqs, depth, key_width)
    context_spec = pl.BlockSpec((tensor_size, reqs, depth, GROUP), lambda g, *_: (0, 0, 0, g))
    table = (reqs, new, GROUP)
    keys, normed, cosine, sine = call(
        key_kernel,
        scalars,
        (groups,),
        [
            whole(tokens.shape),
            whole(norm_gains.shape),
            whole((1, 128)),
            pl.BlockSpec((width, GROUP), lambda g, *_: (0, width // GROUP + g)),
            pl.BlockSpec((reqs, ctx, GROUP), lambda g, *_: (0, 0, g)),
        ],
        [context_spec, whole(tokens.shape), whole(table), whole(table)],
        [shape(context_shape), shape(tokens.shape), shape(table, f32), shape(table, f32)],
        [],
        (tokens, norm_gains, freq, w_qkv, cached),
        2 * flat * width * key_width,
        8 << 20,
    )
    keys_moved = lax.all_to_all(keys, "tensor", split_axis=0, concat_axis=0, tiled=True)
    values, residual, post = call(
        attention_kernel,
        scalars,
        (groups,),
        [
            whole(tokens.shape),
            whole(table),
            whole(table),
            pl.BlockSpec((width, 2 * GROUP), lambda g, *_: (0, g)),
            pl.BlockSpec((width, GROUP), lambda g, *_: (0, (width + key_width) // GROUP + g)),
            context_spec,
            pl.BlockSpec((reqs, ctx, GROUP), lambda g, *_: (0, 0, groups + g)),
            whole(tokens.shape),
            whole(norm_gains.shape),
            pl.BlockSpec(memory_space=pl.ANY),
        ],
        [context_spec, whole((flat, width)), whole((flat, width))],
        [shape(context_shape), shape((flat, width)), shape((flat, width))],
        [
            pltpu.VMEM((flat, width), f32),
            pltpu.VMEM((flat, 2 * GROUP), bf16),
            pltpu.VMEM((groups, 2 * GROUP, width), bf16),
            pltpu.SemaphoreType.DMA((groups,)),
        ],
        (normed, cosine, sine, w_qkv, w_qkv, keys, cached, tokens, norm_gains, w_out),
        12 * flat * width * width,
        16 << 20,
    )
    values_moved = lax.all_to_all(values, "tensor", split_axis=0, concat_axis=0, tiled=True)

    units = mlp_weights.shape[2]
    chunk = 256 if units % 256 == 0 else units

    def mlp(pieces, after):
        count = len(pieces)
        weight_spec = pl.BlockSpec((3, width, chunk), lambda c: (0, 0, c))
        return call(
            mlp_kernel,
            (),
            (units // chunk,),
            [weight_spec] * 2 + [whole((flat, width))] * count,
            [whole((flat, width))] * count,
            [shape((flat, width))] * count,
            [pltpu.VMEM((count * flat, width), f32)],
            (mlp_weights, other_weights, *pieces),
            12 * count * flat * width * units,
            12 * width * units,
            after=after,
        )

    every = request_order.shape[0]
    indices = jnp.arange(every, dtype=jnp.int32)
    slot_of = jnp.sum(
        jnp.where(request_order[:, None] == indices[None, :], decode_slots[None, :], 0), axis=1
    )
    count_of = jnp.sum(
        jnp.where(request_order[:, None] == indices[None, :], new_lengths[None, :], 0), axis=1
    )
    ordinal = jnp.arange(group_reqs, dtype=jnp.int32)

    def inverse(keys_of):
        position = jnp.sum((keys_of[None, :] < keys_of[:, None]).astype(jnp.int32), axis=1)
        return jnp.sum(
            jnp.where(position[None, :] == ordinal[:, None], ordinal[None, :], 0), axis=1
        )

    own_slots = lax.dynamic_slice_in_dim(slot_of, group_index * group_reqs, group_reqs)
    goal = lax.rem(own_slots // group_reqs - group_index + group_total, group_total)
    picked = inverse(goal * group_reqs + lax.rem(own_slots, group_reqs))
    slot_ids = group_index * group_reqs + ordinal
    owners = jnp.sum(
        jnp.where(slot_of[None, :] == slot_ids[:, None], indices[None, :] // group_reqs, 0), axis=1
    )
    origin = lax.rem(group_index - owners + group_total, group_total)
    spots = inverse(origin * group_reqs + ordinal)

    share = group_reqs // group_total
    piece = (share, depth, key_width)
    anywhere = pl.BlockSpec(memory_space=pl.ANY)
    sems = [pltpu.SemaphoreType.DMA((group_reqs,))]
    shifts = [
        [(g, (g + s) % group_total) for g in range(group_total)] for s in range(1, group_total)
    ]

    def pack(moved, after):
        return call(
            pack_kernel, (picked,), (1,), [whole((group_reqs, depth, key_width))],
            [anywhere] * group_total,
            [shape(piece)] * group_total, sems, (moved.reshape(group_reqs, depth, key_width),),
            after=after,
        )

    def across(packed):
        return [packed[0]] + [
            lax.ppermute(rows, "dp", pairs) for rows, pairs in zip(packed[1:], shifts)
        ]

    def unpack(columns, arrived, target, after):
        return call(
            functools.partial(unpack_kernel, columns, group_total), (spots,), (1,),
            [whole(piece)] * group_total + [anywhere] * len(target), anywhere,
            shape((group_reqs, depth, 2 * key_width)), sems, (*arrived, *target),
            aliases={1 + group_total: 0} if target else {}, after=after,
        )

    partners = [
        [(t, t ^ (2 * s)) for t in range(tensor_size)] for s in range(1, tensor_size // 2)
    ]
    gathered = [lax.ppermute(post, "tensor", pairs) for pairs in partners]
    keys_packed = pack(keys_moved, (post,))
    keys_arrived = across(keys_packed)
    partials = list(mlp([post], (keys_packed[0],)))
    values_packed = pack(values_moved, (partials[0],))
    values_arrived = across(values_packed)
    latest = values_packed[0]
    batches = [range(0, 2)] + [range(s, min(s + 2, len(partners))) for s in range(2, len(partners), 2)]
    for batch in batches:
        results = mlp([gathered[s] for s in batch], (latest,))
        latest = results[0]
        partials += [lax.ppermute(rows, "tensor", partners[s]) for s, rows in zip(batch, results)]
    kv_half = unpack(0, keys_arrived, (), (latest,))
    kv_decode = unpack(key_width, values_arrived, (kv_half,), ())

    own_counts = lax.dynamic_slice_in_dim(count_of, device * reqs, reqs)
    live = (jnp.arange(new, dtype=jnp.int32)[None, :] < own_counts[:, None]).reshape(flat, 1)
    total = residual.astype(f32)
    for partial in partials:
        total = total + partial.astype(f32)
    layer_out = jnp.where(live, total, 0.0).astype(bf16).reshape(reqs, new, width)
    return (layer_out, kv_decode)


def solution(mesh):
    in_specs = (
        P(("dp", "tensor"), None, None),
        P(("dp", "tensor"), None, None),
        P(),
        P(),
        P(),
        P(None, None, "tensor"),
        P(),
        P(),
        P(),
        P(),
    )
    out_specs = (P(("dp", "tensor"), None, None), P("dp", "tensor", None))
    return jax.shard_map(local, mesh=mesh, in_specs=in_specs, out_specs=out_specs, check_vma=False)
```

```python
import functools
import math

import jax
import jax.numpy as jnp
import numpy as np
from jax import lax
from jax.experimental import pallas as pl
from jax.experimental.pallas import tpu as pltpu
from jax.sharding import PartitionSpec as P

HEADS = 16
KV_HEADS = 8
HEAD_DIM = 96
GROUP = 384
VMEM = 60 * 1024 * 1024

epsilon = 1e-05
rope_base = 100000.0
bf16 = jnp.bfloat16
f32 = jnp.float32


def frequencies():
    half = HEAD_DIM // 2
    steps = np.arange(half, dtype=np.float32)
    frequency = np.float32(rope_base) ** (np.float32(-2.0) * steps / np.float32(HEAD_DIM))
    row = np.zeros((1, 128), np.float32)
    row[0, :half] = frequency
    row[0, half:HEAD_DIM] = frequency
    return row


def norm_value(values, gain):
    factor = lax.rsqrt(jnp.mean(values * values, axis=-1, keepdims=True) + epsilon)
    return (values * factor * gain).astype(bf16)


def rotate(values, cosine, sine):
    width = values.shape[-1]
    half = HEAD_DIM // 2
    lane = lax.broadcasted_iota(jnp.int32, values.shape, 1)
    first = lax.rem(lane, HEAD_DIM) < half
    swapped = jnp.where(
        first, pltpu.roll(values, width - half, 1), pltpu.roll(values, half, 1)
    )
    return values * cosine + swapped * sine


def place(fresh, cached, new_count, cached_count):
    rows, new = cached.shape[0], fresh.shape[0]
    spot = lax.broadcasted_iota(jnp.int32, (rows, new), 0)
    token = lax.broadcasted_iota(jnp.int32, (rows, new), 1)
    chosen = (spot - cached_count == token) & (token < new_count)
    placed = jnp.dot(jnp.where(chosen, 1.0, 0.0).astype(bf16), fresh, preferred_element_type=f32)
    keep = lax.broadcasted_iota(jnp.int32, cached.shape, 0) < cached_count
    return jnp.where(keep, cached.astype(f32), placed).astype(bf16)


def key_kernel(
    order, news, olds, dev, tokens, gain, freq, weight, cached, context, normed, cosine, sine
):
    reqs, new, width = tokens.shape

    @pl.when(pl.program_id(0) == 0)
    def _():
        lane = lax.broadcasted_iota(jnp.int32, (new, 128), 1)
        row = lax.broadcasted_iota(jnp.int32, (new, 128), 0)
        sign = jnp.where(lane < HEAD_DIM // 2, -1.0, 1.0)
        for r in range(reqs):
            normed[r] = norm_value(tokens[r].astype(f32), gain[0:1, :])
            old = olds[order[dev[0] * reqs + r]]
            angles = (row + old).astype(f32) * freq[...]
            cos_part = jnp.cos(angles)[:, :HEAD_DIM]
            sin_part = (jnp.sin(angles) * sign)[:, :HEAD_DIM]
            cosine[r] = jnp.concatenate([cos_part] * 4, axis=1)
            sine[r] = jnp.concatenate([sin_part] * 4, axis=1)

    rows = normed[...].reshape(reqs * new, width)
    projected = jnp.dot(rows, weight[...], preferred_element_type=f32)
    turned = rotate(
        projected,
        cosine[...].reshape(reqs * new, GROUP),
        sine[...].reshape(reqs * new, GROUP),
    ).astype(bf16)
    parts, _, depth, _ = context.shape
    for r in range(reqs):
        request = order[dev[0] * reqs + r]
        merged = place(turned[r * new : (r + 1) * new], cached[r], news[request], olds[request])
        context[:, r] = merged.reshape(parts, depth, GROUP)


def attention_kernel(
    order, news, olds, dev, normed, cosine, sine, weight, w_value, keys, cached, tokens, gain, w_out,
    values, residual, *rest,
):
    step = pl.program_id(0)
    reqs, new, width = normed.shape
    posts, (total, attended, out_weight, sems) = rest[:reqs], rest[reqs:]
    parts, _, depth, _ = keys.shape
    ctx = parts * depth
    flat = reqs * new

    def stream(g):
        source = w_out.at[pl.ds(g * 2 * GROUP, 2 * GROUP)]
        return pltpu.make_async_copy(source, out_weight.at[g], sems.at[g])

    @pl.when(step == 0)
    def _():
        for g in range(out_weight.shape[0]):
            stream(g).start()

    rows = normed[...].reshape(flat, width)
    fresh = jnp.dot(rows, w_value[...], preferred_element_type=f32).astype(bf16)
    projected = jnp.dot(rows, weight[...], preferred_element_type=f32)
    cos_part = cosine[...].reshape(flat, GROUP)
    sin_part = sine[...].reshape(flat, GROUP)
    queries = [
        rotate(projected[:, GROUP * i : GROUP * (i + 1)], cos_part, sin_part).astype(bf16)
        for i in range(2)
    ]
    spot = lax.broadcasted_iota(jnp.int32, (new, ctx), 1)
    token = lax.broadcasted_iota(jnp.int32, (new, ctx), 0)
    scale = HEAD_DIM ** (-0.5) * math.log2(math.e)
    for r in range(reqs):
        request = order[dev[0] * reqs + r]
        old = olds[request]
        key_rows = keys[:, r].reshape(ctx, GROUP)
        value_rows = place(fresh[r * new : (r + 1) * new], cached[r], news[request], old)
        values[:, r] = value_rows.reshape(parts, depth, GROUP)
        mask = jnp.where(spot <= old + token, 0.0, -jnp.inf)
        bias = jnp.concatenate([mask, mask], axis=0)
        pieces = []
        for k in range(4):
            key = key_rows[:, HEAD_DIM * k : HEAD_DIM * (k + 1)]
            value = value_rows[:, HEAD_DIM * k : HEAD_DIM * (k + 1)]
            pair = []
            for h in (2 * k, 2 * k + 1):
                at = HEAD_DIM * (h % 4)
                pair.append(queries[h // 4][r * new : (r + 1) * new, at : at + HEAD_DIM])
            scores = lax.dot_general(
                jnp.concatenate(pair, axis=0), key, (((1,), (1,)), ((), ())),
                preferred_element_type=f32,
            )
            scores = scores * scale + bias
            exponent = jnp.exp2(scores - jnp.max(scores, axis=-1, keepdims=True))
            bottom = jnp.sum(exponent, axis=-1, keepdims=True)
            mixed = jnp.dot(exponent.astype(bf16), value, preferred_element_type=f32) / bottom
            pieces += [mixed[:new], mixed[new:]]
        attended[r * new : (r + 1) * new, :] = jnp.concatenate(pieces, axis=1).astype(bf16)
    stream(step).wait()
    term = jnp.dot(attended[...], out_weight[step], preferred_element_type=f32)

    @pl.when(step == 0)
    def _():
        total[...] = tokens[...].astype(f32).reshape(flat, width) + term

    @pl.when(step > 0)
    def _():
        total[...] += term

    @pl.when(step == pl.num_programs(0) - 1)
    def _():
        rounded = total[...].astype(bf16)
        residual[...] = rounded
        normal = norm_value(rounded.astype(f32), gain[1:2, :])
        for r in range(reqs):
            posts[r][...] = normal[r * new : (r + 1) * new]


def mlp_kernel(own, other, rows, out, total):
    step = pl.program_id(0)
    values = rows[...]
    term = None
    for weights in (own, other):
        gate = jnp.dot(values, weights[0], preferred_element_type=f32)
        up = jnp.dot(values, weights[1], preferred_element_type=f32)
        hidden = (gate / (1.0 + jnp.exp(-gate)) * up).astype(bf16)
        product = lax.dot_general(
            hidden, weights[2], (((1,), (1,)), ((), ())), preferred_element_type=f32
        )
        term = product if term is None else term + product

    @pl.when(step == 0)
    def _():
        total[...] = term

    @pl.when(step > 0)
    def _():
        total[...] += term

    @pl.when(step == pl.num_programs(0) - 1)
    def _():
        out[...] = total[...].astype(bf16)


def move_rows(pairs, held, arrive, leave):
    inward = [
        pltpu.make_async_copy(source, held.at[i], arrive.at[i])
        for i, (source, _) in enumerate(pairs)
    ]
    outward = [
        pltpu.make_async_copy(held.at[i], target, leave.at[i])
        for i, (_, target) in enumerate(pairs)
    ]
    for copy in inward:
        copy.start()
    for first, second in zip(inward, outward):
        first.wait()
        second.start()
    for copy in outward:
        copy.wait()


def pack_kernel(picked, source, *rest):
    targets, (held, arrive, leave) = rest[:-3], rest[-3:]
    share = targets[0].shape[0]
    move_rows(
        [(source.at[picked[i]], targets[i // share].at[i % share]) for i in range(held.shape[0])],
        held, arrive, leave,
    )


def unpack_kernel(columns, count, spots, *refs):
    sources, (target, held, arrive, leave) = refs[:count], refs[-4:]
    share, _, width = sources[0].shape
    move_rows(
        [
            (
                sources[i // share].at[i % share],
                target.at[spots[i], :, pl.ds(columns, width)],
            )
            for i in range(held.shape[0])
        ],
        held, arrive, leave,
    )


def call(
    kernel, prefetched, grid, in_specs, out_specs, out_shape, scratch, operands,
    flops=0, moved=6 << 20, aliases={}, after=(),
):
    begin = len(prefetched) + len(operands)

    def ordered(*refs):
        kernel(*refs[:begin], *refs[begin + len(after) :])

    return pl.pallas_call(
        ordered,
        out_shape=out_shape,
        grid_spec=pltpu.PrefetchScalarGridSpec(
            num_scalar_prefetch=len(prefetched),
            grid=grid,
            in_specs=list(in_specs) + [pl.BlockSpec(memory_space=pl.ANY)] * len(after),
            out_specs=out_specs,
            scratch_shapes=scratch,
        ),
        compiler_params=pltpu.CompilerParams(vmem_limit_bytes=VMEM),
        cost_estimate=pl.CostEstimate(flops=flops, bytes_accessed=moved, transcendentals=0),
        input_output_aliases=aliases,
    )(*prefetched, *operands, *after)


def shape(dims, dtype=bf16):
    return jax.ShapeDtypeStruct(dims, dtype)


def whole(dims):
    return pl.BlockSpec(dims, lambda *_: (0,) * len(dims))


def local(
    tokens,
    cached,
    norm_gains,
    w_qkv,
    w_out,
    mlp_weights,
    request_order,
    new_lengths,
    cached_lengths,
    decode_slots,
):
    tensor = ("chip", "core")
    chips, cores = lax.axis_size("chip"), lax.axis_size("core")
    tensor_size = chips * cores
    group_total = lax.axis_size("dp")
    reqs, new, width = tokens.shape
    ctx = cached.shape[1]
    depth = ctx // tensor_size
    flat = reqs * new
    group_reqs = reqs * tensor_size
    group_index = lax.axis_index("dp")
    device = group_index * tensor_size + lax.axis_index(tensor)
    dev = device.astype(jnp.int32).reshape(1)
    key_width = KV_HEADS * HEAD_DIM
    groups = key_width // GROUP
    scalars = (request_order, new_lengths, cached_lengths, dev)
    freq = jnp.asarray(frequencies())

    other_weights = lax.ppermute(mlp_weights, "core", [(0, 1), (1, 0)])

    context_shape = (tensor_size, reqs, depth, key_width)
    context_spec = pl.BlockSpec((tensor_size, reqs, depth, GROUP), lambda g, *_: (0, 0, 0, g))
    table = (reqs, new, GROUP)
    keys, normed, cosine, sine = call(
        key_kernel,
        scalars,
        (groups,),
        [
            whole(tokens.shape),
            whole(norm_gains.shape),
            whole((1, 128)),
            pl.BlockSpec((width, GROUP), lambda g, *_: (0, width // GROUP + g)),
            pl.BlockSpec((reqs, ctx, GROUP), lambda g, *_: (0, 0, g)),
        ],
        [context_spec, whole(tokens.shape), whole(table), whole(table)],
        [shape(context_shape), shape(tokens.shape), shape(table, f32), shape(table, f32)],
        [],
        (tokens, norm_gains, freq, w_qkv, cached),
        2 * flat * width * key_width,
        8 << 20,
    )
    keys_moved = lax.all_to_all(keys, tensor, split_axis=0, concat_axis=0, tiled=True)
    values, residual, *posts = call(
        attention_kernel,
        scalars,
        (groups,),
        [
            whole(tokens.shape),
            whole(table),
            whole(table),
            pl.BlockSpec((width, 2 * GROUP), lambda g, *_: (0, g)),
            pl.BlockSpec((width, GROUP), lambda g, *_: (0, (width + key_width) // GROUP + g)),
            context_spec,
            pl.BlockSpec((reqs, ctx, GROUP), lambda g, *_: (0, 0, groups + g)),
            whole(tokens.shape),
            whole(norm_gains.shape),
            pl.BlockSpec(memory_space=pl.ANY),
        ],
        [context_spec, whole((flat, width))] + [whole((new, width))] * reqs,
        [shape(context_shape), shape((flat, width))] + [shape((new, width))] * reqs,
        [
            pltpu.VMEM((flat, width), f32),
            pltpu.VMEM((flat, 2 * GROUP), bf16),
            pltpu.VMEM((groups, 2 * GROUP, width), bf16),
            pltpu.SemaphoreType.DMA((groups,)),
        ],
        (normed, cosine, sine, w_qkv, w_qkv, keys, cached, tokens, norm_gains, w_out),
        12 * flat * width * width,
        16 << 20,
    )
    values_moved = lax.all_to_all(values, tensor, split_axis=0, concat_axis=0, tiled=True)

    units = mlp_weights.shape[2]
    chunk = 256 if units % 256 == 0 else units

    def mlp(rows, after):
        count = rows.shape[0]
        weight_spec = pl.BlockSpec((3, width, chunk), lambda c: (0, 0, c))
        return call(
            mlp_kernel,
            (),
            (units // chunk,),
            [weight_spec] * 2 + [whole((count, width))],
            whole((count, width)),
            shape((count, width)),
            [pltpu.VMEM((count, width), f32)],
            (mlp_weights, other_weights, rows),
            12 * count * width * units,
            12 * width * units,
            after=after,
        )

    every = request_order.shape[0]
    indices = jnp.arange(every, dtype=jnp.int32)
    slot_of = jnp.sum(
        jnp.where(request_order[:, None] == indices[None, :], decode_slots[None, :], 0), axis=1
    )
    count_of = jnp.sum(
        jnp.where(request_order[:, None] == indices[None, :], new_lengths[None, :], 0), axis=1
    )
    ordinal = jnp.arange(group_reqs, dtype=jnp.int32)

    def inverse(keys_of):
        position = jnp.sum((keys_of[None, :] < keys_of[:, None]).astype(jnp.int32), axis=1)
        return jnp.sum(
            jnp.where(position[None, :] == ordinal[:, None], ordinal[None, :], 0), axis=1
        )

    own_slots = lax.dynamic_slice_in_dim(slot_of, group_index * group_reqs, group_reqs)
    goal = lax.rem(own_slots // group_reqs - group_index + group_total, group_total)
    picked = inverse(goal * group_reqs + lax.rem(own_slots, group_reqs))
    slot_ids = group_index * group_reqs + ordinal
    owners = jnp.sum(
        jnp.where(slot_of[None, :] == slot_ids[:, None], indices[None, :] // group_reqs, 0), axis=1
    )
    origin = lax.rem(group_index - owners + group_total, group_total)
    spots = inverse(origin * group_reqs + ordinal)

    share = group_reqs // group_total
    piece = (share, depth, key_width)
    anywhere = pl.BlockSpec(memory_space=pl.ANY)
    sems = [pltpu.VMEM((group_reqs, depth, key_width), bf16)] + [
        pltpu.SemaphoreType.DMA((group_reqs,))
    ] * 2
    shifts = [
        [(g, (g + s) % group_total) for g in range(group_total)] for s in range(1, group_total)
    ]

    def pack(moved, after):
        return call(
            pack_kernel, (picked,), (1,), [anywhere], [anywhere] * group_total,
            [shape(piece)] * group_total, sems, (moved.reshape(group_reqs, depth, key_width),),
            after=after,
        )

    def across(packed):
        return [packed[0]] + [
            lax.ppermute(rows, "dp", pairs) for rows, pairs in zip(packed[1:], shifts)
        ]

    def unpack(columns, arrived, target, after):
        return call(
            functools.partial(unpack_kernel, columns, group_total), (spots,), (1,),
            [anywhere] * (group_total + len(target)), anywhere,
            shape((group_reqs, depth, 2 * key_width)), sems, (*arrived, *target),
            aliases={1 + group_total: 0} if target else {}, after=after,
        )

    gathered = [lax.all_gather(rows, "chip", axis=0, tiled=True) for rows in posts]
    keys_packed = pack(keys_moved, (residual,))
    keys_arrived = across(keys_packed)
    latest = keys_packed[0]
    sums = []
    values_arrived = None
    for rows in gathered:
        partial = mlp(rows, (latest,))
        sums.append(lax.psum_scatter(partial, "chip", scatter_dimension=0, tiled=True))
        latest = partial
        if values_arrived is None:
            values_packed = pack(values_moved, (latest,))
            values_arrived = across(values_packed)
            latest = values_packed[0]
    kv_half = unpack(0, keys_arrived, (), (latest,))
    kv_decode = unpack(key_width, values_arrived, (kv_half,), ())

    own_counts = lax.dynamic_slice_in_dim(count_of, device * reqs, reqs)
    live = jnp.arange(new, dtype=jnp.int32)[None, :, None] < own_counts[:, None, None]
    total = residual.reshape(reqs, new, width).astype(f32) + jnp.stack(sums).astype(f32)
    layer_out = jnp.where(live, total, 0.0).astype(bf16)
    return (layer_out, kv_decode)


def solution(mesh):
    in_specs = (
        P(("dp", "chip", "core"), None, None),
        P(("dp", "chip", "core"), None, None),
        P(),
        P(),
        P(),
        P(None, None, ("chip", "core")),
        P(),
        P(),
        P(),
        P(),
    )
    out_specs = (P(("dp", "chip", "core"), None, None), P("dp", ("chip", "core"), None))
    devices = mesh.devices.reshape(mesh.devices.shape[0], -1, 2)
    mesh = jax.sharding.Mesh(devices, ("dp", "chip", "core"))
    return jax.shard_map(local, mesh=mesh, in_specs=in_specs, out_specs=out_specs, check_vma=False)
```

```python
import functools
import math

import jax
import jax.numpy as jnp
import numpy as np
from jax import lax
from jax.experimental import pallas as pl
from jax.experimental.pallas import tpu as pltpu
from jax.sharding import PartitionSpec as P

HEADS = 16
KV_HEADS = 8
HEAD_DIM = 96
GROUP = 384
VMEM = 60 * 1024 * 1024

epsilon = 1e-05
rope_base = 100000.0
bf16 = jnp.bfloat16
f32 = jnp.float32


def frequencies():
    half = HEAD_DIM // 2
    steps = np.arange(half, dtype=np.float32)
    frequency = np.float32(rope_base) ** (np.float32(-2.0) * steps / np.float32(HEAD_DIM))
    row = np.zeros((1, 128), np.float32)
    row[0, :half] = frequency
    row[0, half:HEAD_DIM] = frequency
    return row


def norm_value(values, gain):
    factor = lax.rsqrt(jnp.mean(values * values, axis=-1, keepdims=True) + epsilon)
    return (values * factor * gain).astype(bf16)


def rotate(values, cosine, sine):
    width = values.shape[-1]
    half = HEAD_DIM // 2
    lane = lax.broadcasted_iota(jnp.int32, values.shape, 1)
    first = lax.rem(lane, HEAD_DIM) < half
    swapped = jnp.where(
        first, pltpu.roll(values, width - half, 1), pltpu.roll(values, half, 1)
    )
    return values * cosine + swapped * sine


def place(fresh, cached, new_count, cached_count):
    rows, new = cached.shape[0], fresh.shape[0]
    spot = lax.broadcasted_iota(jnp.int32, (rows, new), 0)
    token = lax.broadcasted_iota(jnp.int32, (rows, new), 1)
    chosen = (spot - cached_count == token) & (token < new_count)
    placed = jnp.dot(jnp.where(chosen, 1.0, 0.0).astype(bf16), fresh, preferred_element_type=f32)
    keep = lax.broadcasted_iota(jnp.int32, cached.shape, 0) < cached_count
    return jnp.where(keep, cached.astype(f32), placed).astype(bf16)


def key_kernel(
    order, news, olds, dev, tokens, gain, freq, weight, cached, context, normed, cosine, sine
):
    reqs, new, width = tokens.shape

    @pl.when(pl.program_id(0) == 0)
    def _():
        lane = lax.broadcasted_iota(jnp.int32, (new, 128), 1)
        row = lax.broadcasted_iota(jnp.int32, (new, 128), 0)
        sign = jnp.where(lane < HEAD_DIM // 2, -1.0, 1.0)
        for r in range(reqs):
            normed[r] = norm_value(tokens[r].astype(f32), gain[0:1, :])
            old = olds[order[dev[0] * reqs + r]]
            angles = (row + old).astype(f32) * freq[...]
            cos_part = jnp.cos(angles)[:, :HEAD_DIM]
            sin_part = (jnp.sin(angles) * sign)[:, :HEAD_DIM]
            cosine[r] = jnp.concatenate([cos_part] * 4, axis=1)
            sine[r] = jnp.concatenate([sin_part] * 4, axis=1)

    rows = normed[...].reshape(reqs * new, width)
    projected = jnp.dot(rows, weight[...], preferred_element_type=f32)
    turned = rotate(
        projected,
        cosine[...].reshape(reqs * new, GROUP),
        sine[...].reshape(reqs * new, GROUP),
    ).astype(bf16)
    parts, _, depth, _ = context.shape
    for r in range(reqs):
        request = order[dev[0] * reqs + r]
        merged = place(turned[r * new : (r + 1) * new], cached[r], news[request], olds[request])
        context[:, r] = merged.reshape(parts, depth, GROUP)


def attention_kernel(
    order, news, olds, dev, normed, cosine, sine, weight, w_value, keys, cached, tokens, gain, w_out,
    values, residual, post, total, attended, out_weight, sems,
):
    step = pl.program_id(0)
    reqs, new, width = normed.shape
    parts, _, depth, _ = keys.shape
    ctx = parts * depth
    flat = reqs * new

    def stream(g):
        source = w_out.at[pl.ds(g * 2 * GROUP, 2 * GROUP)]
        return pltpu.make_async_copy(source, out_weight.at[g], sems.at[g])

    @pl.when(step == 0)
    def _():
        for g in range(out_weight.shape[0]):
            stream(g).start()

    rows = normed[...].reshape(flat, width)
    fresh = jnp.dot(rows, w_value[...], preferred_element_type=f32).astype(bf16)
    projected = jnp.dot(rows, weight[...], preferred_element_type=f32)
    cos_part = cosine[...].reshape(flat, GROUP)
    sin_part = sine[...].reshape(flat, GROUP)
    queries = [
        rotate(projected[:, GROUP * i : GROUP * (i + 1)], cos_part, sin_part).astype(bf16)
        for i in range(2)
    ]
    spot = lax.broadcasted_iota(jnp.int32, (new, ctx), 1)
    token = lax.broadcasted_iota(jnp.int32, (new, ctx), 0)
    scale = HEAD_DIM ** (-0.5) * math.log2(math.e)
    for r in range(reqs):
        request = order[dev[0] * reqs + r]
        old = olds[request]
        key_rows = keys[:, r].reshape(ctx, GROUP)
        value_rows = place(fresh[r * new : (r + 1) * new], cached[r], news[request], old)
        values[:, r] = value_rows.reshape(parts, depth, GROUP)
        mask = jnp.where(spot <= old + token, 0.0, -jnp.inf)
        bias = jnp.concatenate([mask, mask], axis=0)
        pieces = []
        for k in range(4):
            key = key_rows[:, HEAD_DIM * k : HEAD_DIM * (k + 1)]
            value = value_rows[:, HEAD_DIM * k : HEAD_DIM * (k + 1)]
            pair = []
            for h in (2 * k, 2 * k + 1):
                at = HEAD_DIM * (h % 4)
                pair.append(queries[h // 4][r * new : (r + 1) * new, at : at + HEAD_DIM])
            scores = lax.dot_general(
                jnp.concatenate(pair, axis=0), key, (((1,), (1,)), ((), ())),
                preferred_element_type=f32,
            )
            scores = scores * scale + bias
            exponent = jnp.exp2(scores - jnp.max(scores, axis=-1, keepdims=True))
            bottom = jnp.sum(exponent, axis=-1, keepdims=True)
            mixed = jnp.dot(exponent.astype(bf16), value, preferred_element_type=f32) / bottom
            pieces += [mixed[:new], mixed[new:]]
        attended[r * new : (r + 1) * new, :] = jnp.concatenate(pieces, axis=1).astype(bf16)
    stream(step).wait()
    term = jnp.dot(attended[...], out_weight[step], preferred_element_type=f32)

    @pl.when(step == 0)
    def _():
        total[...] = tokens[...].astype(f32).reshape(flat, width) + term

    @pl.when(step > 0)
    def _():
        total[...] += term

    @pl.when(step == pl.num_programs(0) - 1)
    def _():
        rounded = total[...].astype(bf16)
        residual[...] = rounded
        post[...] = norm_value(rounded.astype(f32), gain[1:2, :])


def mlp_kernel(count, own, other, *refs):
    inputs, outputs, total = refs[:count], refs[count:-1], refs[-1]
    step = pl.program_id(0)
    values = jnp.concatenate([rows[...] for rows in inputs], axis=0)
    term = None
    for weights in (own, other):
        gate = jnp.dot(values, weights[0], preferred_element_type=f32)
        up = jnp.dot(values, weights[1], preferred_element_type=f32)
        hidden = (gate / (1.0 + jnp.exp(-gate)) * up).astype(bf16)
        product = lax.dot_general(
            hidden, weights[2], (((1,), (1,)), ((), ())), preferred_element_type=f32
        )
        term = product if term is None else term + product

    @pl.when(step == 0)
    def _():
        total[...] = term

    @pl.when(step > 0)
    def _():
        total[...] += term

    @pl.when(step == pl.num_programs(0) - 1)
    def _():
        flat = outputs[0].shape[0]
        for i, out in enumerate(outputs):
            out[...] = total[i * flat : (i + 1) * flat].astype(bf16)


def move_rows(pairs, held, arrive, leave):
    inward = [
        pltpu.make_async_copy(source, held.at[i], arrive.at[i])
        for i, (source, _) in enumerate(pairs)
    ]
    outward = [
        pltpu.make_async_copy(held.at[i], target, leave.at[i])
        for i, (_, target) in enumerate(pairs)
    ]
    for copy in inward:
        copy.start()
    for first, second in zip(inward, outward):
        first.wait()
        second.start()
    for copy in outward:
        copy.wait()


def pack_kernel(groups, share, count, passed, picked, group, source, *rest):
    held, arrive, leave = rest[-3:]
    targets = rest[passed : passed + count]
    pairs = []
    for i in range(groups * share):
        if count > 1:
            target = targets[i // share].at[i % share]
        else:
            goal = lax.rem(group[0] + i // share, groups)
            target = targets[0].at[goal * share + i % share]
        pairs.append((source.at[picked[i]], target))
    move_rows(pairs, held, arrive, leave)


def unpack_kernel(columns, groups, share, count, spots, group, *refs):
    sources, (target, held, arrive, leave) = refs[:count], refs[-4:]
    width = sources[0].shape[-1]
    pairs = []
    for i in range(groups * share):
        if count > 1:
            source = sources[i // share].at[i % share]
        else:
            origin = lax.rem(group[0] + groups - i // share, groups)
            source = sources[0].at[origin * share + i % share]
        pairs.append((source, target.at[spots[i], :, pl.ds(columns, width)]))
    move_rows(pairs, held, arrive, leave)


def cut_kernel(first, second, *halves):
    middle = first.shape[0] // 2
    halves[0][...] = second[:middle]
    halves[1][...] = first[middle:]


def call(
    kernel, prefetched, grid, in_specs, out_specs, out_shape, scratch, operands,
    flops=0, moved=6 << 20, aliases={}, after=(),
):
    begin = len(prefetched) + len(operands)

    def ordered(*refs):
        kernel(*refs[:begin], *refs[begin + len(after) :])

    return pl.pallas_call(
        ordered,
        out_shape=out_shape,
        grid_spec=pltpu.PrefetchScalarGridSpec(
            num_scalar_prefetch=len(prefetched),
            grid=grid,
            in_specs=list(in_specs) + [pl.BlockSpec(memory_space=pl.ANY)] * len(after),
            out_specs=out_specs,
            scratch_shapes=scratch,
        ),
        compiler_params=pltpu.CompilerParams(vmem_limit_bytes=VMEM),
        cost_estimate=pl.CostEstimate(flops=flops, bytes_accessed=moved, transcendentals=0),
        input_output_aliases=aliases,
    )(*prefetched, *operands, *after)


def shape(dims, dtype=bf16):
    return jax.ShapeDtypeStruct(dims, dtype)


def whole(dims):
    return pl.BlockSpec(dims, lambda *_: (0,) * len(dims))


def local(
    tokens,
    cached,
    norm_gains,
    w_qkv,
    w_out,
    mlp_weights,
    request_order,
    new_lengths,
    cached_lengths,
    decode_slots,
):
    tensor = ("chip", "core")
    chips, cores = lax.axis_size("chip"), lax.axis_size("core")
    tensor_size = chips * cores
    group_total = lax.axis_size("dp")
    reqs, new, width = tokens.shape
    ctx = cached.shape[1]
    depth = ctx // tensor_size
    flat = reqs * new
    group_reqs = reqs * tensor_size
    group_index = lax.axis_index("dp")
    device = group_index * tensor_size + lax.axis_index(tensor)
    dev = device.astype(jnp.int32).reshape(1)
    key_width = KV_HEADS * HEAD_DIM
    groups = key_width // GROUP
    scalars = (request_order, new_lengths, cached_lengths, dev)
    freq = jnp.asarray(frequencies())

    other_weights = lax.ppermute(mlp_weights, "core", [(0, 1), (1, 0)])

    context_shape = (tensor_size, reqs, depth, key_width)
    context_spec = pl.BlockSpec((tensor_size, reqs, depth, GROUP), lambda g, *_: (0, 0, 0, g))
    table = (reqs, new, GROUP)
    keys, normed, cosine, sine = call(
        key_kernel,
        scalars,
        (groups,),
        [
            whole(tokens.shape),
            whole(norm_gains.shape),
            whole((1, 128)),
            pl.BlockSpec((width, GROUP), lambda g, *_: (0, width // GROUP + g)),
            pl.BlockSpec((reqs, ctx, GROUP), lambda g, *_: (0, 0, g)),
        ],
        [context_spec, whole(tokens.shape), whole(table), whole(table)],
        [shape(context_shape), shape(tokens.shape), shape(table, f32), shape(table, f32)],
        [],
        (tokens, norm_gains, freq, w_qkv, cached),
        2 * flat * width * key_width,
        8 << 20,
    )
    keys_moved = lax.all_to_all(keys, tensor, split_axis=0, concat_axis=0, tiled=True)
    values, residual, post = call(
        attention_kernel,
        scalars,
        (groups,),
        [
            whole(tokens.shape),
            whole(table),
            whole(table),
            pl.BlockSpec((width, 2 * GROUP), lambda g, *_: (0, g)),
            pl.BlockSpec((width, GROUP), lambda g, *_: (0, (width + key_width) // GROUP + g)),
            context_spec,
            pl.BlockSpec((reqs, ctx, GROUP), lambda g, *_: (0, 0, groups + g)),
            whole(tokens.shape),
            whole(norm_gains.shape),
            pl.BlockSpec(memory_space=pl.ANY),
        ],
        [context_spec, whole((flat, width)), whole((flat, width))],
        [shape(context_shape), shape((flat, width)), shape((flat, width))],
        [
            pltpu.VMEM((flat, width), f32),
            pltpu.VMEM((flat, 2 * GROUP), bf16),
            pltpu.VMEM((groups, 2 * GROUP, width), bf16),
            pltpu.SemaphoreType.DMA((groups,)),
        ],
        (normed, cosine, sine, w_qkv, w_qkv, keys, cached, tokens, norm_gains, w_out),
        12 * flat * width * width,
        16 << 20,
    )
    units = mlp_weights.shape[2]
    chunk = 256 if units % 256 == 0 else units

    def mlp(pieces, after):
        total_rows = sum(rows.shape[0] for rows in pieces)
        weight_spec = pl.BlockSpec((3, width, chunk), lambda c: (0, 0, c))
        return call(
            functools.partial(mlp_kernel, len(pieces)),
            (),
            (units // chunk,),
            [weight_spec] * 2 + [whole(rows.shape) for rows in pieces],
            [whole((flat, width))] * (total_rows // flat),
            [shape((flat, width))] * (total_rows // flat),
            [pltpu.VMEM((total_rows, width), f32)],
            (mlp_weights, other_weights, *pieces),
            12 * total_rows * width * units,
            12 * width * units,
            after=after,
        )

    every = request_order.shape[0]
    indices = jnp.arange(every, dtype=jnp.int32)
    slot_of = jnp.sum(
        jnp.where(request_order[:, None] == indices[None, :], decode_slots[None, :], 0), axis=1
    )
    count_of = jnp.sum(
        jnp.where(request_order[:, None] == indices[None, :], new_lengths[None, :], 0), axis=1
    )
    ordinal = jnp.arange(group_reqs, dtype=jnp.int32)

    def inverse(keys_of):
        position = jnp.sum((keys_of[None, :] < keys_of[:, None]).astype(jnp.int32), axis=1)
        return jnp.sum(
            jnp.where(position[None, :] == ordinal[:, None], ordinal[None, :], 0), axis=1
        )

    own_slots = lax.dynamic_slice_in_dim(slot_of, group_index * group_reqs, group_reqs)
    goal = lax.rem(own_slots // group_reqs - group_index + group_total, group_total)
    picked = inverse(goal * group_reqs + lax.rem(own_slots, group_reqs))
    slot_ids = group_index * group_reqs + ordinal
    owners = jnp.sum(
        jnp.where(slot_of[None, :] == slot_ids[:, None], indices[None, :] // group_reqs, 0), axis=1
    )
    origin = lax.rem(group_index - owners + group_total, group_total)
    spots = inverse(origin * group_reqs + ordinal)

    share = group_reqs // group_total
    piece = (share, depth, key_width)
    anywhere = pl.BlockSpec(memory_space=pl.ANY)
    sems = [pltpu.VMEM((group_reqs, depth, key_width), bf16)] + [
        pltpu.SemaphoreType.DMA((group_reqs,))
    ] * 2
    shifts = [
        [(g, (g + s) % group_total) for g in range(group_total)] for s in range(1, group_total)
    ]

    group = group_index.astype(jnp.int32).reshape(1)

    def pack(moved, targets, passed, after):
        return call(
            functools.partial(pack_kernel, group_total, share, len(targets), len(passed)),
            (picked, group), (1,),
            [anywhere] * (1 + len(passed)), [anywhere] * (len(targets) + len(passed)),
            [shape(dims) for dims in targets] + [shape(rows.shape) for rows in passed], sems,
            (moved.reshape(group_reqs, depth, key_width), *passed),
            aliases={3 + i: len(targets) + i for i in range(len(passed))}, after=after,
        )

    def unpack(columns, arrived, target, after):
        return call(
            functools.partial(unpack_kernel, columns, group_total, share, len(arrived)),
            (spots, group), (1,), [anywhere] * (len(arrived) + len(target)), anywhere,
            shape((group_reqs, depth, 2 * key_width)), sems, (*arrived, *target),
            aliases={2 + len(arrived): 0} if target else {}, after=after,
        )

    def swap(rows, mask):
        return lax.ppermute(rows, "chip", [(c, c ^ mask) for c in range(chips)])

    masks = [1, 2] if chips == 4 else range(1, chips)
    gathered = [swap(post, mask) for mask in masks]
    *keys_packed, values = pack(
        keys_moved, [piece] * group_total, (values,), (post, other_weights)
    )
    values_moved = lax.all_to_all(values, tensor, split_axis=0, concat_axis=0, tiled=True)
    keys_arrived = [keys_packed[0]] + [
        lax.ppermute(rows, "dp", pairs) for rows, pairs in zip(keys_packed[1:], shifts)
    ]
    partials = list(mlp([post], (keys_packed[0],)))
    latest = partials[0]
    if chips == 4:
        half = (flat // 2, width)
        halves = call(
            cut_kernel, (), (1,), [whole((flat, width))] * 2, [whole(half)] * 2, [shape(half)] * 2,
            [], tuple(gathered), after=(latest,),
        )
        latest = halves[0]
        batches = [([1, 2], gathered), ([3], [swap(halves[0], 1), swap(halves[1], 2)])]
    else:
        batches = [([mask], [rows]) for mask, rows in zip(masks, gathered)]
    values_packed = None
    for batch_masks, pieces in batches:
        results = mlp(pieces, (latest,))
        latest = results[0]
        partials += [swap(rows, mask) for mask, rows in zip(batch_masks, results)]
        if values_packed is None:
            values_packed = pack(
                values_moved, [(group_reqs, depth, key_width)], (), (latest,)
            )[0]
            values_arrived = lax.all_to_all(
                values_packed, "dp", split_axis=0, concat_axis=0, tiled=True
            )
            kv_half = unpack(0, keys_arrived, (), (values_packed,))
            latest = kv_half
    kv_decode = unpack(key_width, [values_arrived], (kv_half,), ())

    own_counts = lax.dynamic_slice_in_dim(count_of, device * reqs, reqs)
    live = (jnp.arange(new, dtype=jnp.int32)[None, :] < own_counts[:, None]).reshape(flat, 1)
    total = residual.astype(f32)
    for partial in partials:
        total = total + partial.astype(f32)
    layer_out = jnp.where(live, total, 0.0).astype(bf16).reshape(reqs, new, width)
    return (layer_out, kv_decode)


def solution(mesh):
    in_specs = (
        P(("dp", "chip", "core"), None, None),
        P(("dp", "chip", "core"), None, None),
        P(),
        P(),
        P(),
        P(None, None, ("chip", "core")),
        P(),
        P(),
        P(),
        P(),
    )
    out_specs = (P(("dp", "chip", "core"), None, None), P("dp", ("chip", "core"), None))
    devices = mesh.devices.reshape(mesh.devices.shape[0], -1, 2)
    mesh = jax.sharding.Mesh(devices, ("dp", "chip", "core"))
    return jax.shard_map(local, mesh=mesh, in_specs=in_specs, out_specs=out_specs, check_vma=False)
```

```python
import functools
import math

import jax
import jax.numpy as jnp
import numpy as np
from jax import lax
from jax.experimental import pallas as pl
from jax.experimental.pallas import tpu as pltpu
from jax.sharding import PartitionSpec as P

HEADS = 16
KV_HEADS = 8
HEAD_DIM = 96
GROUP = 384
VMEM = 60 * 1024 * 1024

epsilon = 1e-05
rope_base = 100000.0
bf16 = jnp.bfloat16
f32 = jnp.float32


def frequencies():
    half = HEAD_DIM // 2
    steps = np.arange(half, dtype=np.float32)
    frequency = np.float32(rope_base) ** (np.float32(-2.0) * steps / np.float32(HEAD_DIM))
    row = np.zeros((1, 128), np.float32)
    row[0, :half] = frequency
    row[0, half:HEAD_DIM] = frequency
    return row


def norm_value(values, gain):
    factor = lax.rsqrt(jnp.mean(values * values, axis=-1, keepdims=True) + epsilon)
    return (values * factor * gain).astype(bf16)


def rotate(values, cosine, sine):
    width = values.shape[-1]
    half = HEAD_DIM // 2
    lane = lax.broadcasted_iota(jnp.int32, values.shape, 1)
    first = lax.rem(lane, HEAD_DIM) < half
    swapped = jnp.where(
        first, pltpu.roll(values, width - half, 1), pltpu.roll(values, half, 1)
    )
    return values * cosine + swapped * sine


def place(fresh, cached, new_count, cached_count):
    rows, new = cached.shape[0], fresh.shape[0]
    spot = lax.broadcasted_iota(jnp.int32, (rows, new), 0)
    token = lax.broadcasted_iota(jnp.int32, (rows, new), 1)
    chosen = (spot - cached_count == token) & (token < new_count)
    placed = jnp.dot(jnp.where(chosen, 1.0, 0.0).astype(bf16), fresh, preferred_element_type=f32)
    keep = lax.broadcasted_iota(jnp.int32, cached.shape, 0) < cached_count
    return jnp.where(keep, cached.astype(f32), placed).astype(bf16)


def key_kernel(
    order, news, olds, dev, tokens, gain, freq, weight, cached, context, normed, cosine, sine
):
    reqs, new, width = tokens.shape

    @pl.when(pl.program_id(0) == 0)
    def _():
        lane = lax.broadcasted_iota(jnp.int32, (new, 128), 1)
        row = lax.broadcasted_iota(jnp.int32, (new, 128), 0)
        sign = jnp.where(lane < HEAD_DIM // 2, -1.0, 1.0)
        for r in range(reqs):
            normed[r] = norm_value(tokens[r].astype(f32), gain[0:1, :])
            old = olds[order[dev[0] * reqs + r]]
            angles = (row + old).astype(f32) * freq[...]
            cos_part = jnp.cos(angles)[:, :HEAD_DIM]
            sin_part = (jnp.sin(angles) * sign)[:, :HEAD_DIM]
            cosine[r] = jnp.concatenate([cos_part] * 4, axis=1)
            sine[r] = jnp.concatenate([sin_part] * 4, axis=1)

    rows = normed[...].reshape(reqs * new, width)
    projected = jnp.dot(rows, weight[...], preferred_element_type=f32)
    turned = rotate(
        projected,
        cosine[...].reshape(reqs * new, GROUP),
        sine[...].reshape(reqs * new, GROUP),
    ).astype(bf16)
    parts, _, depth, _ = context.shape
    for r in range(reqs):
        request = order[dev[0] * reqs + r]
        merged = place(turned[r * new : (r + 1) * new], cached[r], news[request], olds[request])
        context[:, r] = merged.reshape(parts, depth, GROUP)


def attention_kernel(
    order, news, olds, dev, normed, cosine, sine, weight, w_value, keys, cached, tokens, gain, w_out,
    values, residual, post, total, attended, out_weight, sems,
):
    step = pl.program_id(0)
    reqs, new, width = normed.shape
    parts, _, depth, _ = keys.shape
    ctx = parts * depth
    flat = reqs * new

    def stream(g):
        source = w_out.at[pl.ds(g * 2 * GROUP, 2 * GROUP)]
        return pltpu.make_async_copy(source, out_weight.at[g], sems.at[g])

    @pl.when(step == 0)
    def _():
        for g in range(out_weight.shape[0]):
            stream(g).start()

    rows = normed[...].reshape(flat, width)
    fresh = jnp.dot(rows, w_value[...], preferred_element_type=f32).astype(bf16)
    projected = jnp.dot(rows, weight[...], preferred_element_type=f32)
    cos_part = cosine[...].reshape(flat, GROUP)
    sin_part = sine[...].reshape(flat, GROUP)
    queries = [
        rotate(projected[:, GROUP * i : GROUP * (i + 1)], cos_part, sin_part).astype(bf16)
        for i in range(2)
    ]
    spot = lax.broadcasted_iota(jnp.int32, (new, ctx), 1)
    token = lax.broadcasted_iota(jnp.int32, (new, ctx), 0)
    scale = HEAD_DIM ** (-0.5) * math.log2(math.e)
    for r in range(reqs):
        request = order[dev[0] * reqs + r]
        old = olds[request]
        key_rows = keys[:, r].reshape(ctx, GROUP)
        value_rows = place(fresh[r * new : (r + 1) * new], cached[r], news[request], old)
        values[:, r] = value_rows.reshape(parts, depth, GROUP)
        mask = jnp.where(spot <= old + token, 0.0, -jnp.inf)
        bias = jnp.concatenate([mask, mask], axis=0)
        pieces = []
        for k in range(4):
            key = key_rows[:, HEAD_DIM * k : HEAD_DIM * (k + 1)]
            value = value_rows[:, HEAD_DIM * k : HEAD_DIM * (k + 1)]
            pair = []
            for h in (2 * k, 2 * k + 1):
                at = HEAD_DIM * (h % 4)
                pair.append(queries[h // 4][r * new : (r + 1) * new, at : at + HEAD_DIM])
            scores = lax.dot_general(
                jnp.concatenate(pair, axis=0), key, (((1,), (1,)), ((), ())),
                preferred_element_type=f32,
            )
            scores = scores * scale + bias
            exponent = jnp.exp2(scores - jnp.max(scores, axis=-1, keepdims=True))
            bottom = jnp.sum(exponent, axis=-1, keepdims=True)
            mixed = jnp.dot(exponent.astype(bf16), value, preferred_element_type=f32) / bottom
            pieces += [mixed[:new], mixed[new:]]
        attended[r * new : (r + 1) * new, :] = jnp.concatenate(pieces, axis=1).astype(bf16)
    stream(step).wait()
    term = jnp.dot(attended[...], out_weight[step], preferred_element_type=f32)

    @pl.when(step == 0)
    def _():
        total[...] = tokens[...].astype(f32).reshape(flat, width) + term

    @pl.when(step > 0)
    def _():
        total[...] += term

    @pl.when(step == pl.num_programs(0) - 1)
    def _():
        rounded = total[...].astype(bf16)
        residual[...] = rounded
        post[...] = norm_value(rounded.astype(f32), gain[1:2, :])


def mlp_kernel(count, own, other, *refs):
    inputs, outputs, total = refs[:count], refs[count:-1], refs[-1]
    step = pl.program_id(0)
    values = jnp.concatenate([rows[...] for rows in inputs], axis=0)
    term = None
    for weights in (own, other):
        gate = jnp.dot(values, weights[0], preferred_element_type=f32)
        up = jnp.dot(values, weights[1], preferred_element_type=f32)
        hidden = (gate / (1.0 + jnp.exp(-gate)) * up).astype(bf16)
        product = lax.dot_general(
            hidden, weights[2], (((1,), (1,)), ((), ())), preferred_element_type=f32
        )
        term = product if term is None else term + product

    @pl.when(step == 0)
    def _():
        total[...] = term

    @pl.when(step > 0)
    def _():
        total[...] += term

    @pl.when(step == pl.num_programs(0) - 1)
    def _():
        flat = outputs[0].shape[0]
        for i, out in enumerate(outputs):
            out[...] = total[i * flat : (i + 1) * flat].astype(bf16)


def move_rows(pairs, held, arrive, leave):
    inward = [
        pltpu.make_async_copy(source, held.at[i], arrive.at[i])
        for i, (source, _) in enumerate(pairs)
    ]
    outward = [
        pltpu.make_async_copy(held.at[i], target, leave.at[i])
        for i, (_, target) in enumerate(pairs)
    ]
    for copy in inward:
        copy.start()
    for first, second in zip(inward, outward):
        first.wait()
        second.start()
    for copy in outward:
        copy.wait()


def pack_kernel(groups, share, count, passed, picked, group, source, *rest):
    held, arrive, leave = rest[-3:]
    targets = rest[passed : passed + count]
    pairs = []
    for i in range(groups * share):
        if count > 1:
            target = targets[i // share].at[i % share]
        else:
            goal = lax.rem(group[0] + i // share, groups)
            target = targets[0].at[goal * share + i % share]
        pairs.append((source.at[picked[i]], target))
    move_rows(pairs, held, arrive, leave)


def unpack_kernel(columns, groups, share, count, spots, group, *refs):
    sources, (target, held, arrive, leave) = refs[:count], refs[-4:]
    width = sources[0].shape[-1]
    pairs = []
    for i in range(groups * share):
        if count > 1:
            source = sources[i // share].at[i % share]
        else:
            origin = lax.rem(group[0] + groups - i // share, groups)
            source = sources[0].at[origin * share + i % share]
        pairs.append((source, target.at[spots[i], :, pl.ds(columns, width)]))
    move_rows(pairs, held, arrive, leave)


def cut_kernel(first, second, *halves):
    middle = first.shape[0] // 2
    halves[0][...] = second[:middle]
    halves[1][...] = first[middle:]


def call(
    kernel, prefetched, grid, in_specs, out_specs, out_shape, scratch, operands,
    flops=0, moved=6 << 20, aliases={}, after=(),
):
    begin = len(prefetched) + len(operands)

    def ordered(*refs):
        kernel(*refs[:begin], *refs[begin + len(after) :])

    return pl.pallas_call(
        ordered,
        out_shape=out_shape,
        grid_spec=pltpu.PrefetchScalarGridSpec(
            num_scalar_prefetch=len(prefetched),
            grid=grid,
            in_specs=list(in_specs) + [pl.BlockSpec(memory_space=pl.ANY)] * len(after),
            out_specs=out_specs,
            scratch_shapes=scratch,
        ),
        compiler_params=pltpu.CompilerParams(vmem_limit_bytes=VMEM),
        cost_estimate=pl.CostEstimate(flops=flops, bytes_accessed=moved, transcendentals=0),
        input_output_aliases=aliases,
    )(*prefetched, *operands, *after)


def shape(dims, dtype=bf16):
    return jax.ShapeDtypeStruct(dims, dtype)


def whole(dims):
    return pl.BlockSpec(dims, lambda *_: (0,) * len(dims))


def local(
    tokens,
    cached,
    norm_gains,
    w_qkv,
    w_out,
    mlp_weights,
    request_order,
    new_lengths,
    cached_lengths,
    decode_slots,
):
    tensor = ("chip", "core")
    chips, cores = lax.axis_size("chip"), lax.axis_size("core")
    tensor_size = chips * cores
    group_total = lax.axis_size("dp")
    reqs, new, width = tokens.shape
    ctx = cached.shape[1]
    depth = ctx // tensor_size
    flat = reqs * new
    group_reqs = reqs * tensor_size
    group_index = lax.axis_index("dp")
    device = group_index * tensor_size + lax.axis_index(tensor)
    dev = device.astype(jnp.int32).reshape(1)
    key_width = KV_HEADS * HEAD_DIM
    groups = key_width // GROUP
    scalars = (request_order, new_lengths, cached_lengths, dev)
    freq = jnp.asarray(frequencies())

    other_weights = lax.ppermute(mlp_weights, "core", [(0, 1), (1, 0)])

    context_shape = (tensor_size, reqs, depth, key_width)
    context_spec = pl.BlockSpec((tensor_size, reqs, depth, GROUP), lambda g, *_: (0, 0, 0, g))
    table = (reqs, new, GROUP)
    keys, normed, cosine, sine = call(
        key_kernel,
        scalars,
        (groups,),
        [
            whole(tokens.shape),
            whole(norm_gains.shape),
            whole((1, 128)),
            pl.BlockSpec((width, GROUP), lambda g, *_: (0, width // GROUP + g)),
            pl.BlockSpec((reqs, ctx, GROUP), lambda g, *_: (0, 0, g)),
        ],
        [context_spec, whole(tokens.shape), whole(table), whole(table)],
        [shape(context_shape), shape(tokens.shape), shape(table, f32), shape(table, f32)],
        [],
        (tokens, norm_gains, freq, w_qkv, cached),
        2 * flat * width * key_width,
        8 << 20,
    )
    keys_moved = lax.all_to_all(keys, tensor, split_axis=0, concat_axis=0, tiled=True)
    values, residual, post = call(
        attention_kernel,
        scalars,
        (groups,),
        [
            whole(tokens.shape),
            whole(table),
            whole(table),
            pl.BlockSpec((width, 2 * GROUP), lambda g, *_: (0, g)),
            pl.BlockSpec((width, GROUP), lambda g, *_: (0, (width + key_width) // GROUP + g)),
            context_spec,
            pl.BlockSpec((reqs, ctx, GROUP), lambda g, *_: (0, 0, groups + g)),
            whole(tokens.shape),
            whole(norm_gains.shape),
            pl.BlockSpec(memory_space=pl.ANY),
        ],
        [context_spec, whole((flat, width)), whole((flat, width))],
        [shape(context_shape), shape((flat, width)), shape((flat, width))],
        [
            pltpu.VMEM((flat, width), f32),
            pltpu.VMEM((flat, 2 * GROUP), bf16),
            pltpu.VMEM((groups, 2 * GROUP, width), bf16),
            pltpu.SemaphoreType.DMA((groups,)),
        ],
        (normed, cosine, sine, w_qkv, w_qkv, keys, cached, tokens, norm_gains, w_out),
        12 * flat * width * width,
        16 << 20,
    )
    units = mlp_weights.shape[2]
    chunk = 256 if units % 256 == 0 else units

    def mlp(pieces, after):
        total_rows = sum(rows.shape[0] for rows in pieces)
        weight_spec = pl.BlockSpec((3, width, chunk), lambda c: (0, 0, c))
        return call(
            functools.partial(mlp_kernel, len(pieces)),
            (),
            (units // chunk,),
            [weight_spec] * 2 + [whole(rows.shape) for rows in pieces],
            [whole((flat, width))] * (total_rows // flat),
            [shape((flat, width))] * (total_rows // flat),
            [pltpu.VMEM((total_rows, width), f32)],
            (mlp_weights, other_weights, *pieces),
            12 * total_rows * width * units,
            12 * width * units,
            after=after,
        )

    every = request_order.shape[0]
    indices = jnp.arange(every, dtype=jnp.int32)
    slot_of = jnp.sum(
        jnp.where(request_order[:, None] == indices[None, :], decode_slots[None, :], 0), axis=1
    )
    count_of = jnp.sum(
        jnp.where(request_order[:, None] == indices[None, :], new_lengths[None, :], 0), axis=1
    )
    ordinal = jnp.arange(group_reqs, dtype=jnp.int32)

    def inverse(keys_of):
        position = jnp.sum((keys_of[None, :] < keys_of[:, None]).astype(jnp.int32), axis=1)
        return jnp.sum(
            jnp.where(position[None, :] == ordinal[:, None], ordinal[None, :], 0), axis=1
        )

    own_slots = lax.dynamic_slice_in_dim(slot_of, group_index * group_reqs, group_reqs)
    goal = lax.rem(own_slots // group_reqs - group_index + group_total, group_total)
    picked = inverse(goal * group_reqs + lax.rem(own_slots, group_reqs))
    slot_ids = group_index * group_reqs + ordinal
    owners = jnp.sum(
        jnp.where(slot_of[None, :] == slot_ids[:, None], indices[None, :] // group_reqs, 0), axis=1
    )
    origin = lax.rem(group_index - owners + group_total, group_total)
    spots = inverse(origin * group_reqs + ordinal)

    share = group_reqs // group_total
    piece = (share, depth, key_width)
    anywhere = pl.BlockSpec(memory_space=pl.ANY)
    sems = [pltpu.VMEM((group_reqs, depth, key_width), bf16)] + [
        pltpu.SemaphoreType.DMA((group_reqs,))
    ] * 2
    shifts = [
        [(g, (g + s) % group_total) for g in range(group_total)] for s in range(1, group_total)
    ]

    group = group_index.astype(jnp.int32).reshape(1)

    def pack(moved, targets, passed, after):
        return call(
            functools.partial(pack_kernel, group_total, share, len(targets), len(passed)),
            (picked, group), (1,),
            [anywhere] * (1 + len(passed)), [anywhere] * (len(targets) + len(passed)),
            [shape(dims) for dims in targets] + [shape(rows.shape) for rows in passed], sems,
            (moved.reshape(group_reqs, depth, key_width), *passed),
            aliases={3 + i: len(targets) + i for i in range(len(passed))}, after=after,
        )

    def unpack(columns, arrived, target, after):
        return call(
            functools.partial(unpack_kernel, columns, group_total, share, len(arrived)),
            (spots, group), (1,), [anywhere] * (len(arrived) + len(target)), anywhere,
            shape((group_reqs, depth, 2 * key_width)), sems, (*arrived, *target),
            aliases={2 + len(arrived): 0} if target else {}, after=after,
        )

    def swap(rows, mask):
        return lax.ppermute(rows, "chip", [(c, c ^ mask) for c in range(chips)])

    masks = [1, 2] if chips == 4 else range(1, chips)
    gathered = [swap(post, mask) for mask in masks]
    *keys_packed, values = pack(
        keys_moved, [piece] * group_total, (values,), (post, other_weights)
    )
    values_moved = lax.all_to_all(values, tensor, split_axis=0, concat_axis=0, tiled=True)
    keys_arrived = [keys_packed[0]] + [
        lax.ppermute(rows, "dp", pairs) for rows, pairs in zip(keys_packed[1:], shifts)
    ]
    partials = list(mlp([post], (keys_packed[0],)))
    values_packed = pack(
        values_moved, [(group_reqs, depth, key_width)], (),
        (partials[0], *keys_arrived[1:], *gathered),
    )[0]
    values_arrived = lax.all_to_all(values_packed, "dp", split_axis=0, concat_axis=0, tiled=True)
    latest = values_packed
    if chips == 4:
        half = (flat // 2, width)
        first, second = call(
            cut_kernel, (), (1,), [whole((flat, width))] * 2, [whole(half)] * 2,
            [shape(half)] * 2, [], tuple(gathered), after=(latest,),
        )
        latest = first
        batches = [([1, 2], gathered), ([3], [swap(first, 1), swap(second, 2)])]
    else:
        batches = [([mask], [rows]) for mask, rows in zip(masks, gathered)]
    kv_half = None
    for batch_masks, pieces in batches:
        results = mlp(pieces, (latest,))
        latest = results[0]
        partials += [swap(rows, mask) for mask, rows in zip(batch_masks, results)]
        if kv_half is None:
            kv_half = unpack(0, keys_arrived, (), (latest,))
            latest = kv_half
    kv_decode = unpack(key_width, [values_arrived], (kv_half,), ())

    own_counts = lax.dynamic_slice_in_dim(count_of, device * reqs, reqs)
    live = (jnp.arange(new, dtype=jnp.int32)[None, :] < own_counts[:, None]).reshape(flat, 1)
    total = residual.astype(f32)
    for partial in partials:
        total = total + partial.astype(f32)
    layer_out = jnp.where(live, total, 0.0).astype(bf16).reshape(reqs, new, width)
    return (layer_out, kv_decode)


def solution(mesh):
    in_specs = (
        P(("dp", "chip", "core"), None, None),
        P(("dp", "chip", "core"), None, None),
        P(),
        P(),
        P(),
        P(None, None, ("chip", "core")),
        P(),
        P(),
        P(),
        P(),
    )
    out_specs = (P(("dp", "chip", "core"), None, None), P("dp", ("chip", "core"), None))
    devices = mesh.devices.reshape(mesh.devices.shape[0], -1, 2)
    mesh = jax.sharding.Mesh(devices, ("dp", "chip", "core"))
    return jax.shard_map(local, mesh=mesh, in_specs=in_specs, out_specs=out_specs, check_vma=False)
```

```python
import functools
import math

import jax
import jax.numpy as jnp
import numpy as np
from jax import lax
from jax.experimental import pallas as pl
from jax.experimental.pallas import tpu as pltpu
from jax.sharding import PartitionSpec as P

HEADS = 16
KV_HEADS = 8
HEAD_DIM = 96
GROUP = 384
VMEM = 60 * 1024 * 1024
SMALL = 60 * 1024 * 1024

epsilon = 1e-05
rope_base = 100000.0
bf16 = jnp.bfloat16
f32 = jnp.float32


def frequencies():
    half = HEAD_DIM // 2
    steps = np.arange(half, dtype=np.float32)
    frequency = np.float32(rope_base) ** (np.float32(-2.0) * steps / np.float32(HEAD_DIM))
    row = np.zeros((1, 128), np.float32)
    row[0, :half] = frequency
    row[0, half:HEAD_DIM] = frequency
    return row


def norm_value(values, gain):
    factor = lax.rsqrt(jnp.mean(values * values, axis=-1, keepdims=True) + epsilon)
    return (values * factor * gain).astype(bf16)


def rotate(values, cosine, sine):
    width = values.shape[-1]
    half = HEAD_DIM // 2
    lane = lax.broadcasted_iota(jnp.int32, values.shape, 1)
    first = lax.rem(lane, HEAD_DIM) < half
    swapped = jnp.where(
        first, pltpu.roll(values, width - half, 1), pltpu.roll(values, half, 1)
    )
    return values * cosine + swapped * sine


def place(fresh, cached, new_count, cached_count):
    rows, new = cached.shape[0], fresh.shape[0]
    spot = lax.broadcasted_iota(jnp.int32, (rows, new), 0)
    token = lax.broadcasted_iota(jnp.int32, (rows, new), 1)
    chosen = (spot - cached_count == token) & (token < new_count)
    placed = jnp.dot(jnp.where(chosen, 1.0, 0.0).astype(bf16), fresh, preferred_element_type=f32)
    keep = lax.broadcasted_iota(jnp.int32, cached.shape, 0) < cached_count
    return jnp.where(keep, cached.astype(f32), placed).astype(bf16)


def key_kernel(
    order, news, olds, dev, tokens, gain, freq, weight, cached, context, normed, cosine, sine
):
    reqs, new, width = tokens.shape

    @pl.when(pl.program_id(0) == 0)
    def _():
        lane = lax.broadcasted_iota(jnp.int32, (new, 128), 1)
        row = lax.broadcasted_iota(jnp.int32, (new, 128), 0)
        sign = jnp.where(lane < HEAD_DIM // 2, -1.0, 1.0)
        for r in range(reqs):
            normed[r] = norm_value(tokens[r].astype(f32), gain[0:1, :])
            old = olds[order[dev[0] * reqs + r]]
            angles = (row + old).astype(f32) * freq[...]
            cos_part = jnp.cos(angles)[:, :HEAD_DIM]
            sin_part = (jnp.sin(angles) * sign)[:, :HEAD_DIM]
            cosine[r] = jnp.concatenate([cos_part] * 4, axis=1)
            sine[r] = jnp.concatenate([sin_part] * 4, axis=1)

    rows = normed[...].reshape(reqs * new, width)
    projected = jnp.dot(rows, weight[...], preferred_element_type=f32)
    turned = rotate(
        projected,
        cosine[...].reshape(reqs * new, GROUP),
        sine[...].reshape(reqs * new, GROUP),
    ).astype(bf16)
    parts, _, depth, _ = context.shape
    for r in range(reqs):
        request = order[dev[0] * reqs + r]
        merged = place(turned[r * new : (r + 1) * new], cached[r], news[request], olds[request])
        context[:, r] = merged.reshape(parts, depth, GROUP)


def attention_kernel(
    order, news, olds, dev, normed, cosine, sine, weight, w_value, keys, cached, tokens, gain, w_out,
    values, residual, post, total, attended, out_weight, sems,
):
    step = pl.program_id(0)
    reqs, new, width = normed.shape
    parts, _, depth, _ = keys.shape
    ctx = parts * depth
    flat = reqs * new

    def stream(g):
        source = w_out.at[pl.ds(g * 2 * GROUP, 2 * GROUP)]
        return pltpu.make_async_copy(source, out_weight.at[g], sems.at[g])

    @pl.when(step == 0)
    def _():
        for g in range(out_weight.shape[0]):
            stream(g).start()

    rows = normed[...].reshape(flat, width)
    fresh = jnp.dot(rows, w_value[...], preferred_element_type=f32).astype(bf16)
    projected = jnp.dot(rows, weight[...], preferred_element_type=f32)
    cos_part = cosine[...].reshape(flat, GROUP)
    sin_part = sine[...].reshape(flat, GROUP)
    queries = [
        rotate(projected[:, GROUP * i : GROUP * (i + 1)], cos_part, sin_part).astype(bf16)
        for i in range(2)
    ]
    spot = lax.broadcasted_iota(jnp.int32, (new, ctx), 1)
    token = lax.broadcasted_iota(jnp.int32, (new, ctx), 0)
    scale = HEAD_DIM ** (-0.5) * math.log2(math.e)
    for r in range(reqs):
        request = order[dev[0] * reqs + r]
        old = olds[request]
        key_rows = keys[:, r].reshape(ctx, GROUP)
        value_rows = place(fresh[r * new : (r + 1) * new], cached[r], news[request], old)
        values[:, r] = value_rows.reshape(parts, depth, GROUP)
        mask = jnp.where(spot <= old + token, 0.0, -jnp.inf)
        bias = jnp.concatenate([mask, mask], axis=0)
        pieces = []
        for k in range(4):
            key = key_rows[:, HEAD_DIM * k : HEAD_DIM * (k + 1)]
            value = value_rows[:, HEAD_DIM * k : HEAD_DIM * (k + 1)]
            pair = []
            for h in (2 * k, 2 * k + 1):
                at = HEAD_DIM * (h % 4)
                pair.append(queries[h // 4][r * new : (r + 1) * new, at : at + HEAD_DIM])
            scores = lax.dot_general(
                jnp.concatenate(pair, axis=0), key, (((1,), (1,)), ((), ())),
                preferred_element_type=f32,
            )
            scores = scores * scale + bias
            exponent = jnp.exp2(scores - jnp.max(scores, axis=-1, keepdims=True))
            bottom = jnp.sum(exponent, axis=-1, keepdims=True)
            mixed = jnp.dot(exponent.astype(bf16), value, preferred_element_type=f32) / bottom
            pieces += [mixed[:new], mixed[new:]]
        attended[r * new : (r + 1) * new, :] = jnp.concatenate(pieces, axis=1).astype(bf16)
    stream(step).wait()
    term = jnp.dot(attended[...], out_weight[step], preferred_element_type=f32)

    @pl.when(step == 0)
    def _():
        total[...] = tokens[...].astype(f32).reshape(flat, width) + term

    @pl.when(step > 0)
    def _():
        total[...] += term

    @pl.when(step == pl.num_programs(0) - 1)
    def _():
        rounded = total[...].astype(bf16)
        residual[...] = rounded
        post[...] = norm_value(rounded.astype(f32), gain[1:2, :])


def mlp_kernel(count, own, other, *refs):
    inputs, outputs, total = refs[:count], refs[count:-1], refs[-1]
    step = pl.program_id(0)
    values = jnp.concatenate([rows[...] for rows in inputs], axis=0)
    term = None
    for weights in (own, other):
        gate = jnp.dot(values, weights[0], preferred_element_type=f32)
        up = jnp.dot(values, weights[1], preferred_element_type=f32)
        hidden = (gate / (1.0 + jnp.exp(-gate)) * up).astype(bf16)
        product = lax.dot_general(
            hidden, weights[2], (((1,), (1,)), ((), ())), preferred_element_type=f32
        )
        term = product if term is None else term + product

    @pl.when(step == 0)
    def _():
        total[...] = term

    @pl.when(step > 0)
    def _():
        total[...] += term

    @pl.when(step == pl.num_programs(0) - 1)
    def _():
        flat = outputs[0].shape[0]
        for i, out in enumerate(outputs):
            out[...] = total[i * flat : (i + 1) * flat].astype(bf16)


def move_rows(pairs, held, arrive, leave):
    inward = [
        pltpu.make_async_copy(source, held.at[i], arrive.at[i])
        for i, (source, _) in enumerate(pairs)
    ]
    outward = [
        pltpu.make_async_copy(held.at[i], target, leave.at[i])
        for i, (_, target) in enumerate(pairs)
    ]
    for copy in inward:
        copy.start()
    for first, second in zip(inward, outward):
        first.wait()
        second.start()
    for copy in outward:
        copy.wait()


def pack_kernel(groups, share, count, passed, picked, group, source, *rest):
    held, arrive, leave = rest[-3:]
    targets = rest[passed : passed + count]
    pairs = []
    for i in range(groups * share):
        if count > 1:
            target = targets[i // share].at[i % share]
        else:
            goal = lax.rem(group[0] + i // share, groups)
            target = targets[0].at[goal * share + i % share]
        pairs.append((source.at[picked[i]], target))
    move_rows(pairs, held, arrive, leave)


def unpack_kernel(columns, groups, share, count, spots, group, *refs):
    sources, (target, held, arrive, leave) = refs[:count], refs[-4:]
    width = sources[0].shape[-1]
    pairs = []
    for i in range(groups * share):
        if count > 1:
            source = sources[i // share].at[i % share]
        else:
            origin = lax.rem(group[0] + groups - i // share, groups)
            source = sources[0].at[origin * share + i % share]
        pairs.append((source, target.at[spots[i], :, pl.ds(columns, width)]))
    move_rows(pairs, held, arrive, leave)


def gate_kernel(passed, out):
    pass


def sum_kernel(order, news, dev, residual, *refs):
    partials, out = refs[:-1], refs[-1]
    request = order[dev[0] * pl.num_programs(0) + pl.program_id(0)]
    total = residual[...].astype(f32)
    for partial in partials:
        total = total + partial[...].astype(f32)
    live = lax.broadcasted_iota(jnp.int32, total.shape, 0) < news[request]
    out[0] = jnp.where(live, total, 0.0).astype(bf16)


def cut_kernel(first, second, *halves):
    middle = first.shape[0] // 2
    halves[0][...] = second[:middle]
    halves[1][...] = first[middle:]


def call(
    kernel, prefetched, grid, in_specs, out_specs, out_shape, scratch, operands,
    flops=0, moved=6 << 20, aliases={}, after=(), vmem=VMEM,
):
    begin = len(prefetched) + len(operands)

    def ordered(*refs):
        kernel(*refs[:begin], *refs[begin + len(after) :])

    return pl.pallas_call(
        ordered,
        out_shape=out_shape,
        grid_spec=pltpu.PrefetchScalarGridSpec(
            num_scalar_prefetch=len(prefetched),
            grid=grid,
            in_specs=list(in_specs) + [pl.BlockSpec(memory_space=pl.ANY)] * len(after),
            out_specs=out_specs,
            scratch_shapes=scratch,
        ),
        compiler_params=pltpu.CompilerParams(vmem_limit_bytes=vmem),
        cost_estimate=pl.CostEstimate(flops=flops, bytes_accessed=moved, transcendentals=0),
        input_output_aliases=aliases,
    )(*prefetched, *operands, *after)


def shape(dims, dtype=bf16):
    return jax.ShapeDtypeStruct(dims, dtype)


def whole(dims):
    return pl.BlockSpec(dims, lambda *_: (0,) * len(dims))


def local(
    tokens,
    cached,
    norm_gains,
    w_qkv,
    w_out,
    mlp_weights,
    request_order,
    new_lengths,
    cached_lengths,
    decode_slots,
):
    tensor = ("chip", "core")
    chips, cores = lax.axis_size("chip"), lax.axis_size("core")
    tensor_size = chips * cores
    group_total = lax.axis_size("dp")
    reqs, new, width = tokens.shape
    ctx = cached.shape[1]
    depth = ctx // tensor_size
    flat = reqs * new
    group_reqs = reqs * tensor_size
    group_index = lax.axis_index("dp")
    device = group_index * tensor_size + lax.axis_index(tensor)
    dev = device.astype(jnp.int32).reshape(1)
    key_width = KV_HEADS * HEAD_DIM
    groups = key_width // GROUP
    scalars = (request_order, new_lengths, cached_lengths, dev)
    freq = jnp.asarray(frequencies())

    other_weights = lax.ppermute(mlp_weights, "core", [(0, 1), (1, 0)])

    context_shape = (tensor_size, reqs, depth, key_width)
    context_spec = pl.BlockSpec((tensor_size, reqs, depth, GROUP), lambda g, *_: (0, 0, 0, g))
    table = (reqs, new, GROUP)
    keys, normed, cosine, sine = call(
        key_kernel,
        scalars,
        (groups,),
        [
            whole(tokens.shape),
            whole(norm_gains.shape),
            whole((1, 128)),
            pl.BlockSpec((width, GROUP), lambda g, *_: (0, width // GROUP + g)),
            pl.BlockSpec((reqs, ctx, GROUP), lambda g, *_: (0, 0, g)),
        ],
        [context_spec, whole(tokens.shape), whole(table), whole(table)],
        [shape(context_shape), shape(tokens.shape), shape(table, f32), shape(table, f32)],
        [],
        (tokens, norm_gains, freq, w_qkv, cached),
        2 * flat * width * key_width,
        8 << 20,
    )
    keys_moved = lax.all_to_all(keys, tensor, split_axis=0, concat_axis=0, tiled=True)
    values, residual, post = call(
        attention_kernel,
        scalars,
        (groups,),
        [
            whole(tokens.shape),
            whole(table),
            whole(table),
            pl.BlockSpec((width, 2 * GROUP), lambda g, *_: (0, g)),
            pl.BlockSpec((width, GROUP), lambda g, *_: (0, (width + key_width) // GROUP + g)),
            context_spec,
            pl.BlockSpec((reqs, ctx, GROUP), lambda g, *_: (0, 0, groups + g)),
            whole(tokens.shape),
            whole(norm_gains.shape),
            pl.BlockSpec(memory_space=pl.ANY),
        ],
        [context_spec, whole((flat, width)), whole((flat, width))],
        [shape(context_shape), shape((flat, width)), shape((flat, width))],
        [
            pltpu.VMEM((flat, width), f32),
            pltpu.VMEM((flat, 2 * GROUP), bf16),
            pltpu.VMEM((groups, 2 * GROUP, width), bf16),
            pltpu.SemaphoreType.DMA((groups,)),
        ],
        (normed, cosine, sine, w_qkv, w_qkv, keys, cached, tokens, norm_gains, w_out),
        12 * flat * width * width,
        16 << 20,
    )
    units = mlp_weights.shape[2]
    chunk = 256 if units % 256 == 0 else units

    def mlp(pieces, after):
        total_rows = sum(rows.shape[0] for rows in pieces)
        weight_spec = pl.BlockSpec((3, width, chunk), lambda c: (0, 0, c))
        return call(
            functools.partial(mlp_kernel, len(pieces)),
            (),
            (units // chunk,),
            [weight_spec] * 2 + [whole(rows.shape) for rows in pieces],
            [whole((flat, width))] * (total_rows // flat),
            [shape((flat, width))] * (total_rows // flat),
            [pltpu.VMEM((total_rows, width), f32)],
            (mlp_weights, other_weights, *pieces),
            12 * total_rows * width * units,
            12 * width * units,
            after=after,
        )

    every = request_order.shape[0]
    indices = jnp.arange(every, dtype=jnp.int32)
    slot_of = jnp.sum(
        jnp.where(request_order[:, None] == indices[None, :], decode_slots[None, :], 0), axis=1
    )
    ordinal = jnp.arange(group_reqs, dtype=jnp.int32)

    def inverse(keys_of):
        position = jnp.sum((keys_of[None, :] < keys_of[:, None]).astype(jnp.int32), axis=1)
        return jnp.sum(
            jnp.where(position[None, :] == ordinal[:, None], ordinal[None, :], 0), axis=1
        )

    own_slots = lax.dynamic_slice_in_dim(slot_of, group_index * group_reqs, group_reqs)
    goal = lax.rem(own_slots // group_reqs - group_index + group_total, group_total)
    picked = inverse(goal * group_reqs + lax.rem(own_slots, group_reqs))
    slot_ids = group_index * group_reqs + ordinal
    owners = jnp.sum(
        jnp.where(slot_of[None, :] == slot_ids[:, None], indices[None, :] // group_reqs, 0), axis=1
    )
    origin = lax.rem(group_index - owners + group_total, group_total)
    spots = inverse(origin * group_reqs + ordinal)

    share = group_reqs // group_total
    piece = (share, depth, key_width)
    anywhere = pl.BlockSpec(memory_space=pl.ANY)
    sems = [pltpu.VMEM((group_reqs, depth, key_width), bf16)] + [
        pltpu.SemaphoreType.DMA((group_reqs,))
    ] * 2
    shifts = [
        [(g, (g + s) % group_total) for g in range(group_total)] for s in range(1, group_total)
    ]

    group = group_index.astype(jnp.int32).reshape(1)

    def pack(moved, targets, passed, after):
        return call(
            functools.partial(pack_kernel, group_total, share, len(targets), len(passed)),
            (picked, group), (1,),
            [anywhere] * (1 + len(passed)), [anywhere] * (len(targets) + len(passed)),
            [shape(dims) for dims in targets] + [shape(rows.shape) for rows in passed], sems,
            (moved.reshape(group_reqs, depth, key_width), *passed),
            aliases={3 + i: len(targets) + i for i in range(len(passed))}, after=after, vmem=SMALL,
        )

    def unpack(columns, arrived, target, after):
        return call(
            functools.partial(unpack_kernel, columns, group_total, share, len(arrived)),
            (spots, group), (1,), [anywhere] * (len(arrived) + len(target)), anywhere,
            shape((group_reqs, depth, 2 * key_width)), sems, (*arrived, *target),
            aliases={2 + len(arrived): 0} if target else {}, after=after, vmem=SMALL,
        )

    def swap(rows, mask):
        return lax.ppermute(rows, "chip", [(c, c ^ mask) for c in range(chips)])

    masks = [1, 2] if chips == 4 else range(1, chips)
    gathered = [swap(post, mask) for mask in masks]
    *keys_packed, values = pack(
        keys_moved, [piece] * group_total, (values,), (post, other_weights)
    )
    values_moved = lax.all_to_all(values, tensor, split_axis=0, concat_axis=0, tiled=True)
    keys_arrived = [keys_packed[0]] + [
        lax.ppermute(rows, "dp", pairs) for rows, pairs in zip(keys_packed[1:], shifts)
    ]
    partials = list(mlp([post], (keys_packed[0], spots)))
    values_packed = pack(
        values_moved, [(group_reqs, depth, key_width)], (), (partials[0],)
    )[0]
    latest = values_packed
    if chips == 4:
        half = (flat // 2, width)
        first, second = call(
            cut_kernel, (), (1,), [whole((flat, width))] * 2, [whole(half)] * 2,
            [shape(half)] * 2, [], tuple(gathered), after=(latest,),
        )
        latest = first
        batches = [([1, 2], gathered), ([3], [swap(first, 1), swap(second, 2)])]
    else:
        batches = [([mask], [rows]) for mask, rows in zip(masks, gathered)]
    values_ready = call(
        gate_kernel, (), (1,), [anywhere], anywhere, shape(values_packed.shape), [],
        (values_packed,), moved=1 << 10, aliases={0: 0}, after=(latest, *keys_arrived[1:]),
    )
    values_arrived = lax.all_to_all(values_ready, "dp", split_axis=0, concat_axis=0, tiled=True)
    latest = values_ready
    for batch_masks, pieces in batches:
        results = mlp(pieces, (latest,))
        latest = results[0]
        partials += [swap(rows, mask) for mask, rows in zip(batch_masks, results)]
    kv_half = unpack(0, keys_arrived, (), (latest,))
    kv_decode = unpack(key_width, [values_arrived], (kv_half,), ())

    layer_out = call(
        sum_kernel, (request_order, new_lengths, dev), (reqs,),
        [pl.BlockSpec((new, width), lambda r, *_: (r, 0))] * (1 + len(partials)),
        pl.BlockSpec((1, new, width), lambda r, *_: (r, 0, 0)),
        shape(tokens.shape), [], (residual, *partials), after=(kv_decode,), vmem=SMALL,
    )
    return (layer_out, kv_decode)


def solution(mesh):
    in_specs = (
        P(("dp", "chip", "core"), None, None),
        P(("dp", "chip", "core"), None, None),
        P(),
        P(),
        P(),
        P(None, None, ("chip", "core")),
        P(),
        P(),
        P(),
        P(),
    )
    out_specs = (P(("dp", "chip", "core"), None, None), P("dp", ("chip", "core"), None))
    devices = mesh.devices.reshape(mesh.devices.shape[0], -1, 2)
    mesh = jax.sharding.Mesh(devices, ("dp", "chip", "core"))
    return jax.shard_map(local, mesh=mesh, in_specs=in_specs, out_specs=out_specs, check_vma=False)
```

```python
import functools
import math

import jax
import jax.numpy as jnp
import numpy as np
from jax import lax
from jax.experimental import pallas as pl
from jax.experimental.pallas import tpu as pltpu
from jax.sharding import PartitionSpec as P

HEADS = 16
KV_HEADS = 8
HEAD_DIM = 96
GROUP = 384
VMEM = 60 * 1024 * 1024
LONG = 40

epsilon = 1e-05
rope_base = 100000.0
bf16 = jnp.bfloat16
f32 = jnp.float32


def frequencies():
    half = HEAD_DIM // 2
    steps = np.arange(half, dtype=np.float32)
    frequency = np.float32(rope_base) ** (np.float32(-2.0) * steps / np.float32(HEAD_DIM))
    row = np.zeros((1, 128), np.float32)
    row[0, :half] = frequency
    row[0, half:HEAD_DIM] = frequency
    return row


def norm_value(values, gain):
    factor = lax.rsqrt(jnp.mean(values * values, axis=-1, keepdims=True) + epsilon)
    return (values * factor * gain).astype(bf16)


def rotate(values, cosine, sine):
    width = values.shape[-1]
    half = HEAD_DIM // 2
    lane = lax.broadcasted_iota(jnp.int32, values.shape, 1)
    first = lax.rem(lane, HEAD_DIM) < half
    swapped = jnp.where(
        first, pltpu.roll(values, width - half, 1), pltpu.roll(values, half, 1)
    )
    return values * cosine + swapped * sine


def place(fresh, cached, new_count, cached_count):
    rows, new = cached.shape[0], fresh.shape[0]
    spot = lax.broadcasted_iota(jnp.int32, (rows, new), 0)
    token = lax.broadcasted_iota(jnp.int32, (rows, new), 1)
    chosen = (spot - cached_count == token) & (token < new_count)
    placed = jnp.dot(jnp.where(chosen, 1.0, 0.0).astype(bf16), fresh, preferred_element_type=f32)
    keep = lax.broadcasted_iota(jnp.int32, cached.shape, 0) < cached_count
    return jnp.where(keep, cached.astype(f32), placed).astype(bf16)


def key_kernel(
    order, news, olds, dev, tokens, gain, freq, weight, cached, context, normed, cosine, sine
):
    reqs, new, width = tokens.shape

    @pl.when(pl.program_id(0) == 0)
    def _():
        lane = lax.broadcasted_iota(jnp.int32, (new, 128), 1)
        row = lax.broadcasted_iota(jnp.int32, (new, 128), 0)
        sign = jnp.where(lane < HEAD_DIM // 2, -1.0, 1.0)
        for r in range(reqs):
            normed[r] = norm_value(tokens[r].astype(f32), gain[0:1, :])
            old = olds[order[dev[0] * reqs + r]]
            angles = (row + old).astype(f32) * freq[...]
            cos_part = jnp.cos(angles)[:, :HEAD_DIM]
            sin_part = (jnp.sin(angles) * sign)[:, :HEAD_DIM]
            cosine[r] = jnp.concatenate([cos_part] * 4, axis=1)
            sine[r] = jnp.concatenate([sin_part] * 4, axis=1)

    rows = normed[...].reshape(reqs * new, width)
    projected = jnp.dot(rows, weight[...], preferred_element_type=f32)
    turned = rotate(
        projected,
        cosine[...].reshape(reqs * new, GROUP),
        sine[...].reshape(reqs * new, GROUP),
    ).astype(bf16)
    parts, _, depth, _ = context.shape
    for r in range(reqs):
        request = order[dev[0] * reqs + r]
        merged = place(turned[r * new : (r + 1) * new], cached[r], news[request], olds[request])
        context[:, r] = merged.reshape(parts, depth, GROUP)


def attention_kernel(
    order, news, olds, dev, normed, cosine, sine, weight, w_value, keys, cached, tokens, gain, w_out,
    values, residual, post, total, attended, out_weight, sems,
):
    step = pl.program_id(0)
    reqs, new, width = normed.shape
    parts, _, depth, _ = keys.shape
    ctx = parts * depth
    flat = reqs * new

    def stream(g):
        source = w_out.at[pl.ds(g * 2 * GROUP, 2 * GROUP)]
        return pltpu.make_async_copy(source, out_weight.at[g], sems.at[g])

    @pl.when(step == 0)
    def _():
        for g in range(out_weight.shape[0]):
            stream(g).start()

    rows = normed[...].reshape(flat, width)
    fresh = jnp.dot(rows, w_value[...], preferred_element_type=f32).astype(bf16)
    projected = jnp.dot(rows, weight[...], preferred_element_type=f32)
    cos_part = cosine[...].reshape(flat, GROUP)
    sin_part = sine[...].reshape(flat, GROUP)
    queries = [
        rotate(projected[:, GROUP * i : GROUP * (i + 1)], cos_part, sin_part).astype(bf16)
        for i in range(2)
    ]
    spot = lax.broadcasted_iota(jnp.int32, (new, ctx), 1)
    token = lax.broadcasted_iota(jnp.int32, (new, ctx), 0)
    scale = HEAD_DIM ** (-0.5) * math.log2(math.e)
    for r in range(reqs):
        request = order[dev[0] * reqs + r]
        old = olds[request]
        key_rows = keys[:, r].reshape(ctx, GROUP)
        value_rows = place(fresh[r * new : (r + 1) * new], cached[r], news[request], old)
        values[:, r] = value_rows.reshape(parts, depth, GROUP)
        mask = jnp.where(spot <= old + token, 0.0, -jnp.inf)
        bias = jnp.concatenate([mask, mask], axis=0)
        pieces = []
        for k in range(4):
            key = key_rows[:, HEAD_DIM * k : HEAD_DIM * (k + 1)]
            value = value_rows[:, HEAD_DIM * k : HEAD_DIM * (k + 1)]
            pair = []
            for h in (2 * k, 2 * k + 1):
                at = HEAD_DIM * (h % 4)
                pair.append(queries[h // 4][r * new : (r + 1) * new, at : at + HEAD_DIM])
            scores = lax.dot_general(
                jnp.concatenate(pair, axis=0), key, (((1,), (1,)), ((), ())),
                preferred_element_type=f32,
            )
            scores = scores * scale + bias
            exponent = jnp.exp2(scores - jnp.max(scores, axis=-1, keepdims=True))
            bottom = jnp.sum(exponent, axis=-1, keepdims=True)
            mixed = jnp.dot(exponent.astype(bf16), value, preferred_element_type=f32) / bottom
            pieces += [mixed[:new], mixed[new:]]
        attended[r * new : (r + 1) * new, :] = jnp.concatenate(pieces, axis=1).astype(bf16)
    stream(step).wait()
    term = jnp.dot(attended[...], out_weight[step], preferred_element_type=f32)

    @pl.when(step == 0)
    def _():
        total[...] = tokens[...].astype(f32).reshape(flat, width) + term

    @pl.when(step > 0)
    def _():
        total[...] += term

    @pl.when(step == pl.num_programs(0) - 1)
    def _():
        rounded = total[...].astype(bf16)
        residual[...] = rounded
        post[...] = norm_value(rounded.astype(f32), gain[1:2, :])


def mlp_kernel(count, own, other, *refs):
    inputs, outputs, total = refs[:count], refs[count:-1], refs[-1]
    step = pl.program_id(0)
    values = jnp.concatenate([rows[...] for rows in inputs], axis=0)
    term = None
    for weights in (own, other):
        gate = jnp.dot(values, weights[0], preferred_element_type=f32)
        up = jnp.dot(values, weights[1], preferred_element_type=f32)
        hidden = (gate / (1.0 + jnp.exp(-gate)) * up).astype(bf16)
        product = lax.dot_general(
            hidden, weights[2], (((1,), (1,)), ((), ())), preferred_element_type=f32
        )
        term = product if term is None else term + product

    @pl.when(step == 0)
    def _():
        total[...] = term

    @pl.when(step > 0)
    def _():
        total[...] += term

    @pl.when(step == pl.num_programs(0) - 1)
    def _():
        flat = outputs[0].shape[0]
        for i, out in enumerate(outputs):
            out[...] = total[i * flat : (i + 1) * flat].astype(bf16)


def move_rows(pairs, held, arrive, leave):
    inward = [
        pltpu.make_async_copy(source, held.at[i], arrive.at[i])
        for i, (source, _) in enumerate(pairs)
    ]
    outward = [
        pltpu.make_async_copy(held.at[i], target, leave.at[i])
        for i, (_, target) in enumerate(pairs)
    ]
    for copy in inward:
        copy.start()
    for first, second in zip(inward, outward):
        first.wait()
        second.start()
    for copy in outward:
        copy.wait()


def pack_kernel(groups, share, count, passed, picked, group, source, *rest):
    held, arrive, leave = rest[-3:]
    targets = rest[passed : passed + count]
    pairs = []
    for i in range(groups * share):
        if count > 1:
            target = targets[i // share].at[i % share]
        else:
            goal = lax.rem(group[0] + i // share, groups)
            target = targets[0].at[goal * share + i % share]
        pairs.append((source.at[picked[i]], target))
    move_rows(pairs, held, arrive, leave)


def unpack_kernel(columns, groups, share, count, spots, group, *refs):
    sources, (target, held, arrive, leave) = refs[:count], refs[-4:]
    width = sources[0].shape[-1]
    pairs = []
    for i in range(groups * share):
        if count > 1:
            source = sources[i // share].at[i % share]
        else:
            origin = lax.rem(group[0] + groups - i // share, groups)
            source = sources[0].at[origin * share + i % share]
        pairs.append((source, target.at[spots[i], :, pl.ds(columns, width)]))
    move_rows(pairs, held, arrive, leave)


def gate_kernel(*passed):
    pass


def cut_kernel(first, second, *halves):
    middle = first.shape[0] // 2
    halves[0][...] = second[:middle]
    halves[1][...] = first[middle:]


def sum_kernel(order, news, dev, *refs):
    terms, out = refs[:-1], refs[-1]
    request = order[dev[0] * pl.num_programs(0) + pl.program_id(0)]
    total = terms[0][...].astype(f32)
    for term in terms[1:]:
        total = total + term[...].astype(f32)
    live = lax.broadcasted_iota(jnp.int32, total.shape, 0) < news[request]
    out[0] = jnp.where(live, total, 0.0).astype(out.dtype)


def call(
    kernel, prefetched, grid, in_specs, out_specs, out_shape, scratch, operands,
    flops=0, moved=6 << 20, aliases={}, after=(),
):
    begin = len(prefetched) + len(operands)

    def ordered(*refs):
        kernel(*refs[:begin], *refs[begin + len(after) :])

    return pl.pallas_call(
        ordered,
        out_shape=out_shape,
        grid_spec=pltpu.PrefetchScalarGridSpec(
            num_scalar_prefetch=len(prefetched),
            grid=grid,
            in_specs=list(in_specs) + [pl.BlockSpec(memory_space=pl.ANY)] * len(after),
            out_specs=out_specs,
            scratch_shapes=scratch,
        ),
        compiler_params=pltpu.CompilerParams(vmem_limit_bytes=VMEM),
        cost_estimate=pl.CostEstimate(flops=flops, bytes_accessed=moved, transcendentals=0),
        input_output_aliases=aliases,
    )(*prefetched, *operands, *after)


def shape(dims, dtype=bf16):
    return jax.ShapeDtypeStruct(dims, dtype)


def whole(dims):
    return pl.BlockSpec(dims, lambda *_: (0,) * len(dims))


def local(
    tokens,
    cached,
    norm_gains,
    w_qkv,
    w_out,
    mlp_weights,
    request_order,
    new_lengths,
    cached_lengths,
    decode_slots,
):
    tensor = ("chip", "core")
    chips, cores = lax.axis_size("chip"), lax.axis_size("core")
    tensor_size = chips * cores
    group_total = lax.axis_size("dp")
    reqs, new, width = tokens.shape
    ctx = cached.shape[1]
    depth = ctx // tensor_size
    flat = reqs * new
    group_reqs = reqs * tensor_size
    group_index = lax.axis_index("dp")
    device = group_index * tensor_size + lax.axis_index(tensor)
    dev = device.astype(jnp.int32).reshape(1)
    key_width = KV_HEADS * HEAD_DIM
    groups = key_width // GROUP
    scalars = (request_order, new_lengths, cached_lengths, dev)
    freq = jnp.asarray(frequencies())

    other_weights = lax.ppermute(mlp_weights, "core", [(0, 1), (1, 0)])

    context_shape = (tensor_size, reqs, depth, key_width)
    context_spec = pl.BlockSpec((tensor_size, reqs, depth, GROUP), lambda g, *_: (0, 0, 0, g))
    table = (reqs, new, GROUP)
    keys, normed, cosine, sine = call(
        key_kernel,
        scalars,
        (groups,),
        [
            whole(tokens.shape),
            whole(norm_gains.shape),
            whole((1, 128)),
            pl.BlockSpec((width, GROUP), lambda g, *_: (0, width // GROUP + g)),
            pl.BlockSpec((reqs, ctx, GROUP), lambda g, *_: (0, 0, g)),
        ],
        [context_spec, whole(tokens.shape), whole(table), whole(table)],
        [shape(context_shape), shape(tokens.shape), shape(table, f32), shape(table, f32)],
        [],
        (tokens, norm_gains, freq, w_qkv, cached),
        2 * flat * width * key_width,
        8 << 20,
    )
    keys_moved = lax.all_to_all(keys, tensor, split_axis=0, concat_axis=0, tiled=True)
    values, residual, post = call(
        attention_kernel,
        scalars,
        (groups,),
        [
            whole(tokens.shape),
            whole(table),
            whole(table),
            pl.BlockSpec((width, 2 * GROUP), lambda g, *_: (0, g)),
            pl.BlockSpec((width, GROUP), lambda g, *_: (0, (width + key_width) // GROUP + g)),
            context_spec,
            pl.BlockSpec((reqs, ctx, GROUP), lambda g, *_: (0, 0, groups + g)),
            whole(tokens.shape),
            whole(norm_gains.shape),
            pl.BlockSpec(memory_space=pl.ANY),
        ],
        [context_spec, whole((flat, width)), whole((flat, width))],
        [shape(context_shape), shape((flat, width)), shape((flat, width))],
        [
            pltpu.VMEM((flat, width), f32),
            pltpu.VMEM((flat, 2 * GROUP), bf16),
            pltpu.VMEM((groups, 2 * GROUP, width), bf16),
            pltpu.SemaphoreType.DMA((groups,)),
        ],
        (normed, cosine, sine, w_qkv, w_qkv, keys, cached, tokens, norm_gains, w_out),
        12 * flat * width * width,
        16 << 20,
    )
    units = mlp_weights.shape[2]
    chunk = 256 if units % 256 == 0 else units

    def mlp(pieces, after, weight=1):
        total_rows = sum(rows.shape[0] for rows in pieces)
        weight_spec = pl.BlockSpec((3, width, chunk), lambda c: (0, 0, c))
        return call(
            functools.partial(mlp_kernel, len(pieces)),
            (),
            (units // chunk,),
            [weight_spec] * 2 + [whole(rows.shape) for rows in pieces],
            [whole((flat, width))] * (total_rows // flat),
            [shape((flat, width))] * (total_rows // flat),
            [pltpu.VMEM((total_rows, width), f32)],
            (mlp_weights, other_weights, *pieces),
            weight * 12 * total_rows * width * units,
            12 * width * units,
            after=after,
        )

    every = request_order.shape[0]
    indices = jnp.arange(every, dtype=jnp.int32)
    slot_of = jnp.sum(
        jnp.where(request_order[:, None] == indices[None, :], decode_slots[None, :], 0), axis=1
    )
    ordinal = jnp.arange(group_reqs, dtype=jnp.int32)

    def inverse(keys_of):
        position = jnp.sum((keys_of[None, :] < keys_of[:, None]).astype(jnp.int32), axis=1)
        return jnp.sum(
            jnp.where(position[None, :] == ordinal[:, None], ordinal[None, :], 0), axis=1
        )

    own_slots = lax.dynamic_slice_in_dim(slot_of, group_index * group_reqs, group_reqs)
    goal = lax.rem(own_slots // group_reqs - group_index + group_total, group_total)
    picked = inverse(goal * group_reqs + lax.rem(own_slots, group_reqs))
    slot_ids = group_index * group_reqs + ordinal
    owners = jnp.sum(
        jnp.where(slot_of[None, :] == slot_ids[:, None], indices[None, :] // group_reqs, 0), axis=1
    )
    origin = lax.rem(group_index - owners + group_total, group_total)
    spots = inverse(origin * group_reqs + ordinal)

    share = group_reqs // group_total
    piece = (share, depth, key_width)
    anywhere = pl.BlockSpec(memory_space=pl.ANY)
    sems = [pltpu.VMEM((group_reqs, depth, key_width), bf16)] + [
        pltpu.SemaphoreType.DMA((group_reqs,))
    ] * 2
    shifts = [
        [(g, (g + s) % group_total) for g in range(group_total)] for s in range(1, group_total)
    ]

    group = group_index.astype(jnp.int32).reshape(1)

    def pack(moved, targets, passed, after):
        return call(
            functools.partial(pack_kernel, group_total, share, len(targets), len(passed)),
            (picked, group), (1,),
            [anywhere] * (1 + len(passed)), [anywhere] * (len(targets) + len(passed)),
            [shape(dims) for dims in targets] + [shape(rows.shape) for rows in passed], sems,
            (moved.reshape(group_reqs, depth, key_width), *passed),
            aliases={3 + i: len(targets) + i for i in range(len(passed))}, after=after,
        )

    def unpack(columns, arrived, target, after):
        return call(
            functools.partial(unpack_kernel, columns, group_total, share, len(arrived)),
            (spots, group), (1,), [anywhere] * (len(arrived) + len(target)), anywhere,
            shape((group_reqs, depth, 2 * key_width)), sems, (*arrived, *target),
            aliases={2 + len(arrived): 0} if target else {}, after=after,
        )

    def swap(rows, mask):
        return lax.ppermute(rows, "chip", [(c, c ^ mask) for c in range(chips)])

    masks = [1, 2] if chips == 4 else range(1, chips)
    gathered = [swap(post, mask) for mask in masks]
    *keys_packed, values = pack(
        keys_moved, [piece] * group_total, (values,), (post, other_weights)
    )
    values_moved = lax.all_to_all(values, tensor, split_axis=0, concat_axis=0, tiled=True)
    keys_arrived = [keys_packed[0]] + [
        lax.ppermute(rows, "dp", pairs) for rows, pairs in zip(keys_packed[1:], shifts)
    ]
    latest = keys_packed[0]
    if chips == 4:
        half = (flat // 2, width)
        first, second = call(
            cut_kernel, (), (1,), [whole((flat, width))] * 2, [whole(half)] * 2,
            [shape(half)] * 2, [], tuple(gathered), after=(latest,),
        )
        latest = first
        batches = [([1, 2], gathered), ([3], [swap(first, 1), swap(second, 2)])]
    else:
        batches = [([mask], [rows]) for mask, rows in zip(masks, gathered)]
    partials = list(mlp([post], (latest, spots), LONG))
    values_packed = pack(
        values_moved, [(group_reqs, depth, key_width)], (), (partials[0],)
    )[0]
    latest = values_packed
    pair = mlp(batches[0][1], (latest, *(rows for batch in batches[1:2] for rows in batch[1])))
    latest = pair[0]
    values_ready, *pair = call(
        gate_kernel, (), (1,), [anywhere] * (1 + len(pair)), [anywhere] * (1 + len(pair)),
        [shape(rows.shape) for rows in (values_packed, *pair)], [], (values_packed, *pair),
        moved=1 << 10, aliases={i: i for i in range(1 + len(pair))}, after=tuple(keys_arrived[1:]),
    )
    values_arrived = lax.all_to_all(values_ready, "dp", split_axis=0, concat_axis=0, tiled=True)
    latest = values_ready
    for i, (batch_masks, pieces) in enumerate(batches):
        results = mlp(pieces, (latest,)) if i else pair
        latest = results[0] if i else latest
        partials += [swap(rows, mask) for mask, rows in zip(batch_masks, results)]

    def add(terms, out_shape, after, flops):
        return call(
            sum_kernel, (request_order, new_lengths, dev), (reqs,),
            [pl.BlockSpec((new, width), lambda r, *_: (r, 0))] * len(terms),
            pl.BlockSpec((1, new, width), lambda r, *_: (r, 0, 0)),
            out_shape, [], tuple(terms), flops, after=after,
        )

    most = add(
        [residual, *partials[:-1]], shape(tokens.shape, f32), (values_ready,), LONG * flat * width * width * 8
    )
    layer_out = add([most.reshape(flat, width), partials[-1]], shape(tokens.shape), (), 0)
    kv_half = unpack(0, keys_arrived, (), (layer_out,))
    kv_decode = unpack(key_width, [values_arrived], (kv_half,), ())
    return (layer_out, kv_decode)


def solution(mesh):
    in_specs = (
        P(("dp", "chip", "core"), None, None),
        P(("dp", "chip", "core"), None, None),
        P(),
        P(),
        P(),
        P(None, None, ("chip", "core")),
        P(),
        P(),
        P(),
        P(),
    )
    out_specs = (P(("dp", "chip", "core"), None, None), P("dp", ("chip", "core"), None))
    devices = mesh.devices.reshape(mesh.devices.shape[0], -1, 2)
    mesh = jax.sharding.Mesh(devices, ("dp", "chip", "core"))
    return jax.shard_map(local, mesh=mesh, in_specs=in_specs, out_specs=out_specs, check_vma=False)
```

```python
import functools
import math

import jax
import jax.numpy as jnp
import numpy as np
from jax import lax
from jax.experimental import pallas as pl
from jax.experimental.pallas import tpu as pltpu
from jax.sharding import PartitionSpec as P

HEADS = 16
KV_HEADS = 8
HEAD_DIM = 96
GROUP = 384
VMEM = 60 * 1024 * 1024
LONG = 40

epsilon = 1e-05
rope_base = 100000.0
bf16 = jnp.bfloat16
f32 = jnp.float32


def frequencies():
    half = HEAD_DIM // 2
    steps = np.arange(half, dtype=np.float32)
    frequency = np.float32(rope_base) ** (np.float32(-2.0) * steps / np.float32(HEAD_DIM))
    row = np.zeros((1, 128), np.float32)
    row[0, :half] = frequency
    row[0, half:HEAD_DIM] = frequency
    return row


def norm_value(values, gain):
    factor = lax.rsqrt(jnp.mean(values * values, axis=-1, keepdims=True) + epsilon)
    return (values * factor * gain).astype(bf16)


def rotate(values, cosine, sine):
    width = values.shape[-1]
    half = HEAD_DIM // 2
    lane = lax.broadcasted_iota(jnp.int32, values.shape, 1)
    first = lax.rem(lane, HEAD_DIM) < half
    swapped = jnp.where(
        first, pltpu.roll(values, width - half, 1), pltpu.roll(values, half, 1)
    )
    return values * cosine + swapped * sine


def place(fresh, cached, new_count, cached_count):
    rows, new = cached.shape[0], fresh.shape[0]
    spot = lax.broadcasted_iota(jnp.int32, (rows, new), 0)
    token = lax.broadcasted_iota(jnp.int32, (rows, new), 1)
    chosen = (spot - cached_count == token) & (token < new_count)
    placed = jnp.dot(jnp.where(chosen, 1.0, 0.0).astype(bf16), fresh, preferred_element_type=f32)
    keep = lax.broadcasted_iota(jnp.int32, cached.shape, 0) < cached_count
    return jnp.where(keep, cached.astype(f32), placed).astype(bf16)


def key_kernel(
    order, news, olds, dev, tokens, gain, freq, weight, cached, context, normed, cosine, sine
):
    reqs, new, width = tokens.shape

    @pl.when(pl.program_id(0) == 0)
    def _():
        lane = lax.broadcasted_iota(jnp.int32, (new, 128), 1)
        row = lax.broadcasted_iota(jnp.int32, (new, 128), 0)
        sign = jnp.where(lane < HEAD_DIM // 2, -1.0, 1.0)
        for r in range(reqs):
            normed[r] = norm_value(tokens[r].astype(f32), gain[0:1, :])
            old = olds[order[dev[0] * reqs + r]]
            angles = (row + old).astype(f32) * freq[...]
            cos_part = jnp.cos(angles)[:, :HEAD_DIM]
            sin_part = (jnp.sin(angles) * sign)[:, :HEAD_DIM]
            cosine[r] = jnp.concatenate([cos_part] * 4, axis=1)
            sine[r] = jnp.concatenate([sin_part] * 4, axis=1)

    rows = normed[...].reshape(reqs * new, width)
    projected = jnp.dot(rows, weight[...], preferred_element_type=f32)
    turned = rotate(
        projected,
        cosine[...].reshape(reqs * new, GROUP),
        sine[...].reshape(reqs * new, GROUP),
    ).astype(bf16)
    parts, _, depth, _ = context.shape
    for r in range(reqs):
        request = order[dev[0] * reqs + r]
        merged = place(turned[r * new : (r + 1) * new], cached[r], news[request], olds[request])
        context[:, r] = merged.reshape(parts, depth, GROUP)


def attention_kernel(
    order, news, olds, dev, normed, cosine, sine, weight, w_value, keys, cached, tokens, gain, w_out,
    values, residual, post, total, attended, out_weight, sems,
):
    step = pl.program_id(0)
    reqs, new, width = normed.shape
    parts, _, depth, _ = keys.shape
    ctx = parts * depth
    flat = reqs * new

    def stream(g):
        source = w_out.at[pl.ds(g * 2 * GROUP, 2 * GROUP)]
        return pltpu.make_async_copy(source, out_weight.at[g], sems.at[g])

    @pl.when(step == 0)
    def _():
        for g in range(out_weight.shape[0]):
            stream(g).start()

    rows = normed[...].reshape(flat, width)
    fresh = jnp.dot(rows, w_value[...], preferred_element_type=f32).astype(bf16)
    projected = jnp.dot(rows, weight[...], preferred_element_type=f32)
    cos_part = cosine[...].reshape(flat, GROUP)
    sin_part = sine[...].reshape(flat, GROUP)
    queries = [
        rotate(projected[:, GROUP * i : GROUP * (i + 1)], cos_part, sin_part).astype(bf16)
        for i in range(2)
    ]
    spot = lax.broadcasted_iota(jnp.int32, (new, ctx), 1)
    token = lax.broadcasted_iota(jnp.int32, (new, ctx), 0)
    scale = HEAD_DIM ** (-0.5) * math.log2(math.e)
    for r in range(reqs):
        request = order[dev[0] * reqs + r]
        old = olds[request]
        key_rows = keys[:, r].reshape(ctx, GROUP)
        value_rows = place(fresh[r * new : (r + 1) * new], cached[r], news[request], old)
        values[:, r] = value_rows.reshape(parts, depth, GROUP)
        mask = jnp.where(spot <= old + token, 0.0, -jnp.inf)
        bias = jnp.concatenate([mask, mask], axis=0)
        pieces = []
        for k in range(4):
            key = key_rows[:, HEAD_DIM * k : HEAD_DIM * (k + 1)]
            value = value_rows[:, HEAD_DIM * k : HEAD_DIM * (k + 1)]
            pair = []
            for h in (2 * k, 2 * k + 1):
                at = HEAD_DIM * (h % 4)
                pair.append(queries[h // 4][r * new : (r + 1) * new, at : at + HEAD_DIM])
            scores = lax.dot_general(
                jnp.concatenate(pair, axis=0), key, (((1,), (1,)), ((), ())),
                preferred_element_type=f32,
            )
            scores = scores * scale + bias
            exponent = jnp.exp2(scores - jnp.max(scores, axis=-1, keepdims=True))
            bottom = jnp.sum(exponent, axis=-1, keepdims=True)
            mixed = jnp.dot(exponent.astype(bf16), value, preferred_element_type=f32) / bottom
            pieces += [mixed[:new], mixed[new:]]
        attended[r * new : (r + 1) * new, :] = jnp.concatenate(pieces, axis=1).astype(bf16)
    stream(step).wait()
    term = jnp.dot(attended[...], out_weight[step], preferred_element_type=f32)

    @pl.when(step == 0)
    def _():
        total[...] = tokens[...].astype(f32).reshape(flat, width) + term

    @pl.when(step > 0)
    def _():
        total[...] += term

    @pl.when(step == pl.num_programs(0) - 1)
    def _():
        rounded = total[...].astype(bf16)
        residual[...] = rounded
        post[...] = norm_value(rounded.astype(f32), gain[1:2, :])


def mlp_kernel(count, own, other, *refs):
    inputs, outputs, total = refs[:count], refs[count:-1], refs[-1]
    step = pl.program_id(0)
    values = jnp.concatenate([rows[...] for rows in inputs], axis=0)
    term = None
    for weights in (own, other):
        gate = jnp.dot(values, weights[0], preferred_element_type=f32)
        up = jnp.dot(values, weights[1], preferred_element_type=f32)
        hidden = (gate / (1.0 + jnp.exp(-gate)) * up).astype(bf16)
        product = lax.dot_general(
            hidden, weights[2], (((1,), (1,)), ((), ())), preferred_element_type=f32
        )
        term = product if term is None else term + product

    @pl.when(step == 0)
    def _():
        total[...] = term

    @pl.when(step > 0)
    def _():
        total[...] += term

    @pl.when(step == pl.num_programs(0) - 1)
    def _():
        flat = outputs[0].shape[0]
        for i, out in enumerate(outputs):
            out[...] = total[i * flat : (i + 1) * flat].astype(bf16)


def move_rows(pairs, held, arrive, leave):
    inward = [
        pltpu.make_async_copy(source, held.at[i], arrive.at[i])
        for i, (source, _) in enumerate(pairs)
    ]
    outward = [
        pltpu.make_async_copy(held.at[i], target, leave.at[i])
        for i, (_, target) in enumerate(pairs)
    ]
    for copy in inward:
        copy.start()
    for first, second in zip(inward, outward):
        first.wait()
        second.start()
    for copy in outward:
        copy.wait()


def pack_kernel(groups, share, count, passed, picked, group, source, *rest):
    held, arrive, leave = rest[-3:]
    targets = rest[passed : passed + count]
    pairs = []
    for i in range(groups * share):
        if count > 1:
            target = targets[i // share].at[i % share]
        else:
            goal = lax.rem(group[0] + i // share, groups)
            target = targets[0].at[goal * share + i % share]
        pairs.append((source.at[picked[i]], target))
    move_rows(pairs, held, arrive, leave)


def unpack_kernel(columns, groups, share, count, spots, group, *refs):
    sources, (target, held, arrive, leave) = refs[:count], refs[-4:]
    width = sources[0].shape[-1]
    pairs = []
    for i in range(groups * share):
        if count > 1:
            source = sources[i // share].at[i % share]
        else:
            origin = lax.rem(group[0] + groups - i // share, groups)
            source = sources[0].at[origin * share + i % share]
        pairs.append((source, target.at[spots[i], :, pl.ds(columns, width)]))
    move_rows(pairs, held, arrive, leave)


def gate_kernel(*passed):
    pass


def cut_kernel(first, second, *halves):
    middle = first.shape[0] // 2
    halves[0][...] = second[:middle]
    halves[1][...] = first[middle:]


def sum_kernel(order, news, dev, *refs):
    terms, out = refs[:-1], refs[-1]
    request = order[dev[0] * pl.num_programs(0) + pl.program_id(0)]
    total = terms[0][...].astype(f32)
    for term in terms[1:]:
        total = total + term[...].astype(f32)
    live = lax.broadcasted_iota(jnp.int32, total.shape, 0) < news[request]
    out[0] = jnp.where(live, total, 0.0).astype(out.dtype)


def call(
    kernel, prefetched, grid, in_specs, out_specs, out_shape, scratch, operands,
    flops=0, moved=6 << 20, aliases={}, after=(),
):
    begin = len(prefetched) + len(operands)

    def ordered(*refs):
        kernel(*refs[:begin], *refs[begin + len(after) :])

    return pl.pallas_call(
        ordered,
        out_shape=out_shape,
        grid_spec=pltpu.PrefetchScalarGridSpec(
            num_scalar_prefetch=len(prefetched),
            grid=grid,
            in_specs=list(in_specs) + [pl.BlockSpec(memory_space=pl.ANY)] * len(after),
            out_specs=out_specs,
            scratch_shapes=scratch,
        ),
        compiler_params=pltpu.CompilerParams(vmem_limit_bytes=VMEM),
        cost_estimate=pl.CostEstimate(flops=flops, bytes_accessed=moved, transcendentals=0),
        input_output_aliases=aliases,
    )(*prefetched, *operands, *after)


def shape(dims, dtype=bf16):
    return jax.ShapeDtypeStruct(dims, dtype)


def whole(dims):
    return pl.BlockSpec(dims, lambda *_: (0,) * len(dims))


def local(
    tokens,
    cached,
    norm_gains,
    w_qkv,
    w_out,
    mlp_weights,
    request_order,
    new_lengths,
    cached_lengths,
    decode_slots,
):
    tensor = ("chip", "core")
    chips, cores = lax.axis_size("chip"), lax.axis_size("core")
    tensor_size = chips * cores
    group_total = lax.axis_size("dp")
    reqs, new, width = tokens.shape
    ctx = cached.shape[1]
    depth = ctx // tensor_size
    flat = reqs * new
    group_reqs = reqs * tensor_size
    group_index = lax.axis_index("dp")
    device = group_index * tensor_size + lax.axis_index(tensor)
    dev = device.astype(jnp.int32).reshape(1)
    key_width = KV_HEADS * HEAD_DIM
    groups = key_width // GROUP
    scalars = (request_order, new_lengths, cached_lengths, dev)
    freq = jnp.asarray(frequencies())

    other_weights = lax.ppermute(mlp_weights, "core", [(0, 1), (1, 0)])

    context_shape = (tensor_size, reqs, depth, key_width)
    context_spec = pl.BlockSpec((tensor_size, reqs, depth, GROUP), lambda g, *_: (0, 0, 0, g))
    table = (reqs, new, GROUP)
    keys, normed, cosine, sine = call(
        key_kernel,
        scalars,
        (groups,),
        [
            whole(tokens.shape),
            whole(norm_gains.shape),
            whole((1, 128)),
            pl.BlockSpec((width, GROUP), lambda g, *_: (0, width // GROUP + g)),
            pl.BlockSpec((reqs, ctx, GROUP), lambda g, *_: (0, 0, g)),
        ],
        [context_spec, whole(tokens.shape), whole(table), whole(table)],
        [shape(context_shape), shape(tokens.shape), shape(table, f32), shape(table, f32)],
        [],
        (tokens, norm_gains, freq, w_qkv, cached),
        2 * flat * width * key_width,
        8 << 20,
    )
    keys_moved = lax.all_to_all(keys, tensor, split_axis=0, concat_axis=0, tiled=True)
    values, residual, post = call(
        attention_kernel,
        scalars,
        (groups,),
        [
            whole(tokens.shape),
            whole(table),
            whole(table),
            pl.BlockSpec((width, 2 * GROUP), lambda g, *_: (0, g)),
            pl.BlockSpec((width, GROUP), lambda g, *_: (0, (width + key_width) // GROUP + g)),
            context_spec,
            pl.BlockSpec((reqs, ctx, GROUP), lambda g, *_: (0, 0, groups + g)),
            whole(tokens.shape),
            whole(norm_gains.shape),
            pl.BlockSpec(memory_space=pl.ANY),
        ],
        [context_spec, whole((flat, width)), whole((flat, width))],
        [shape(context_shape), shape((flat, width)), shape((flat, width))],
        [
            pltpu.VMEM((flat, width), f32),
            pltpu.VMEM((flat, 2 * GROUP), bf16),
            pltpu.VMEM((groups, 2 * GROUP, width), bf16),
            pltpu.SemaphoreType.DMA((groups,)),
        ],
        (normed, cosine, sine, w_qkv, w_qkv, keys, cached, tokens, norm_gains, w_out),
        12 * flat * width * width,
        16 << 20,
    )
    units = mlp_weights.shape[2]
    chunk = 256 if units % 256 == 0 else units

    def mlp(pieces, after, weight=1):
        total_rows = sum(rows.shape[0] for rows in pieces)
        weight_spec = pl.BlockSpec((3, width, chunk), lambda c: (0, 0, c))
        return call(
            functools.partial(mlp_kernel, len(pieces)),
            (),
            (units // chunk,),
            [weight_spec] * 2 + [whole(rows.shape) for rows in pieces],
            [whole((flat, width))] * (total_rows // flat),
            [shape((flat, width))] * (total_rows // flat),
            [pltpu.VMEM((total_rows, width), f32)],
            (mlp_weights, other_weights, *pieces),
            weight * 12 * total_rows * width * units,
            12 * width * units,
            after=after,
        )

    every = request_order.shape[0]
    indices = jnp.arange(every, dtype=jnp.int32)
    slot_of = jnp.sum(
        jnp.where(request_order[:, None] == indices[None, :], decode_slots[None, :], 0), axis=1
    )
    ordinal = jnp.arange(group_reqs, dtype=jnp.int32)

    def inverse(keys_of):
        position = jnp.sum((keys_of[None, :] < keys_of[:, None]).astype(jnp.int32), axis=1)
        return jnp.sum(
            jnp.where(position[None, :] == ordinal[:, None], ordinal[None, :], 0), axis=1
        )

    own_slots = lax.dynamic_slice_in_dim(slot_of, group_index * group_reqs, group_reqs)
    goal = lax.rem(own_slots // group_reqs - group_index + group_total, group_total)
    picked = inverse(goal * group_reqs + lax.rem(own_slots, group_reqs))
    slot_ids = group_index * group_reqs + ordinal
    owners = jnp.sum(
        jnp.where(slot_of[None, :] == slot_ids[:, None], indices[None, :] // group_reqs, 0), axis=1
    )
    origin = lax.rem(group_index - owners + group_total, group_total)
    spots = inverse(origin * group_reqs + ordinal)

    share = group_reqs // group_total
    piece = (share, depth, key_width)
    anywhere = pl.BlockSpec(memory_space=pl.ANY)
    sems = [pltpu.VMEM((group_reqs, depth, key_width), bf16)] + [
        pltpu.SemaphoreType.DMA((group_reqs,))
    ] * 2
    shifts = [
        [(g, (g + s) % group_total) for g in range(group_total)] for s in range(1, group_total)
    ]

    group = group_index.astype(jnp.int32).reshape(1)

    def pack(moved, targets, passed, after):
        return call(
            functools.partial(pack_kernel, group_total, share, len(targets), len(passed)),
            (picked, group), (1,),
            [anywhere] * (1 + len(passed)), [anywhere] * (len(targets) + len(passed)),
            [shape(dims) for dims in targets] + [shape(rows.shape) for rows in passed], sems,
            (moved.reshape(group_reqs, depth, key_width), *passed),
            aliases={3 + i: len(targets) + i for i in range(len(passed))}, after=after,
        )

    def unpack(columns, arrived, target, after, flops=0):
        return call(
            functools.partial(unpack_kernel, columns, group_total, share, len(arrived)),
            (spots, group), (1,), [anywhere] * (len(arrived) + len(target)), anywhere,
            shape((group_reqs, depth, 2 * key_width)), sems, (*arrived, *target), flops,
            aliases={2 + len(arrived): 0} if target else {}, after=after,
        )

    def swap(rows, mask):
        return lax.ppermute(rows, "chip", [(c, c ^ mask) for c in range(chips)])

    masks = [1, 2] if chips == 4 else range(1, chips)
    gathered = [swap(post, mask) for mask in masks]
    *keys_packed, values = pack(
        keys_moved, [piece] * group_total, (values,), (post, other_weights)
    )
    values_moved = lax.all_to_all(values, tensor, split_axis=0, concat_axis=0, tiled=True)
    keys_arrived = [keys_packed[0]] + [
        lax.ppermute(rows, "dp", pairs) for rows, pairs in zip(keys_packed[1:], shifts)
    ]
    latest = keys_packed[0]
    if chips == 4:
        half = (flat // 2, width)
        first, second = call(
            cut_kernel, (), (1,), [whole((flat, width))] * 2, [whole(half)] * 2,
            [shape(half)] * 2, [], tuple(gathered), after=(latest,),
        )
        latest = first
        batches = [([1, 2], gathered), ([3], [swap(first, 1), swap(second, 2)])]
    else:
        batches = [([mask], [rows]) for mask, rows in zip(masks, gathered)]
    partials = list(mlp([post], (latest, spots), LONG))
    values_packed = pack(
        values_moved, [(group_reqs, depth, key_width)], (), (partials[0],)
    )[0]
    latest = values_packed
    pair = mlp(batches[0][1], (latest, *(rows for batch in batches[1:2] for rows in batch[1])))
    latest = pair[0]
    values_ready, *pair = call(
        gate_kernel, (), (1,), [anywhere] * (1 + len(pair)), [anywhere] * (1 + len(pair)),
        [shape(rows.shape) for rows in (values_packed, *pair)], [], (values_packed, *pair),
        moved=1 << 10, aliases={i: i for i in range(1 + len(pair))}, after=tuple(keys_arrived[1:]),
    )
    values_arrived = lax.all_to_all(values_ready, "dp", split_axis=0, concat_axis=0, tiled=True)
    latest = values_ready
    for i, (batch_masks, pieces) in enumerate(batches):
        results = mlp(pieces, (latest,)) if i else pair
        latest = results[0] if i else latest
        partials += [swap(rows, mask) for mask, rows in zip(batch_masks, results)]

    kv_half = unpack(0, keys_arrived, (), (latest,))

    def add(terms, out_shape, after, flops):
        return call(
            sum_kernel, (request_order, new_lengths, dev), (reqs,),
            [pl.BlockSpec((new, width), lambda r, *_: (r, 0))] * len(terms),
            pl.BlockSpec((1, new, width), lambda r, *_: (r, 0, 0)),
            out_shape, [], tuple(terms), flops, after=after,
        )

    kv_decode = unpack(
        key_width, [values_arrived], (kv_half,), tuple(partials[1:-1]), LONG * flat * width * width * 8
    )
    layer_out = add([residual, *partials], shape(tokens.shape), (kv_decode,), 0)
    return (layer_out, kv_decode)


def solution(mesh):
    in_specs = (
        P(("dp", "chip", "core"), None, None),
        P(("dp", "chip", "core"), None, None),
        P(),
        P(),
        P(),
        P(None, None, ("chip", "core")),
        P(),
        P(),
        P(),
        P(),
    )
    out_specs = (P(("dp", "chip", "core"), None, None), P("dp", ("chip", "core"), None))
    devices = mesh.devices.reshape(mesh.devices.shape[0], -1, 2)
    mesh = jax.sharding.Mesh(devices, ("dp", "chip", "core"))
    return jax.shard_map(local, mesh=mesh, in_specs=in_specs, out_specs=out_specs, check_vma=False)
```

```python
import functools
import math

import jax
import jax.numpy as jnp
import numpy as np
from jax import lax
from jax.experimental import pallas as pl
from jax.experimental.pallas import tpu as pltpu
from jax.sharding import PartitionSpec as P

HEADS = 16
KV_HEADS = 8
HEAD_DIM = 96
GROUP = 384
VMEM = 60 * 1024 * 1024
LONG = 40

epsilon = 1e-05
rope_base = 100000.0
bf16 = jnp.bfloat16
f32 = jnp.float32


def frequencies():
    half = HEAD_DIM // 2
    steps = np.arange(half, dtype=np.float32)
    frequency = np.float32(rope_base) ** (np.float32(-2.0) * steps / np.float32(HEAD_DIM))
    row = np.zeros((1, 128), np.float32)
    row[0, :half] = frequency
    row[0, half:HEAD_DIM] = frequency
    return row


def norm_value(values, gain):
    factor = lax.rsqrt(jnp.mean(values * values, axis=-1, keepdims=True) + epsilon)
    return (values * factor * gain).astype(bf16)


def rotate(values, cosine, sine):
    width = values.shape[-1]
    half = HEAD_DIM // 2
    lane = lax.broadcasted_iota(jnp.int32, values.shape, 1)
    first = lax.rem(lane, HEAD_DIM) < half
    swapped = jnp.where(
        first, pltpu.roll(values, width - half, 1), pltpu.roll(values, half, 1)
    )
    return values * cosine + swapped * sine


def place(fresh, cached, new_count, cached_count):
    rows, new = cached.shape[0], fresh.shape[0]
    spot = lax.broadcasted_iota(jnp.int32, (rows, new), 0)
    token = lax.broadcasted_iota(jnp.int32, (rows, new), 1)
    chosen = (spot - cached_count == token) & (token < new_count)
    placed = jnp.dot(jnp.where(chosen, 1.0, 0.0).astype(bf16), fresh, preferred_element_type=f32)
    keep = lax.broadcasted_iota(jnp.int32, cached.shape, 0) < cached_count
    return jnp.where(keep, cached.astype(f32), placed).astype(bf16)


def key_kernel(
    order, news, olds, dev, tokens, gain, freq, weight, cached, context, normed, cosine, sine
):
    reqs, new, width = tokens.shape

    @pl.when(pl.program_id(0) == 0)
    def _():
        lane = lax.broadcasted_iota(jnp.int32, (new, 128), 1)
        row = lax.broadcasted_iota(jnp.int32, (new, 128), 0)
        sign = jnp.where(lane < HEAD_DIM // 2, -1.0, 1.0)
        for r in range(reqs):
            normed[r] = norm_value(tokens[r].astype(f32), gain[0:1, :])
            old = olds[order[dev[0] * reqs + r]]
            angles = (row + old).astype(f32) * freq[...]
            cos_part = jnp.cos(angles)[:, :HEAD_DIM]
            sin_part = (jnp.sin(angles) * sign)[:, :HEAD_DIM]
            cosine[r] = jnp.concatenate([cos_part] * 4, axis=1)
            sine[r] = jnp.concatenate([sin_part] * 4, axis=1)

    rows = normed[...].reshape(reqs * new, width)
    projected = jnp.dot(rows, weight[...], preferred_element_type=f32)
    turned = rotate(
        projected,
        cosine[...].reshape(reqs * new, GROUP),
        sine[...].reshape(reqs * new, GROUP),
    ).astype(bf16)
    parts, _, depth, _ = context.shape
    for r in range(reqs):
        request = order[dev[0] * reqs + r]
        merged = place(turned[r * new : (r + 1) * new], cached[r], news[request], olds[request])
        context[:, r] = merged.reshape(parts, depth, GROUP)


def attention_kernel(
    order, news, olds, dev, normed, cosine, sine, weight, w_value, keys, cached, tokens, gain, w_out,
    values, residual, post, total, attended, out_weight, sems,
):
    step = pl.program_id(0)
    reqs, new, width = normed.shape
    parts, _, depth, _ = keys.shape
    ctx = parts * depth
    flat = reqs * new

    def stream(g):
        source = w_out.at[pl.ds(g * 2 * GROUP, 2 * GROUP)]
        return pltpu.make_async_copy(source, out_weight.at[g], sems.at[g])

    @pl.when(step == 0)
    def _():
        for g in range(out_weight.shape[0]):
            stream(g).start()

    rows = normed[...].reshape(flat, width)
    fresh = jnp.dot(rows, w_value[...], preferred_element_type=f32).astype(bf16)
    projected = jnp.dot(rows, weight[...], preferred_element_type=f32)
    cos_part = cosine[...].reshape(flat, GROUP)
    sin_part = sine[...].reshape(flat, GROUP)
    queries = [
        rotate(projected[:, GROUP * i : GROUP * (i + 1)], cos_part, sin_part).astype(bf16)
        for i in range(2)
    ]
    spot = lax.broadcasted_iota(jnp.int32, (new, ctx), 1)
    token = lax.broadcasted_iota(jnp.int32, (new, ctx), 0)
    scale = HEAD_DIM ** (-0.5) * math.log2(math.e)
    for r in range(reqs):
        request = order[dev[0] * reqs + r]
        old = olds[request]
        key_rows = keys[:, r].reshape(ctx, GROUP)
        value_rows = place(fresh[r * new : (r + 1) * new], cached[r], news[request], old)
        values[:, r] = value_rows.reshape(parts, depth, GROUP)
        mask = jnp.where(spot <= old + token, 0.0, -jnp.inf)
        bias = jnp.concatenate([mask, mask], axis=0)
        pieces = []
        for k in range(4):
            key = key_rows[:, HEAD_DIM * k : HEAD_DIM * (k + 1)]
            value = value_rows[:, HEAD_DIM * k : HEAD_DIM * (k + 1)]
            pair = []
            for h in (2 * k, 2 * k + 1):
                at = HEAD_DIM * (h % 4)
                pair.append(queries[h // 4][r * new : (r + 1) * new, at : at + HEAD_DIM])
            scores = lax.dot_general(
                jnp.concatenate(pair, axis=0), key, (((1,), (1,)), ((), ())),
                preferred_element_type=f32,
            )
            scores = scores * scale + bias
            exponent = jnp.exp2(scores - jnp.max(scores, axis=-1, keepdims=True))
            bottom = jnp.sum(exponent, axis=-1, keepdims=True)
            mixed = jnp.dot(exponent.astype(bf16), value, preferred_element_type=f32) / bottom
            pieces += [mixed[:new], mixed[new:]]
        attended[r * new : (r + 1) * new, :] = jnp.concatenate(pieces, axis=1).astype(bf16)
    stream(step).wait()
    term = jnp.dot(attended[...], out_weight[step], preferred_element_type=f32)

    @pl.when(step == 0)
    def _():
        total[...] = tokens[...].astype(f32).reshape(flat, width) + term

    @pl.when(step > 0)
    def _():
        total[...] += term

    @pl.when(step == pl.num_programs(0) - 1)
    def _():
        rounded = total[...].astype(bf16)
        residual[...] = rounded
        post[...] = norm_value(rounded.astype(f32), gain[1:2, :])


def mlp_kernel(count, own, other, *refs):
    inputs, outputs, total = refs[:count], refs[count:-1], refs[-1]
    step = pl.program_id(0)
    values = jnp.concatenate([rows[...] for rows in inputs], axis=0)
    term = None
    for weights in (own, other):
        gate = jnp.dot(values, weights[0], preferred_element_type=f32)
        up = jnp.dot(values, weights[1], preferred_element_type=f32)
        hidden = (gate / (1.0 + jnp.exp(-gate)) * up).astype(bf16)
        product = lax.dot_general(
            hidden, weights[2], (((1,), (1,)), ((), ())), preferred_element_type=f32
        )
        term = product if term is None else term + product

    @pl.when(step == 0)
    def _():
        total[...] = term

    @pl.when(step > 0)
    def _():
        total[...] += term

    @pl.when(step == pl.num_programs(0) - 1)
    def _():
        flat = outputs[0].shape[0]
        for i, out in enumerate(outputs):
            out[...] = total[i * flat : (i + 1) * flat].astype(bf16)


def move_rows(pairs, held, arrive, leave):
    inward = [
        pltpu.make_async_copy(source, held.at[i], arrive.at[i])
        for i, (source, _) in enumerate(pairs)
    ]
    outward = [
        pltpu.make_async_copy(held.at[i], target, leave.at[i])
        for i, (_, target) in enumerate(pairs)
    ]
    for copy in inward:
        copy.start()
    for first, second in zip(inward, outward):
        first.wait()
        second.start()
    for copy in outward:
        copy.wait()


def pack_kernel(groups, share, count, passed, picked, group, source, *rest):
    held, arrive, leave = rest[-3:]
    targets = rest[passed : passed + count]
    pairs = []
    for i in range(groups * share):
        if count > 1:
            target = targets[i // share].at[i % share]
        else:
            goal = lax.rem(group[0] + i // share, groups)
            target = targets[0].at[goal * share + i % share]
        pairs.append((source.at[picked[i]], target))
    move_rows(pairs, held, arrive, leave)


def unpack_kernel(columns, groups, share, count, spots, group, *refs):
    sources, (target, held, arrive, leave) = refs[:count], refs[-4:]
    width = sources[0].shape[-1]
    pairs = []
    for i in range(groups * share):
        if count > 1:
            source = sources[i // share].at[i % share]
        else:
            origin = lax.rem(group[0] + groups - i // share, groups)
            source = sources[0].at[origin * share + i % share]
        pairs.append((source, target.at[spots[i], :, pl.ds(columns, width)]))
    move_rows(pairs, held, arrive, leave)


def gate_kernel(*passed):
    pass


def cut_kernel(first, second, *halves):
    middle = first.shape[0] // 2
    halves[0][...] = second[:middle]
    halves[1][...] = first[middle:]


def sum_kernel(order, news, dev, *refs):
    terms, out = refs[:-1], refs[-1]
    request = order[dev[0] * pl.num_programs(0) + pl.program_id(0)]
    total = terms[0][...].astype(f32)
    for term in terms[1:]:
        total = total + term[...].astype(f32)
    token = lax.broadcasted_iota(jnp.int32, total.shape, 0)
    live = token + pl.program_id(1) * total.shape[0] < news[request]
    out[0] = jnp.where(live, total, 0.0).astype(out.dtype)


def call(
    kernel, prefetched, grid, in_specs, out_specs, out_shape, scratch, operands,
    flops=0, moved=6 << 20, aliases={}, after=(),
):
    begin = len(prefetched) + len(operands)

    def ordered(*refs):
        kernel(*refs[:begin], *refs[begin + len(after) :])

    return pl.pallas_call(
        ordered,
        out_shape=out_shape,
        grid_spec=pltpu.PrefetchScalarGridSpec(
            num_scalar_prefetch=len(prefetched),
            grid=grid,
            in_specs=list(in_specs) + [pl.BlockSpec(memory_space=pl.ANY)] * len(after),
            out_specs=out_specs,
            scratch_shapes=scratch,
        ),
        compiler_params=pltpu.CompilerParams(vmem_limit_bytes=VMEM),
        cost_estimate=pl.CostEstimate(flops=flops, bytes_accessed=moved, transcendentals=0),
        input_output_aliases=aliases,
    )(*prefetched, *operands, *after)


def shape(dims, dtype=bf16):
    return jax.ShapeDtypeStruct(dims, dtype)


def whole(dims):
    return pl.BlockSpec(dims, lambda *_: (0,) * len(dims))


def local(
    tokens,
    cached,
    norm_gains,
    w_qkv,
    w_out,
    mlp_weights,
    request_order,
    new_lengths,
    cached_lengths,
    decode_slots,
):
    tensor = ("chip", "core")
    chips, cores = lax.axis_size("chip"), lax.axis_size("core")
    tensor_size = chips * cores
    group_total = lax.axis_size("dp")
    reqs, new, width = tokens.shape
    ctx = cached.shape[1]
    depth = ctx // tensor_size
    flat = reqs * new
    group_reqs = reqs * tensor_size
    group_index = lax.axis_index("dp")
    device = group_index * tensor_size + lax.axis_index(tensor)
    dev = device.astype(jnp.int32).reshape(1)
    key_width = KV_HEADS * HEAD_DIM
    groups = key_width // GROUP
    scalars = (request_order, new_lengths, cached_lengths, dev)
    freq = jnp.asarray(frequencies())

    other_weights = lax.ppermute(mlp_weights, "core", [(0, 1), (1, 0)])

    context_shape = (tensor_size, reqs, depth, key_width)
    context_spec = pl.BlockSpec((tensor_size, reqs, depth, GROUP), lambda g, *_: (0, 0, 0, g))
    table = (reqs, new, GROUP)
    keys, normed, cosine, sine = call(
        key_kernel,
        scalars,
        (groups,),
        [
            whole(tokens.shape),
            whole(norm_gains.shape),
            whole((1, 128)),
            pl.BlockSpec((width, GROUP), lambda g, *_: (0, width // GROUP + g)),
            pl.BlockSpec((reqs, ctx, GROUP), lambda g, *_: (0, 0, g)),
        ],
        [context_spec, whole(tokens.shape), whole(table), whole(table)],
        [shape(context_shape), shape(tokens.shape), shape(table, f32), shape(table, f32)],
        [],
        (tokens, norm_gains, freq, w_qkv, cached),
        2 * flat * width * key_width,
        8 << 20,
    )
    keys_moved = lax.all_to_all(keys, tensor, split_axis=0, concat_axis=0, tiled=True)
    values, residual, post = call(
        attention_kernel,
        scalars,
        (groups,),
        [
            whole(tokens.shape),
            whole(table),
            whole(table),
            pl.BlockSpec((width, 2 * GROUP), lambda g, *_: (0, g)),
            pl.BlockSpec((width, GROUP), lambda g, *_: (0, (width + key_width) // GROUP + g)),
            context_spec,
            pl.BlockSpec((reqs, ctx, GROUP), lambda g, *_: (0, 0, groups + g)),
            whole(tokens.shape),
            whole(norm_gains.shape),
            pl.BlockSpec(memory_space=pl.ANY),
        ],
        [context_spec, whole((flat, width)), whole((flat, width))],
        [shape(context_shape), shape((flat, width)), shape((flat, width))],
        [
            pltpu.VMEM((flat, width), f32),
            pltpu.VMEM((flat, 2 * GROUP), bf16),
            pltpu.VMEM((groups, 2 * GROUP, width), bf16),
            pltpu.SemaphoreType.DMA((groups,)),
        ],
        (normed, cosine, sine, w_qkv, w_qkv, keys, cached, tokens, norm_gains, w_out),
        12 * flat * width * width,
        16 << 20,
    )
    units = mlp_weights.shape[2]
    chunk = 256 if units % 256 == 0 else units

    def mlp(pieces, after, weight=1):
        total_rows = sum(rows.shape[0] for rows in pieces)
        weight_spec = pl.BlockSpec((3, width, chunk), lambda c: (0, 0, c))
        return call(
            functools.partial(mlp_kernel, len(pieces)),
            (),
            (units // chunk,),
            [weight_spec] * 2 + [whole(rows.shape) for rows in pieces],
            [whole((flat, width))] * (total_rows // flat),
            [shape((flat, width))] * (total_rows // flat),
            [pltpu.VMEM((total_rows, width), f32)],
            (mlp_weights, other_weights, *pieces),
            weight * 12 * total_rows * width * units,
            12 * width * units,
            after=after,
        )

    every = request_order.shape[0]
    indices = jnp.arange(every, dtype=jnp.int32)
    slot_of = jnp.sum(
        jnp.where(request_order[:, None] == indices[None, :], decode_slots[None, :], 0), axis=1
    )
    ordinal = jnp.arange(group_reqs, dtype=jnp.int32)

    def inverse(keys_of):
        position = jnp.sum((keys_of[None, :] < keys_of[:, None]).astype(jnp.int32), axis=1)
        return jnp.sum(
            jnp.where(position[None, :] == ordinal[:, None], ordinal[None, :], 0), axis=1
        )

    own_slots = lax.dynamic_slice_in_dim(slot_of, group_index * group_reqs, group_reqs)
    goal = lax.rem(own_slots // group_reqs - group_index + group_total, group_total)
    picked = inverse(goal * group_reqs + lax.rem(own_slots, group_reqs))
    slot_ids = group_index * group_reqs + ordinal
    owners = jnp.sum(
        jnp.where(slot_of[None, :] == slot_ids[:, None], indices[None, :] // group_reqs, 0), axis=1
    )
    origin = lax.rem(group_index - owners + group_total, group_total)
    spots = inverse(origin * group_reqs + ordinal)

    share = group_reqs // group_total
    piece = (share, depth, key_width)
    anywhere = pl.BlockSpec(memory_space=pl.ANY)
    sems = [pltpu.VMEM((group_reqs, depth, key_width), bf16)] + [
        pltpu.SemaphoreType.DMA((group_reqs,))
    ] * 2
    shifts = [
        [(g, (g + s) % group_total) for g in range(group_total)] for s in range(1, group_total)
    ]

    group = group_index.astype(jnp.int32).reshape(1)

    def pack(moved, targets, passed, after):
        return call(
            functools.partial(pack_kernel, group_total, share, len(targets), len(passed)),
            (picked, group), (1,),
            [anywhere] * (1 + len(passed)), [anywhere] * (len(targets) + len(passed)),
            [shape(dims) for dims in targets] + [shape(rows.shape) for rows in passed], sems,
            (moved.reshape(group_reqs, depth, key_width), *passed),
            aliases={3 + i: len(targets) + i for i in range(len(passed))}, after=after,
        )

    def unpack(columns, arrived, target, after, flops=0):
        return call(
            functools.partial(unpack_kernel, columns, group_total, share, len(arrived)),
            (spots, group), (1,), [anywhere] * (len(arrived) + len(target)), anywhere,
            shape((group_reqs, depth, 2 * key_width)), sems, (*arrived, *target), flops,
            aliases={2 + len(arrived): 0} if target else {}, after=after,
        )

    def swap(rows, mask):
        return lax.ppermute(rows, "chip", [(c, c ^ mask) for c in range(chips)])

    masks = [1, 2] if chips == 4 else range(1, chips)
    gathered = [swap(post, mask) for mask in masks]
    *keys_packed, values = pack(
        keys_moved, [piece] * group_total, (values,), (post, other_weights)
    )
    values_moved = lax.all_to_all(values, tensor, split_axis=0, concat_axis=0, tiled=True)
    keys_arrived = [keys_packed[0]] + [
        lax.ppermute(rows, "dp", pairs) for rows, pairs in zip(keys_packed[1:], shifts)
    ]
    latest = keys_packed[0]
    if chips == 4:
        half = (flat // 2, width)
        first, second = call(
            cut_kernel, (), (1,), [whole((flat, width))] * 2, [whole(half)] * 2,
            [shape(half)] * 2, [], tuple(gathered), after=(latest,),
        )
        latest = first
        batches = [([1, 2], gathered), ([3], [swap(first, 1), swap(second, 2)])]
    else:
        batches = [([mask], [rows]) for mask, rows in zip(masks, gathered)]
    partials = list(mlp([post], (latest, spots), LONG))
    values_packed = pack(
        values_moved, [(group_reqs, depth, key_width)], (), (partials[0],)
    )[0]
    latest = values_packed
    pair = mlp(batches[0][1], (latest, *(rows for batch in batches[1:2] for rows in batch[1])))
    latest = pair[0]
    values_ready, *pair = call(
        gate_kernel, (), (1,), [anywhere] * (1 + len(pair)), [anywhere] * (1 + len(pair)),
        [shape(rows.shape) for rows in (values_packed, *pair)], [], (values_packed, *pair),
        moved=1 << 10, aliases={i: i for i in range(1 + len(pair))}, after=tuple(keys_arrived[1:]),
    )
    values_arrived = lax.all_to_all(values_ready, "dp", split_axis=0, concat_axis=0, tiled=True)
    latest = values_ready
    for i, (batch_masks, pieces) in enumerate(batches):
        results = mlp(pieces, (latest,)) if i else pair
        latest = results[0] if i else latest
        partials += [swap(rows, mask) for mask, rows in zip(batch_masks, results)]

    kv_half = unpack(0, keys_arrived, (), (latest,))

    def add(terms, out_shape, after, flops):
        return call(
            sum_kernel, (request_order, new_lengths, dev), (reqs, 2),
            [pl.BlockSpec((new // 2, width), lambda r, h, *_: (2 * r + h, 0))] * len(terms),
            pl.BlockSpec((1, new // 2, width), lambda r, h, *_: (r, h, 0)),
            out_shape, [], tuple(terms), flops, after=after,
        )

    kv_decode = unpack(
        key_width, [values_arrived], (kv_half,), tuple(partials[1:2]), LONG * flat * width * width * 8
    )
    layer_out = add([residual, *partials], shape(tokens.shape), (kv_decode,), 0)
    return (layer_out, kv_decode)


def solution(mesh):
    in_specs = (
        P(("dp", "chip", "core"), None, None),
        P(("dp", "chip", "core"), None, None),
        P(),
        P(),
        P(),
        P(None, None, ("chip", "core")),
        P(),
        P(),
        P(),
        P(),
    )
    out_specs = (P(("dp", "chip", "core"), None, None), P("dp", ("chip", "core"), None))
    devices = mesh.devices.reshape(mesh.devices.shape[0], -1, 2)
    mesh = jax.sharding.Mesh(devices, ("dp", "chip", "core"))
    return jax.shard_map(local, mesh=mesh, in_specs=in_specs, out_specs=out_specs, check_vma=False)
```

```python
import functools
import math

import jax
import jax.numpy as jnp
import numpy as np
from jax import lax
from jax.experimental import pallas as pl
from jax.experimental.pallas import tpu as pltpu
from jax.sharding import PartitionSpec as P

HEADS = 16
KV_HEADS = 8
HEAD_DIM = 96
GROUP = 384
VMEM = 60 * 1024 * 1024
LONG = 40

epsilon = 1e-05
rope_base = 100000.0
bf16 = jnp.bfloat16
f32 = jnp.float32


def frequencies():
    half = HEAD_DIM // 2
    steps = np.arange(half, dtype=np.float32)
    frequency = np.float32(rope_base) ** (np.float32(-2.0) * steps / np.float32(HEAD_DIM))
    row = np.zeros((1, 128), np.float32)
    row[0, :half] = frequency
    row[0, half:HEAD_DIM] = frequency
    return row


def norm_value(values, gain):
    factor = lax.rsqrt(jnp.mean(values * values, axis=-1, keepdims=True) + epsilon)
    return (values * factor * gain).astype(bf16)


def rotate(values, cosine, sine):
    width = values.shape[-1]
    half = HEAD_DIM // 2
    lane = lax.broadcasted_iota(jnp.int32, values.shape, 1)
    first = lax.rem(lane, HEAD_DIM) < half
    swapped = jnp.where(
        first, pltpu.roll(values, width - half, 1), pltpu.roll(values, half, 1)
    )
    return values * cosine + swapped * sine


def place(fresh, cached, new_count, cached_count):
    rows, new = cached.shape[0], fresh.shape[0]
    spot = lax.broadcasted_iota(jnp.int32, (rows, new), 0)
    token = lax.broadcasted_iota(jnp.int32, (rows, new), 1)
    chosen = (spot - cached_count == token) & (token < new_count)
    placed = jnp.dot(jnp.where(chosen, 1.0, 0.0).astype(bf16), fresh, preferred_element_type=f32)
    keep = lax.broadcasted_iota(jnp.int32, cached.shape, 0) < cached_count
    return jnp.where(keep, cached.astype(f32), placed).astype(bf16)


def key_kernel(
    order, news, olds, dev, tokens, gain, freq, weight, cached, context, normed, cosine, sine
):
    reqs, new, width = tokens.shape

    @pl.when(pl.program_id(0) == 0)
    def _():
        lane = lax.broadcasted_iota(jnp.int32, (new, 128), 1)
        row = lax.broadcasted_iota(jnp.int32, (new, 128), 0)
        sign = jnp.where(lane < HEAD_DIM // 2, -1.0, 1.0)
        for r in range(reqs):
            normed[r] = norm_value(tokens[r].astype(f32), gain[0:1, :])
            old = olds[order[dev[0] * reqs + r]]
            angles = (row + old).astype(f32) * freq[...]
            cos_part = jnp.cos(angles)[:, :HEAD_DIM]
            sin_part = (jnp.sin(angles) * sign)[:, :HEAD_DIM]
            cosine[r] = jnp.concatenate([cos_part] * 4, axis=1)
            sine[r] = jnp.concatenate([sin_part] * 4, axis=1)

    rows = normed[...].reshape(reqs * new, width)
    projected = jnp.dot(rows, weight[...], preferred_element_type=f32)
    turned = rotate(
        projected,
        cosine[...].reshape(reqs * new, GROUP),
        sine[...].reshape(reqs * new, GROUP),
    ).astype(bf16)
    parts, _, depth, _ = context.shape
    for r in range(reqs):
        request = order[dev[0] * reqs + r]
        merged = place(turned[r * new : (r + 1) * new], cached[r], news[request], olds[request])
        context[:, r] = merged.reshape(parts, depth, GROUP)


def attention_kernel(
    order, news, olds, dev, normed, cosine, sine, weight, w_value, keys, cached, tokens, gain, w_out,
    values, residual, post, total, attended, out_weight, sems,
):
    step = pl.program_id(0)
    reqs, new, width = normed.shape
    parts, _, depth, _ = keys.shape
    ctx = parts * depth
    flat = reqs * new

    def stream(g):
        source = w_out.at[pl.ds(g * 2 * GROUP, 2 * GROUP)]
        return pltpu.make_async_copy(source, out_weight.at[g], sems.at[g])

    @pl.when(step == 0)
    def _():
        for g in range(out_weight.shape[0]):
            stream(g).start()

    rows = normed[...].reshape(flat, width)
    fresh = jnp.dot(rows, w_value[...], preferred_element_type=f32).astype(bf16)
    projected = jnp.dot(rows, weight[...], preferred_element_type=f32)
    cos_part = cosine[...].reshape(flat, GROUP)
    sin_part = sine[...].reshape(flat, GROUP)
    queries = [
        rotate(projected[:, GROUP * i : GROUP * (i + 1)], cos_part, sin_part).astype(bf16)
        for i in range(2)
    ]
    spot = lax.broadcasted_iota(jnp.int32, (new, ctx), 1)
    token = lax.broadcasted_iota(jnp.int32, (new, ctx), 0)
    scale = HEAD_DIM ** (-0.5) * math.log2(math.e)
    for r in range(reqs):
        request = order[dev[0] * reqs + r]
        old = olds[request]
        key_rows = keys[:, r].reshape(ctx, GROUP)
        value_rows = place(fresh[r * new : (r + 1) * new], cached[r], news[request], old)
        values[:, r] = value_rows.reshape(parts, depth, GROUP)
        mask = jnp.where(spot <= old + token, 0.0, -jnp.inf)
        bias = jnp.concatenate([mask, mask], axis=0)
        pieces = []
        for k in range(4):
            key = key_rows[:, HEAD_DIM * k : HEAD_DIM * (k + 1)]
            value = value_rows[:, HEAD_DIM * k : HEAD_DIM * (k + 1)]
            pair = []
            for h in (2 * k, 2 * k + 1):
                at = HEAD_DIM * (h % 4)
                pair.append(queries[h // 4][r * new : (r + 1) * new, at : at + HEAD_DIM])
            scores = lax.dot_general(
                jnp.concatenate(pair, axis=0), key, (((1,), (1,)), ((), ())),
                preferred_element_type=f32,
            )
            scores = scores * scale + bias
            exponent = jnp.exp2(scores - jnp.max(scores, axis=-1, keepdims=True))
            bottom = jnp.sum(exponent, axis=-1, keepdims=True)
            mixed = jnp.dot(exponent.astype(bf16), value, preferred_element_type=f32) / bottom
            pieces += [mixed[:new], mixed[new:]]
        attended[r * new : (r + 1) * new, :] = jnp.concatenate(pieces, axis=1).astype(bf16)
    stream(step).wait()
    term = jnp.dot(attended[...], out_weight[step], preferred_element_type=f32)

    @pl.when(step == 0)
    def _():
        total[...] = tokens[...].astype(f32).reshape(flat, width) + term

    @pl.when(step > 0)
    def _():
        total[...] += term

    @pl.when(step == pl.num_programs(0) - 1)
    def _():
        rounded = total[...].astype(bf16)
        residual[...] = rounded
        post[...] = norm_value(rounded.astype(f32), gain[1:2, :])


def mlp_kernel(count, own, other, *refs):
    inputs, outputs, total = refs[:count], refs[count:-1], refs[-1]
    step = pl.program_id(0)
    values = jnp.concatenate([rows[...] for rows in inputs], axis=0)
    term = None
    for weights in (own, other):
        gate = jnp.dot(values, weights[0], preferred_element_type=f32)
        up = jnp.dot(values, weights[1], preferred_element_type=f32)
        hidden = (gate / (1.0 + jnp.exp(-gate)) * up).astype(bf16)
        product = lax.dot_general(
            hidden, weights[2], (((1,), (1,)), ((), ())), preferred_element_type=f32
        )
        term = product if term is None else term + product

    @pl.when(step == 0)
    def _():
        total[...] = term

    @pl.when(step > 0)
    def _():
        total[...] += term

    @pl.when(step == pl.num_programs(0) - 1)
    def _():
        flat = outputs[0].shape[0]
        for i, out in enumerate(outputs):
            out[...] = total[i * flat : (i + 1) * flat].astype(bf16)


def move_rows(pairs, held, arrive, leave):
    inward = [
        pltpu.make_async_copy(source, held.at[i], arrive.at[i])
        for i, (source, _) in enumerate(pairs)
    ]
    outward = [
        pltpu.make_async_copy(held.at[i], target, leave.at[i])
        for i, (_, target) in enumerate(pairs)
    ]
    for copy in inward:
        copy.start()
    for first, second in zip(inward, outward):
        first.wait()
        second.start()
    for copy in outward:
        copy.wait()


def pack_kernel(groups, share, count, passed, picked, group, source, *rest):
    held, arrive, leave = rest[-3:]
    targets = rest[passed : passed + count]
    pairs = []
    for i in range(groups * share):
        if count > 1:
            target = targets[i // share].at[i % share]
        else:
            goal = lax.rem(group[0] + i // share, groups)
            target = targets[0].at[goal * share + i % share]
        pairs.append((source.at[picked[i]], target))
    move_rows(pairs, held, arrive, leave)


def unpack_kernel(columns, groups, share, count, spots, group, *refs):
    sources, (target, held, arrive, leave) = refs[:count], refs[-4:]
    width = sources[0].shape[-1]
    pairs = []
    for i in range(groups * share):
        if count > 1:
            source = sources[i // share].at[i % share]
        else:
            origin = lax.rem(group[0] + groups - i // share, groups)
            source = sources[0].at[origin * share + i % share]
        pairs.append((source, target.at[spots[i], :, pl.ds(columns, width)]))
    move_rows(pairs, held, arrive, leave)


def gate_kernel(*passed):
    pass


def cut_kernel(first, second, *halves):
    middle = first.shape[0] // 2
    halves[0][...] = second[:middle]
    halves[1][...] = first[middle:]


def sum_kernel(order, news, dev, *refs):
    terms, out = refs[:-1], refs[-1]
    request = order[dev[0] * pl.num_programs(0) + pl.program_id(0)]
    total = terms[0][...].astype(f32)
    for term in terms[1:]:
        total = total + term[...].astype(f32)
    live = lax.broadcasted_iota(jnp.int32, total.shape, 0) < news[request]
    out[0] = jnp.where(live, total, 0.0).astype(out.dtype)


def call(
    kernel, prefetched, grid, in_specs, out_specs, out_shape, scratch, operands,
    flops=0, moved=6 << 20, aliases={}, after=(), vmem=VMEM,
):
    begin = len(prefetched) + len(operands)

    def ordered(*refs):
        kernel(*refs[:begin], *refs[begin + len(after) :])

    return pl.pallas_call(
        ordered,
        out_shape=out_shape,
        grid_spec=pltpu.PrefetchScalarGridSpec(
            num_scalar_prefetch=len(prefetched),
            grid=grid,
            in_specs=list(in_specs) + [pl.BlockSpec(memory_space=pl.ANY)] * len(after),
            out_specs=out_specs,
            scratch_shapes=scratch,
        ),
        compiler_params=pltpu.CompilerParams(vmem_limit_bytes=vmem),
        cost_estimate=pl.CostEstimate(flops=flops, bytes_accessed=moved, transcendentals=0),
        input_output_aliases=aliases,
    )(*prefetched, *operands, *after)


def shape(dims, dtype=bf16):
    return jax.ShapeDtypeStruct(dims, dtype)


def whole(dims):
    return pl.BlockSpec(dims, lambda *_: (0,) * len(dims))


def local(
    tokens,
    cached,
    norm_gains,
    w_qkv,
    w_out,
    mlp_weights,
    request_order,
    new_lengths,
    cached_lengths,
    decode_slots,
):
    tensor = ("chip", "core")
    chips, cores = lax.axis_size("chip"), lax.axis_size("core")
    tensor_size = chips * cores
    group_total = lax.axis_size("dp")
    reqs, new, width = tokens.shape
    ctx = cached.shape[1]
    depth = ctx // tensor_size
    flat = reqs * new
    group_reqs = reqs * tensor_size
    group_index = lax.axis_index("dp")
    device = group_index * tensor_size + lax.axis_index(tensor)
    dev = device.astype(jnp.int32).reshape(1)
    key_width = KV_HEADS * HEAD_DIM
    groups = key_width // GROUP
    scalars = (request_order, new_lengths, cached_lengths, dev)
    freq = jnp.asarray(frequencies())

    other_weights = lax.ppermute(mlp_weights, "core", [(0, 1), (1, 0)])

    context_shape = (tensor_size, reqs, depth, key_width)
    context_spec = pl.BlockSpec((tensor_size, reqs, depth, GROUP), lambda g, *_: (0, 0, 0, g))
    table = (reqs, new, GROUP)
    keys, normed, cosine, sine = call(
        key_kernel,
        scalars,
        (groups,),
        [
            whole(tokens.shape),
            whole(norm_gains.shape),
            whole((1, 128)),
            pl.BlockSpec((width, GROUP), lambda g, *_: (0, width // GROUP + g)),
            pl.BlockSpec((reqs, ctx, GROUP), lambda g, *_: (0, 0, g)),
        ],
        [context_spec, whole(tokens.shape), whole(table), whole(table)],
        [shape(context_shape), shape(tokens.shape), shape(table, f32), shape(table, f32)],
        [],
        (tokens, norm_gains, freq, w_qkv, cached),
        2 * flat * width * key_width,
        8 << 20,
    )
    keys_moved = lax.all_to_all(keys, tensor, split_axis=0, concat_axis=0, tiled=True)
    values, residual, post = call(
        attention_kernel,
        scalars,
        (groups,),
        [
            whole(tokens.shape),
            whole(table),
            whole(table),
            pl.BlockSpec((width, 2 * GROUP), lambda g, *_: (0, g)),
            pl.BlockSpec((width, GROUP), lambda g, *_: (0, (width + key_width) // GROUP + g)),
            context_spec,
            pl.BlockSpec((reqs, ctx, GROUP), lambda g, *_: (0, 0, groups + g)),
            whole(tokens.shape),
            whole(norm_gains.shape),
            pl.BlockSpec(memory_space=pl.ANY),
        ],
        [context_spec, whole((flat, width)), whole((flat, width))],
        [shape(context_shape), shape((flat, width)), shape((flat, width))],
        [
            pltpu.VMEM((flat, width), f32),
            pltpu.VMEM((flat, 2 * GROUP), bf16),
            pltpu.VMEM((groups, 2 * GROUP, width), bf16),
            pltpu.SemaphoreType.DMA((groups,)),
        ],
        (normed, cosine, sine, w_qkv, w_qkv, keys, cached, tokens, norm_gains, w_out),
        12 * flat * width * width,
        16 << 20,
    )
    units = mlp_weights.shape[2]
    chunk = 256 if units % 256 == 0 else units

    def mlp(pieces, after, weight=1):
        total_rows = sum(rows.shape[0] for rows in pieces)
        weight_spec = pl.BlockSpec((3, width, chunk), lambda c: (0, 0, c))
        return call(
            functools.partial(mlp_kernel, len(pieces)),
            (),
            (units // chunk,),
            [weight_spec] * 2 + [whole(rows.shape) for rows in pieces],
            [whole((flat, width))] * (total_rows // flat),
            [shape((flat, width))] * (total_rows // flat),
            [pltpu.VMEM((total_rows, width), f32)],
            (mlp_weights, other_weights, *pieces),
            weight * 12 * total_rows * width * units,
            12 * width * units,
            after=after,
        )

    every = request_order.shape[0]
    indices = jnp.arange(every, dtype=jnp.int32)
    slot_of = jnp.sum(
        jnp.where(request_order[:, None] == indices[None, :], decode_slots[None, :], 0), axis=1
    )
    ordinal = jnp.arange(group_reqs, dtype=jnp.int32)

    def inverse(keys_of):
        position = jnp.sum((keys_of[None, :] < keys_of[:, None]).astype(jnp.int32), axis=1)
        return jnp.sum(
            jnp.where(position[None, :] == ordinal[:, None], ordinal[None, :], 0), axis=1
        )

    own_slots = lax.dynamic_slice_in_dim(slot_of, group_index * group_reqs, group_reqs)
    goal = lax.rem(own_slots // group_reqs - group_index + group_total, group_total)
    picked = inverse(goal * group_reqs + lax.rem(own_slots, group_reqs))
    slot_ids = group_index * group_reqs + ordinal
    owners = jnp.sum(
        jnp.where(slot_of[None, :] == slot_ids[:, None], indices[None, :] // group_reqs, 0), axis=1
    )
    origin = lax.rem(group_index - owners + group_total, group_total)
    spots = inverse(origin * group_reqs + ordinal)

    share = group_reqs // group_total
    piece = (share, depth, key_width)
    anywhere = pl.BlockSpec(memory_space=pl.ANY)
    sems = [pltpu.VMEM((group_reqs, depth, key_width), bf16)] + [
        pltpu.SemaphoreType.DMA((group_reqs,))
    ] * 2
    shifts = [
        [(g, (g + s) % group_total) for g in range(group_total)] for s in range(1, group_total)
    ]

    group = group_index.astype(jnp.int32).reshape(1)

    def pack(moved, targets, passed, after):
        return call(
            functools.partial(pack_kernel, group_total, share, len(targets), len(passed)),
            (picked, group), (1,),
            [anywhere] * (1 + len(passed)), [anywhere] * (len(targets) + len(passed)),
            [shape(dims) for dims in targets] + [shape(rows.shape) for rows in passed], sems,
            (moved.reshape(group_reqs, depth, key_width), *passed),
            aliases={3 + i: len(targets) + i for i in range(len(passed))}, after=after,
        )

    def unpack(columns, arrived, target, after, flops=0):
        return call(
            functools.partial(unpack_kernel, columns, group_total, share, len(arrived)),
            (spots, group), (1,), [anywhere] * (len(arrived) + len(target)), anywhere,
            shape((group_reqs, depth, 2 * key_width)), sems, (*arrived, *target), flops,
            aliases={2 + len(arrived): 0} if target else {}, after=after,
            vmem=VMEM // 8 if target else VMEM,
        )

    def swap(rows, mask):
        return lax.ppermute(rows, "chip", [(c, c ^ mask) for c in range(chips)])

    masks = [1, 2] if chips == 4 else range(1, chips)
    gathered = [swap(post, mask) for mask in masks]
    *keys_packed, values = pack(
        keys_moved, [piece] * group_total, (values,), (post, other_weights)
    )
    values_moved = lax.all_to_all(values, tensor, split_axis=0, concat_axis=0, tiled=True)
    keys_arrived = [keys_packed[0]] + [
        lax.ppermute(rows, "dp", pairs) for rows, pairs in zip(keys_packed[1:], shifts)
    ]
    latest = keys_packed[0]
    if chips == 4:
        half = (flat // 2, width)
        first, second = call(
            cut_kernel, (), (1,), [whole((flat, width))] * 2, [whole(half)] * 2,
            [shape(half)] * 2, [], tuple(gathered), after=(latest,),
        )
        latest = first
        batches = [([1, 2], gathered), ([3], [swap(first, 1), swap(second, 2)])]
    else:
        batches = [([mask], [rows]) for mask, rows in zip(masks, gathered)]
    partials = list(mlp([post], (latest, spots), LONG))
    values_packed = pack(
        values_moved, [(group_reqs, depth, key_width)], (), (partials[0],)
    )[0]
    latest = values_packed
    pair = mlp(batches[0][1], (latest, *(rows for batch in batches[1:2] for rows in batch[1])))
    latest = pair[0]
    values_ready, *pair = call(
        gate_kernel, (), (1,), [anywhere] * (1 + len(pair)), [anywhere] * (1 + len(pair)),
        [shape(rows.shape) for rows in (values_packed, *pair)], [], (values_packed, *pair),
        moved=1 << 10, aliases={i: i for i in range(1 + len(pair))}, after=tuple(keys_arrived[1:]),
    )
    values_arrived = lax.all_to_all(values_ready, "dp", split_axis=0, concat_axis=0, tiled=True)
    latest = values_ready
    for i, (batch_masks, pieces) in enumerate(batches):
        results = mlp(pieces, (latest,)) if i else pair
        latest = results[0] if i else latest
        partials += [swap(rows, mask) for mask, rows in zip(batch_masks, results)]

    kv_half = unpack(0, keys_arrived, (), (latest,))

    def add(terms, out_shape, after, flops):
        return call(
            sum_kernel, (request_order, new_lengths, dev), (reqs,),
            [pl.BlockSpec((new, width), lambda r, *_: (r, 0))] * len(terms),
            pl.BlockSpec((1, new, width), lambda r, *_: (r, 0, 0)),
            out_shape, [], tuple(terms), flops, after=after,
        )

    kv_decode = unpack(
        key_width, [values_arrived], (kv_half,), tuple(partials[1:2]), LONG * flat * width * width * 8
    )
    layer_out = add([residual, *partials], shape(tokens.shape), (kv_decode,), 0)
    return (layer_out, kv_decode)


def solution(mesh):
    in_specs = (
        P(("dp", "chip", "core"), None, None),
        P(("dp", "chip", "core"), None, None),
        P(),
        P(),
        P(),
        P(None, None, ("chip", "core")),
        P(),
        P(),
        P(),
        P(),
    )
    out_specs = (P(("dp", "chip", "core"), None, None), P("dp", ("chip", "core"), None))
    devices = mesh.devices.reshape(mesh.devices.shape[0], -1, 2)
    mesh = jax.sharding.Mesh(devices, ("dp", "chip", "core"))
    return jax.shard_map(local, mesh=mesh, in_specs=in_specs, out_specs=out_specs, check_vma=False)
```

```python
import functools
import math

import jax
import jax.numpy as jnp
import numpy as np
from jax import lax
from jax.experimental import pallas as pl
from jax.experimental.pallas import tpu as pltpu
from jax.sharding import PartitionSpec as P

HEADS = 16
KV_HEADS = 8
HEAD_DIM = 96
GROUP = 384
VMEM = 60 * 1024 * 1024
LONG = 40

epsilon = 1e-05
rope_base = 100000.0
bf16 = jnp.bfloat16
f32 = jnp.float32


def frequencies():
    half = HEAD_DIM // 2
    steps = np.arange(half, dtype=np.float32)
    frequency = np.float32(rope_base) ** (np.float32(-2.0) * steps / np.float32(HEAD_DIM))
    row = np.zeros((1, 128), np.float32)
    row[0, :half] = frequency
    row[0, half:HEAD_DIM] = frequency
    return row


def norm_value(values, gain):
    factor = lax.rsqrt(jnp.mean(values * values, axis=-1, keepdims=True) + epsilon)
    return (values * factor * gain).astype(bf16)


def rotate(values, cosine, sine):
    width = values.shape[-1]
    half = HEAD_DIM // 2
    lane = lax.broadcasted_iota(jnp.int32, values.shape, 1)
    first = lax.rem(lane, HEAD_DIM) < half
    swapped = jnp.where(
        first, pltpu.roll(values, width - half, 1), pltpu.roll(values, half, 1)
    )
    return values * cosine + swapped * sine


def place(fresh, cached, new_count, cached_count):
    rows, new = cached.shape[0], fresh.shape[0]
    spot = lax.broadcasted_iota(jnp.int32, (rows, new), 0)
    token = lax.broadcasted_iota(jnp.int32, (rows, new), 1)
    chosen = (spot - cached_count == token) & (token < new_count)
    placed = jnp.dot(jnp.where(chosen, 1.0, 0.0).astype(bf16), fresh, preferred_element_type=f32)
    keep = lax.broadcasted_iota(jnp.int32, cached.shape, 0) < cached_count
    return jnp.where(keep, cached.astype(f32), placed).astype(bf16)


def key_kernel(
    order, news, olds, dev, tokens, gain, freq, weight, cached, context, normed, cosine, sine
):
    reqs, new, width = tokens.shape

    @pl.when(pl.program_id(0) == 0)
    def _():
        lane = lax.broadcasted_iota(jnp.int32, (new, 128), 1)
        row = lax.broadcasted_iota(jnp.int32, (new, 128), 0)
        sign = jnp.where(lane < HEAD_DIM // 2, -1.0, 1.0)
        for r in range(reqs):
            normed[r] = norm_value(tokens[r].astype(f32), gain[0:1, :])
            old = olds[order[dev[0] * reqs + r]]
            angles = (row + old).astype(f32) * freq[...]
            cos_part = jnp.cos(angles)[:, :HEAD_DIM]
            sin_part = (jnp.sin(angles) * sign)[:, :HEAD_DIM]
            cosine[r] = jnp.concatenate([cos_part] * 4, axis=1)
            sine[r] = jnp.concatenate([sin_part] * 4, axis=1)

    rows = normed[...].reshape(reqs * new, width)
    projected = jnp.dot(rows, weight[...], preferred_element_type=f32)
    turned = rotate(
        projected,
        cosine[...].reshape(reqs * new, GROUP),
        sine[...].reshape(reqs * new, GROUP),
    ).astype(bf16)
    parts, _, depth, _ = context.shape
    for r in range(reqs):
        request = order[dev[0] * reqs + r]
        merged = place(turned[r * new : (r + 1) * new], cached[r], news[request], olds[request])
        context[:, r] = merged.reshape(parts, depth, GROUP)


def attention_kernel(
    order, news, olds, dev, normed, cosine, sine, weight, w_value, keys, cached, tokens, gain, w_out,
    values, residual, post, total, attended, out_weight, sems,
):
    step = pl.program_id(0)
    reqs, new, width = normed.shape
    parts, _, depth, _ = keys.shape
    ctx = parts * depth
    flat = reqs * new

    def stream(g):
        source = w_out.at[pl.ds(g * 2 * GROUP, 2 * GROUP)]
        return pltpu.make_async_copy(source, out_weight.at[g], sems.at[g])

    @pl.when(step == 0)
    def _():
        for g in range(out_weight.shape[0]):
            stream(g).start()

    rows = normed[...].reshape(flat, width)
    fresh = jnp.dot(rows, w_value[...], preferred_element_type=f32).astype(bf16)
    projected = jnp.dot(rows, weight[...], preferred_element_type=f32)
    cos_part = cosine[...].reshape(flat, GROUP)
    sin_part = sine[...].reshape(flat, GROUP)
    queries = [
        rotate(projected[:, GROUP * i : GROUP * (i + 1)], cos_part, sin_part).astype(bf16)
        for i in range(2)
    ]
    spot = lax.broadcasted_iota(jnp.int32, (new, ctx), 1)
    token = lax.broadcasted_iota(jnp.int32, (new, ctx), 0)
    scale = HEAD_DIM ** (-0.5) * math.log2(math.e)
    for r in range(reqs):
        request = order[dev[0] * reqs + r]
        old = olds[request]
        key_rows = keys[:, r].reshape(ctx, GROUP)
        value_rows = place(fresh[r * new : (r + 1) * new], cached[r], news[request], old)
        values[:, r] = value_rows.reshape(parts, depth, GROUP)
        mask = jnp.where(spot <= old + token, 0.0, -jnp.inf)
        bias = jnp.concatenate([mask, mask], axis=0)
        pieces = []
        for k in range(4):
            key = key_rows[:, HEAD_DIM * k : HEAD_DIM * (k + 1)]
            value = value_rows[:, HEAD_DIM * k : HEAD_DIM * (k + 1)]
            pair = []
            for h in (2 * k, 2 * k + 1):
                at = HEAD_DIM * (h % 4)
                pair.append(queries[h // 4][r * new : (r + 1) * new, at : at + HEAD_DIM])
            scores = lax.dot_general(
                jnp.concatenate(pair, axis=0), key, (((1,), (1,)), ((), ())),
                preferred_element_type=f32,
            )
            scores = scores * scale + bias
            exponent = jnp.exp2(scores - jnp.max(scores, axis=-1, keepdims=True))
            bottom = jnp.sum(exponent, axis=-1, keepdims=True)
            mixed = jnp.dot(exponent.astype(bf16), value, preferred_element_type=f32) / bottom
            pieces += [mixed[:new], mixed[new:]]
        attended[r * new : (r + 1) * new, :] = jnp.concatenate(pieces, axis=1).astype(bf16)
    stream(step).wait()
    term = jnp.dot(attended[...], out_weight[step], preferred_element_type=f32)

    @pl.when(step == 0)
    def _():
        total[...] = tokens[...].astype(f32).reshape(flat, width) + term

    @pl.when(step > 0)
    def _():
        total[...] += term

    @pl.when(step == pl.num_programs(0) - 1)
    def _():
        rounded = total[...].astype(bf16)
        residual[...] = rounded
        post[...] = norm_value(rounded.astype(f32), gain[1:2, :])


def mlp_kernel(count, own, other, *refs):
    inputs, outputs, total = refs[:count], refs[count:-1], refs[-1]
    step = pl.program_id(0)
    values = jnp.concatenate([rows[...] for rows in inputs], axis=0)
    term = None
    for weights in (own, other):
        gate = jnp.dot(values, weights[0], preferred_element_type=f32)
        up = jnp.dot(values, weights[1], preferred_element_type=f32)
        hidden = (gate / (1.0 + jnp.exp(-gate)) * up).astype(bf16)
        product = lax.dot_general(
            hidden, weights[2], (((1,), (1,)), ((), ())), preferred_element_type=f32
        )
        term = product if term is None else term + product

    @pl.when(step == 0)
    def _():
        total[...] = term

    @pl.when(step > 0)
    def _():
        total[...] += term

    @pl.when(step == pl.num_programs(0) - 1)
    def _():
        flat = outputs[0].shape[0]
        for i, out in enumerate(outputs):
            out[...] = total[i * flat : (i + 1) * flat].astype(bf16)


def move_rows(pairs, held, arrive, leave):
    inward = [
        pltpu.make_async_copy(source, held.at[i], arrive.at[i])
        for i, (source, _) in enumerate(pairs)
    ]
    outward = [
        pltpu.make_async_copy(held.at[i], target, leave.at[i])
        for i, (_, target) in enumerate(pairs)
    ]
    for copy in inward:
        copy.start()
    for first, second in zip(inward, outward):
        first.wait()
        second.start()
    for copy in outward:
        copy.wait()


def pack_kernel(groups, share, count, passed, picked, group, source, *rest):
    held, arrive, leave = rest[-3:]
    targets = rest[passed : passed + count]
    pairs = []
    for i in range(groups * share):
        if count > 1:
            target = targets[i // share].at[i % share]
        else:
            goal = lax.rem(group[0] + i // share, groups)
            target = targets[0].at[goal * share + i % share]
        pairs.append((source.at[picked[i]], target))
    move_rows(pairs, held, arrive, leave)


def unpack_kernel(columns, groups, share, count, spots, group, *refs):
    sources, (target, held, arrive, leave) = refs[:count], refs[-4:]
    width = sources[0].shape[-1]
    pairs = []
    for i in range(groups * share):
        if count > 1:
            source = sources[i // share].at[i % share]
        else:
            origin = lax.rem(group[0] + groups - i // share, groups)
            source = sources[0].at[origin * share + i % share]
        pairs.append((source, target.at[spots[i], :, pl.ds(columns, width)]))
    move_rows(pairs, held, arrive, leave)


def gate_kernel(*passed):
    pass


def cut_kernel(first, second, *halves):
    middle = first.shape[0] // 2
    halves[0][...] = second[:middle]
    halves[1][...] = first[middle:]


def sum_kernel(order, news, dev, *refs):
    terms, out = refs[:-1], refs[-1]
    request = order[dev[0] * pl.num_programs(0) + pl.program_id(0)]
    total = terms[0][...].astype(f32)
    for term in terms[1:]:
        total = total + term[...].astype(f32)
    live = lax.broadcasted_iota(jnp.int32, total.shape, 0) < news[request]
    out[0] = jnp.where(live, total, 0.0).astype(out.dtype)


def call(
    kernel, prefetched, grid, in_specs, out_specs, out_shape, scratch, operands,
    flops=0, moved=6 << 20, aliases={}, after=(), vmem=VMEM,
):
    begin = len(prefetched) + len(operands)

    def ordered(*refs):
        kernel(*refs[:begin], *refs[begin + len(after) :])

    return pl.pallas_call(
        ordered,
        out_shape=out_shape,
        grid_spec=pltpu.PrefetchScalarGridSpec(
            num_scalar_prefetch=len(prefetched),
            grid=grid,
            in_specs=list(in_specs) + [pl.BlockSpec(memory_space=pl.ANY)] * len(after),
            out_specs=out_specs,
            scratch_shapes=scratch,
        ),
        compiler_params=pltpu.CompilerParams(vmem_limit_bytes=vmem),
        cost_estimate=pl.CostEstimate(flops=flops, bytes_accessed=moved, transcendentals=0),
        input_output_aliases=aliases,
    )(*prefetched, *operands, *after)


def shape(dims, dtype=bf16):
    return jax.ShapeDtypeStruct(dims, dtype)


def whole(dims):
    return pl.BlockSpec(dims, lambda *_: (0,) * len(dims))


def local(
    tokens,
    cached,
    norm_gains,
    w_qkv,
    w_out,
    mlp_weights,
    request_order,
    new_lengths,
    cached_lengths,
    decode_slots,
):
    tensor = ("chip", "core")
    chips, cores = lax.axis_size("chip"), lax.axis_size("core")
    tensor_size = chips * cores
    group_total = lax.axis_size("dp")
    reqs, new, width = tokens.shape
    ctx = cached.shape[1]
    depth = ctx // tensor_size
    flat = reqs * new
    group_reqs = reqs * tensor_size
    group_index = lax.axis_index("dp")
    device = group_index * tensor_size + lax.axis_index(tensor)
    dev = device.astype(jnp.int32).reshape(1)
    key_width = KV_HEADS * HEAD_DIM
    groups = key_width // GROUP
    scalars = (request_order, new_lengths, cached_lengths, dev)
    freq = jnp.asarray(frequencies())

    other_weights = lax.ppermute(mlp_weights, "core", [(0, 1), (1, 0)])

    context_shape = (tensor_size, reqs, depth, key_width)
    context_spec = pl.BlockSpec((tensor_size, reqs, depth, GROUP), lambda g, *_: (0, 0, 0, g))
    table = (reqs, new, GROUP)
    keys, normed, cosine, sine = call(
        key_kernel,
        scalars,
        (groups,),
        [
            whole(tokens.shape),
            whole(norm_gains.shape),
            whole((1, 128)),
            pl.BlockSpec((width, GROUP), lambda g, *_: (0, width // GROUP + g)),
            pl.BlockSpec((reqs, ctx, GROUP), lambda g, *_: (0, 0, g)),
        ],
        [context_spec, whole(tokens.shape), whole(table), whole(table)],
        [shape(context_shape), shape(tokens.shape), shape(table, f32), shape(table, f32)],
        [],
        (tokens, norm_gains, freq, w_qkv, cached),
        2 * flat * width * key_width,
        8 << 20,
    )
    keys_moved = lax.all_to_all(keys, tensor, split_axis=0, concat_axis=0, tiled=True)
    values, residual, post = call(
        attention_kernel,
        scalars,
        (groups,),
        [
            whole(tokens.shape),
            whole(table),
            whole(table),
            pl.BlockSpec((width, 2 * GROUP), lambda g, *_: (0, g)),
            pl.BlockSpec((width, GROUP), lambda g, *_: (0, (width + key_width) // GROUP + g)),
            context_spec,
            pl.BlockSpec((reqs, ctx, GROUP), lambda g, *_: (0, 0, groups + g)),
            whole(tokens.shape),
            whole(norm_gains.shape),
            pl.BlockSpec(memory_space=pl.ANY),
        ],
        [context_spec, whole((flat, width)), whole((flat, width))],
        [shape(context_shape), shape((flat, width)), shape((flat, width))],
        [
            pltpu.VMEM((flat, width), f32),
            pltpu.VMEM((flat, 2 * GROUP), bf16),
            pltpu.VMEM((groups, 2 * GROUP, width), bf16),
            pltpu.SemaphoreType.DMA((groups,)),
        ],
        (normed, cosine, sine, w_qkv, w_qkv, keys, cached, tokens, norm_gains, w_out),
        12 * flat * width * width,
        16 << 20,
    )
    units = mlp_weights.shape[2]
    chunk = 256 if units % 256 == 0 else units

    def mlp(pieces, after, weight=1):
        total_rows = sum(rows.shape[0] for rows in pieces)
        weight_spec = pl.BlockSpec((3, width, chunk), lambda c: (0, 0, c))
        return call(
            functools.partial(mlp_kernel, len(pieces)),
            (),
            (units // chunk,),
            [weight_spec] * 2 + [whole(rows.shape) for rows in pieces],
            [whole((flat, width))] * (total_rows // flat),
            [shape((flat, width))] * (total_rows // flat),
            [pltpu.VMEM((total_rows, width), f32)],
            (mlp_weights, other_weights, *pieces),
            weight * 12 * total_rows * width * units,
            12 * width * units,
            after=after,
        )

    every = request_order.shape[0]
    indices = jnp.arange(every, dtype=jnp.int32)
    slot_of = jnp.sum(
        jnp.where(request_order[:, None] == indices[None, :], decode_slots[None, :], 0), axis=1
    )
    ordinal = jnp.arange(group_reqs, dtype=jnp.int32)

    def inverse(keys_of):
        position = jnp.sum((keys_of[None, :] < keys_of[:, None]).astype(jnp.int32), axis=1)
        return jnp.sum(
            jnp.where(position[None, :] == ordinal[:, None], ordinal[None, :], 0), axis=1
        )

    own_slots = lax.dynamic_slice_in_dim(slot_of, group_index * group_reqs, group_reqs)
    goal = lax.rem(own_slots // group_reqs - group_index + group_total, group_total)
    picked = inverse(goal * group_reqs + lax.rem(own_slots, group_reqs))
    slot_ids = group_index * group_reqs + ordinal
    owners = jnp.sum(
        jnp.where(slot_of[None, :] == slot_ids[:, None], indices[None, :] // group_reqs, 0), axis=1
    )
    origin = lax.rem(group_index - owners + group_total, group_total)
    spots = inverse(origin * group_reqs + ordinal)

    share = group_reqs // group_total
    piece = (share, depth, key_width)
    anywhere = pl.BlockSpec(memory_space=pl.ANY)
    sems = [pltpu.VMEM((group_reqs, depth, key_width), bf16)] + [
        pltpu.SemaphoreType.DMA((group_reqs,))
    ] * 2
    shifts = [
        [(g, (g + s) % group_total) for g in range(group_total)] for s in range(1, group_total)
    ]

    group = group_index.astype(jnp.int32).reshape(1)

    def pack(moved, targets, passed, after):
        return call(
            functools.partial(pack_kernel, group_total, share, len(targets), len(passed)),
            (picked, group), (1,),
            [anywhere] * (1 + len(passed)), [anywhere] * (len(targets) + len(passed)),
            [shape(dims) for dims in targets] + [shape(rows.shape) for rows in passed], sems,
            (moved.reshape(group_reqs, depth, key_width), *passed),
            aliases={3 + i: len(targets) + i for i in range(len(passed))}, after=after,
        )

    def unpack(columns, arrived, target, after, flops=0):
        return call(
            functools.partial(unpack_kernel, columns, group_total, share, len(arrived)),
            (spots, group), (1,), [anywhere] * (len(arrived) + len(target)), anywhere,
            shape((group_reqs, depth, 2 * key_width)), sems, (*arrived, *target), flops,
            aliases={2 + len(arrived): 0} if target else {}, after=after,
            vmem=VMEM // 8 if target else VMEM,
        )

    def swap(rows, mask):
        return lax.ppermute(rows, "chip", [(c, c ^ mask) for c in range(chips)])

    masks = [1, 2] if chips == 4 else range(1, chips)
    gathered = [swap(post, mask) for mask in masks]
    *keys_packed, values = pack(
        keys_moved, [piece] * group_total, (values,), (post, other_weights)
    )
    values_moved = lax.all_to_all(values, tensor, split_axis=0, concat_axis=0, tiled=True)
    keys_arrived = [keys_packed[0]] + [
        lax.ppermute(rows, "dp", pairs) for rows, pairs in zip(keys_packed[1:], shifts)
    ]
    latest = keys_packed[0]
    if chips == 4:
        half = (flat // 2, width)
        first, second = call(
            cut_kernel, (), (1,), [whole((flat, width))] * 2, [whole(half)] * 2,
            [shape(half)] * 2, [], tuple(gathered), after=(latest,),
        )
        latest = first
        batches = [([1, 2], gathered), ([3], [swap(first, 1), swap(second, 2)])]
    else:
        batches = [([mask], [rows]) for mask, rows in zip(masks, gathered)]
    partials = list(mlp([post], (latest, spots), LONG))
    values_packed = pack(
        values_moved, [(group_reqs, depth, key_width)], (), (partials[0],)
    )[0]
    latest = values_packed
    pair = mlp(batches[0][1], (latest, *(rows for batch in batches[1:2] for rows in batch[1])))
    latest = pair[0]
    values_ready, *pair = call(
        gate_kernel, (), (1,), [anywhere] * (1 + len(pair)), [anywhere] * (1 + len(pair)),
        [shape(rows.shape) for rows in (values_packed, *pair)], [], (values_packed, *pair),
        moved=1 << 10, aliases={i: i for i in range(1 + len(pair))}, after=tuple(keys_arrived[1:]),
    )
    values_arrived = lax.all_to_all(values_ready, "dp", split_axis=0, concat_axis=0, tiled=True)
    latest = values_ready
    for i, (batch_masks, pieces) in enumerate(batches):
        results = mlp(pieces, (latest,)) if i else pair
        latest = results[0] if i else latest
        partials += [swap(rows, mask) for mask, rows in zip(batch_masks, results)]

    kv_half = unpack(0, keys_arrived, (), (latest,))

    def add(terms, out_shape, after, flops):
        return call(
            sum_kernel, (request_order, new_lengths, dev), (reqs,),
            [pl.BlockSpec((new, width), lambda r, *_: (r, 0))] * len(terms),
            pl.BlockSpec((1, new, width), lambda r, *_: (r, 0, 0)),
            out_shape, [], tuple(terms), flops, after=after,
        )

    most = add([residual, *partials[:2]], shape(tokens.shape, f32), (kv_half,), 0)
    kv_decode = unpack(
        key_width, [values_arrived], (kv_half,), (most,), LONG * flat * width * width * 8
    )
    layer_out = add(
        [most.reshape(flat, width), *partials[2:]], shape(tokens.shape), (kv_decode,), 0
    )
    return (layer_out, kv_decode)


def solution(mesh):
    in_specs = (
        P(("dp", "chip", "core"), None, None),
        P(("dp", "chip", "core"), None, None),
        P(),
        P(),
        P(),
        P(None, None, ("chip", "core")),
        P(),
        P(),
        P(),
        P(),
    )
    out_specs = (P(("dp", "chip", "core"), None, None), P("dp", ("chip", "core"), None))
    devices = mesh.devices.reshape(mesh.devices.shape[0], -1, 2)
    mesh = jax.sharding.Mesh(devices, ("dp", "chip", "core"))
    return jax.shard_map(local, mesh=mesh, in_specs=in_specs, out_specs=out_specs, check_vma=False)
```
